128 devices in a mesh: wide: 32 (over x, y_hi, z), narrow: 4 (over y_lo, core).
Axes of the slice: x: 4, y: 4 (y_hi: 2, y_lo: 2; y = y_hi * 2 + y_lo), z: 4, core: 2. Of those that a mesh axis runs over, the one named last changes fastest.
Arguments:
- target_ids: int32 [128, 256], P(('wide', 'narrow')), may hold values from 0 to 250111, as said below
- tgt_len: int32 [128], P(('wide', 'narrow')), may hold values from 64 to 256
- mem_len: int32 [128], P(('wide', 'narrow')), may hold values from 264 to 1056
- embed_table: bfloat16 [250112, 768], P(('wide', 'narrow')), may hold values from -6 to 6
- memory: bfloat16 [128, 1056, 768], P(('wide', 'narrow')), may hold values from -6 to 6
- self_qkv: bfloat16 [3, 768, 768], P(None, ('wide', 'narrow')), may hold values from -0.21875 to 0.21875
- self_out: bfloat16 [768, 768], P(('wide', 'narrow')), may hold values from -0.875 to 0.875
- gain_self: bfloat16 [768], P(('wide', 'narrow')), may hold values from 0.5 to 1.5
- cross_qkv: bfloat16 [3, 768, 768], P(None, ('wide', 'narrow')), may hold values from -0.21875 to 0.21875
- cross_out: bfloat16 [768, 768], P(('wide', 'narrow')), may hold values from -1.25 to 1.25
- gain_cross: bfloat16 [768], P(('wide', 'narrow')), may hold values from 0.5 to 1.5
- ffn_in: bfloat16 [2, 768, 2048], P(None, ('wide', 'narrow')), may hold values from -0.21875 to 0.21875
- ffn_out: bfloat16 [2048, 768], P(('wide', 'narrow')), may hold values from -0.125 to 0.125
- gain_ffn: bfloat16 [768], P(('wide', 'narrow')), may hold values from 0.5 to 1.5
- out_grad: bfloat16 [128, 256, 768], P(('wide', 'narrow')), may hold values from -6 to 6
Outputs:
- out: float32 [128, 256, 768], P(('wide', 'narrow'))
- memory_grad: float32 [128, 1056, 768], P(('wide', 'narrow'))
- embed_table_grad: float32 [250112, 768], P(('wide', 'narrow'))
- self_qkv_grad: float32 [3, 768, 768], P(None, ('wide', 'narrow'))
- self_out_grad: float32 [768, 768], P(('wide', 'narrow'))
- gain_self_grad: float32 [768], P(('wide', 'narrow'))
- cross_qkv_grad: float32 [3, 768, 768], P(None, ('wide', 'narrow'))
- cross_out_grad: float32 [768, 768], P(('wide', 'narrow'))
- gain_cross_grad: float32 [768], P(('wide', 'narrow'))
- ffn_in_grad: float32 [2, 768, 2048], P(None, ('wide', 'narrow'))
- ffn_out_grad: float32 [2048, 768], P(('wide', 'narrow'))
- gain_ffn_grad: float32 [768], P(('wide', 'narrow'))
The draws below stay inside these ranges and needn't reach their ends.
Inputs may be any that keep to these rules, and one draw needn't show every extreme that they name: `target_ids`: the table rows held by one device are 1954 consecutive rows. Among the ids of one device's 1 sequence, at most 4 fall within the rows of any one device; in every draw each device's ids reach 4 for some device's rows, and one device's rows receive exactly 4 from every device's sequences.
All inputs are finite; a program needn't handle non-finite values.
Results may differ from the reference program's by a relative error of at most 0.034.
Values may be sent and summed in bfloat16 or wider, within the bound.
No kernel may reach another device: no remote copies, remote signals or barrier semaphores. Data moves between devices by JAX's collectives and lax.ppermute only.
A program may use at most 256 MiB of HBM per device.

```python
import jax
import jax.numpy as jnp
from jax import lax

D = 768
HEADS = 12
HEAD_SIZE = 64
FF = 2048
VOCAB = 250112
TGT = 256
MEM = 1056
SEQ_DEV = 1
SEQUENCES = 128
ROWS_OWN = 1954
CAP = 4


def draw_target_ids(key, part):
    key = jax.random.fold_in(key, 11)
    owner_count = VOCAB // ROWS_OWN
    block_rows = SEQ_DEV * TGT
    common_key, blocks_key = jax.random.split(key)
    common_owner = jax.random.randint(common_key, (), 0, owner_count)
    slot_owner = jnp.arange(owner_count * CAP) // CAP

    def one_block(block_key):
        split_keys = jax.random.split(block_key, 5)
        chosen = jax.random.randint(split_keys[0], (), 0, owner_count)
        scores = jax.random.permutation(split_keys[1], owner_count * CAP).astype(jnp.int32)
        scores = jnp.where(slot_owner == common_owner, -2, jnp.where(slot_owner == chosen, -1, scores))
        picked = jnp.argsort(scores)[:block_rows]
        owners_taken = jax.random.permutation(split_keys[2], slot_owner[picked])
        row_limit = jax.random.randint(split_keys[3], (block_rows,), 1, ROWS_OWN + 1)
        local_row = jax.random.randint(split_keys[4], (block_rows,), 0, row_limit)
        return (owners_taken * ROWS_OWN + local_row).astype(jnp.int32)
    blocks = jax.vmap(one_block)(jax.random.split(blocks_key, owner_count))
    return blocks.reshape(SEQUENCES, TGT).astype(jnp.int32)


def draw_tgt_len(key, part):
    key = jax.random.fold_in(key, 12)
    length_key, pick_key = jax.random.split(key)
    lengths = jax.random.randint(length_key, (SEQUENCES,), TGT // 4, TGT + 1)
    longest = jax.random.randint(pick_key, (), 0, SEQUENCES)
    return jnp.where(jnp.arange(SEQUENCES) == longest, TGT, lengths).astype(jnp.int32)


def draw_mem_len(key, part):
    key = jax.random.fold_in(key, 13)
    length_key, pick_key = jax.random.split(key)
    lengths = jax.random.randint(length_key, (SEQUENCES,), MEM // 4, MEM + 1)
    longest = jax.random.randint(pick_key, (), 0, SEQUENCES)
    return jnp.where(jnp.arange(SEQUENCES) == longest, MEM, lengths).astype(jnp.int32)


def steps_of(own_key, dims, cuts, smallest, largest):
    level, own = 1.0, jax.random.fold_in(own_key, 6)
    for dim, shards_of in cuts:
        draws = jnp.exp(jax.random.uniform(jax.random.fold_in(own, dim), (shards_of,), jnp.float32, smallest / len(cuts), largest / len(cuts)))
        level = level * jnp.repeat(draws, dims[dim] // shards_of).reshape([-1 if axis == dim else 1 for axis in range(len(dims))])
    return level


def bell_draw(rng, dims, width, reach, pieces=(), kind=jnp.bfloat16):
    values = jax.random.normal(rng, dims, jnp.float32) * width
    if len(pieces) > 0:
        values = steps_of(rng, dims, pieces, -0.22, 0.18) * values
    return jnp.clip(values, min=-reach, max=reach).astype(kind)


def setup_inputs(seed: int = 0) -> dict:
    seeds = jax.random.split(jax.random.key(seed), 16)
    return {
        "target_ids": draw_target_ids(jax.random.fold_in(seeds[15], 71), 0),
        "tgt_len": draw_tgt_len(jax.random.fold_in(seeds[15], 71), 0),
        "mem_len": draw_mem_len(jax.random.fold_in(seeds[15], 71), 0),
        "embed_table": bell_draw(seeds[3], (VOCAB, D), 1.0, 6.0, ((0, 128),)),
        "memory": bell_draw(seeds[4], (SEQUENCES, MEM, D), 1.0, 6.0, ((0, 128),)),
        "self_qkv": bell_draw(seeds[5], (3, D, D), D ** -0.5, 0.21875, ((1, 128),)),
        "self_out": bell_draw(seeds[6], (D, D), (D // 16) ** -0.5, 0.875, ((0, 128),)),
        "gain_self": jnp.clip(1.0 + 0.1 * jax.random.normal(seeds[7], (D,), jnp.float32), 0.5, 1.5).astype(jnp.bfloat16),
        "cross_qkv": bell_draw(seeds[8], (3, D, D), D ** -0.5, 0.21875, ((1, 128),)),
        "cross_out": bell_draw(seeds[9], (D, D), (D // 32) ** -0.5, 1.25, ((0, 128),)),
        "gain_cross": jnp.clip(1.0 + 0.1 * jax.random.normal(seeds[10], (D,), jnp.float32), 0.5, 1.5).astype(jnp.bfloat16),
        "ffn_in": bell_draw(seeds[11], (2, D, FF), D ** -0.5, 0.21875, ((1, 128),)),
        "ffn_out": bell_draw(seeds[12], (FF, D), FF ** -0.5, 0.125, ((0, 128),)),
        "gain_ffn": jnp.clip(1.0 + 0.1 * jax.random.normal(seeds[13], (D,), jnp.float32), 0.5, 1.5).astype(jnp.bfloat16),
        "out_grad": bell_draw(seeds[14], (SEQUENCES, TGT, D), 1.0, 6.0, ((0, 128),)),
    }


@jax.custom_vjp
def low(v):
    return lax.optimization_barrier(v.astype(jnp.bfloat16)).astype(jnp.float32)

@jax.custom_vjp
def low_back(v):
    return v

def low_keep(v):
    return (low(v), None)

def low_pass(kept, grad):
    return (grad,)

def back_keep(v):
    return (v, None)

def back_low(kept, grad):
    return (low(grad),)
low.defvjp(low_keep, low_pass)
low_back.defvjp(back_keep, back_low)
eps = 1e-06
masked_score = -1e+30

def both_ways(value):
    return low(low_back(value))

def matmul(left, right):
    return jnp.dot(left, right, precision=lax.Precision.HIGHEST)

def rms_norm(hidden, gain):
    scale = lax.rsqrt(lax.optimization_barrier(jnp.mean(hidden * hidden, axis=-1, keepdims=True)) + eps)
    return hidden * scale * gain

def attend(queries, key_rows, values, valid):
    query_count = queries.shape[0]
    split_q = queries.reshape(query_count, HEADS, HEAD_SIZE)
    split_k = key_rows.reshape(key_rows.shape[0], HEADS, HEAD_SIZE)
    split_v = values.reshape(values.shape[0], HEADS, HEAD_SIZE)
    scores = low_back(jnp.einsum('qhd,khd->hqk', split_q, split_k, precision=lax.Precision.HIGHEST) * 0.125)
    scores = jnp.where(valid[None], scores, masked_score)
    row_top = lax.optimization_barrier(jnp.max(scores, axis=-1, keepdims=True))
    expanded = jnp.exp(scores - row_top)
    attn_weights = expanded / lax.optimization_barrier(jnp.sum(expanded, axis=-1, keepdims=True))
    mixed = jnp.einsum('hqk,khd->qhd', low(attn_weights), split_v, precision=lax.Precision.HIGHEST)
    return both_ways(mixed.reshape(query_count, HEADS * HEAD_SIZE))

def decoder_layer(embedded, memory_rows, target_len, memory_len, weights):
    self_qkv, self_out, gain_self, cross_qkv, cross_out, gain_cross, ffn_in, ffn_out, gain_ffn = weights
    positions = jnp.arange(TGT)
    causal = positions[None, :] <= positions[:, None]
    normed = low(rms_norm(embedded, gain_self))
    queries = both_ways(matmul(normed, self_qkv[0]))
    key_rows = both_ways(matmul(normed, self_qkv[1]))
    values = both_ways(matmul(normed, self_qkv[2]))
    hidden = embedded + low_back(matmul(attend(queries, key_rows, values, causal), self_out))
    normed = low(rms_norm(hidden, gain_cross))
    queries = both_ways(matmul(normed, cross_qkv[0]))
    key_rows = both_ways(matmul(memory_rows, cross_qkv[1]))
    values = both_ways(matmul(memory_rows, cross_qkv[2]))
    memory_reach = jnp.broadcast_to(jnp.arange(MEM)[None, :] < memory_len, (TGT, MEM))
    hidden = hidden + low_back(matmul(attend(queries, key_rows, values, memory_reach), cross_out))
    normed = low(rms_norm(hidden, gain_ffn))
    gate = low_back(matmul(normed, ffn_in[0]))
    upward = low_back(matmul(normed, ffn_in[1]))
    inner_rows = low(jax.nn.gelu(gate, approximate=True) * upward)
    hidden = hidden + low_back(matmul(inner_rows, ffn_out))
    keep_rows = (positions < target_len).astype(hidden.dtype)[:, None]
    return hidden * keep_rows

def run_group(weights, group_block):
    embedded, memory_rows, target_len, memory_len = group_block
    return jax.vmap(decoder_layer, in_axes=(0, 0, 0, 0, None))(embedded, memory_rows, target_len, memory_len, weights)

def reference(target_ids, tgt_len, mem_len, embed_table, memory, self_qkv, self_out, gain_self, cross_qkv, cross_out, gain_cross, ffn_in, ffn_out, gain_ffn, out_grad):
    floats = tuple((array_in.astype(jnp.float32) for array_in in (embed_table, memory, self_qkv, self_out, gain_self, cross_qkv, cross_out, gain_cross, ffn_in, ffn_out, gain_ffn)))
    group_size = min(8, SEQUENCES)
    group_count = SEQUENCES // group_size
    checked = jax.checkpoint(run_group)

    def forward(table_rows, memory_all, *weights):
        embedded = table_rows[target_ids]
        blocks = (embedded.reshape(group_count, group_size, TGT, D), memory_all.reshape(group_count, group_size, MEM, D), tgt_len.reshape(group_count, group_size), mem_len.reshape(group_count, group_size))

        def scan_step(carried, group_block):
            return (carried, checked(weights, group_block))
        unused, outputs = lax.scan(scan_step, jnp.zeros((), jnp.float32), blocks)
        return outputs.reshape(SEQUENCES, TGT, D)
    result, pull_back = jax.vjp(forward, *floats)
    grads = pull_back(out_grad.astype(jnp.float32))
    return (result.astype(jnp.float32), grads[1], grads[0], grads[2], grads[3], grads[4], grads[5], grads[6], grads[7], grads[8], grads[9], grads[10])
```

```python
import functools

import jax
import jax.numpy as jnp
from jax import lax
from jax.experimental import pallas as pl
from jax.experimental.pallas import tpu as pltpu
from jax.sharding import Mesh, PartitionSpec as P

HEAD_SIZE = 64


eps = 1e-06
masked_score = -1e30

AXES = ("x", "yh", "zh", "zl", "yl", "c")
SIZES = (4, 2, 2, 2, 2, 2)
RING_X, RING_Y, RING_Z = ("x",), ("yh", "yl"), ("zh", "zl")
CHIPS = ("x", "yh", "zh", "zl", "yl")
EIGHT = ("zl", "yl", "c")
BLOCK = 48
SLOTS = 4
GAINS = 18


def ring_shift(v, ring, by):
    return lax.ppermute(v, ring, [(i, (i + by) % 4) for i in range(4)])


def ring_pair(v, ring, first):
    perm = []
    for i in range(4):
        for c in range(2):
            perm.append((2 * i + c, 2 * (i ^ (1 if (c == 0) == first else 3)) + c))
    return lax.ppermute(v, ring + ("c",), perm)


def swap_cores(v):
    return lax.ppermute(v, "c", [(0, 1), (1, 0)])


def gather_ring(v, ring):
    return jnp.stack([v] + [ring_shift(v, ring, by) for by in (1, 2, 3)])


def gather_last(v, ring):
    near = ring_pair(v, ring, True)
    other = ring_pair(v, ring, False)
    far = ring_pair(near, ring, False)
    own = [v, near, other, far]
    return own + [swap_cores(b) for b in own]


def place_kernel(last, targets, pos_ref, *refs):
    blocks, outs, sem = refs[:8], refs[8:-1], refs[-1]
    me = {"x": pos_ref[0], "y": pos_ref[1], "z": pos_ref[2]}
    middle = "z" if last == "y" else "y"
    for source in range(2):
        core = pos_ref[3] if source == 0 else 1 - pos_ref[3]
        near, other = 1 + 2 * core, 3 - 2 * core
        for k in range(4):
            at = {last: me[last] ^ (0, near, other, 2)[k]}
            for j2 in range(4):
                at[middle] = (me[middle] + 4 - j2) & 3
                for j1 in range(4):
                    at["x"] = (me["x"] + 4 - j1) & 3
                    group = at["x"] * 4 + (at["y"] >> 1) * 2 + (at["z"] >> 1)
                    member = (at["z"] & 1) * 4 + (at["y"] & 1) * 2 + core
                    for src, out, dst in targets(group, member):
                        pltpu.make_async_copy(
                            blocks[4 * source + k].at[(j2, j1) + src], outs[out].at[dst], sem
                        ).start()
    for out in outs:
        pltpu.make_async_copy(out, out, sem).wait()


def square_targets(width, group, member):
    row = pl.multiple_of(group * BLOCK, 16)
    column = pl.multiple_of(member * width, 128)
    return [((slice(None), slice(None)), 0, (pl.ds(row, BLOCK), pl.ds(column, width)))]


def ffn_targets(group, member):
    row = pl.multiple_of(group * BLOCK, 16)
    column = pl.multiple_of(member * 512, 128)
    found = [
        ((slice(None), pl.ds(0, 512)), 0, (pl.ds(row, BLOCK), pl.ds(column, 512)))
    ]
    own = pl.multiple_of((group * 8 + member) * 16, 16)
    for t in range(3):
        found.append(
            ((pl.ds(16 * t, 16), pl.ds(512, 256)), 1, (pl.ds(own, 16), pl.ds(256 * t, 256)))
        )
    return found


def place(pos, blocks, last, targets, shapes):
    return pl.pallas_call(
        functools.partial(place_kernel, last, targets),
        in_specs=[pl.BlockSpec(memory_space=pltpu.SMEM)] + [pl.BlockSpec(memory_space=pl.ANY)] * 8,
        out_specs=[pl.BlockSpec(memory_space=pltpu.VMEM)] * len(shapes),
        out_shape=[jax.ShapeDtypeStruct(s, jnp.bfloat16) for s in shapes],
        scratch_shapes=[pltpu.SemaphoreType.DMA],
        cost_estimate=pl.CostEstimate(
            flops=0, bytes_accessed=4 * sum(a * b for a, b in shapes), transcendentals=0
        ),
        compiler_params=pltpu.CompilerParams(vmem_limit_bytes=32 * 2**20),
    )(pos, *blocks)


def all_weights(pos, self_qkv, self_out, cross_qkv, cross_out, ffn_in, ffn_out):
    def chunks(v):
        return v.reshape(6, 8, -1).swapaxes(0, 1)

    flat = [
        jnp.concatenate([jnp.swapaxes(qkv, 0, 1).reshape(6, -1), out], axis=1)
        for qkv, out in ((self_qkv, self_out), (cross_qkv, cross_out))
    ]
    flat.append(jnp.swapaxes(ffn_in, 0, 1).reshape(6, -1))
    turned = jnp.concatenate([chunks(v) for v in flat], axis=2)
    turned = lax.all_to_all(turned, EIGHT, 0, 0, tiled=True).reshape(BLOCK, -1)
    tail = ffn_out.reshape(16, 3, 256).swapaxes(0, 1).reshape(BLOCK, 256)
    piece = jnp.concatenate([turned, tail], axis=1)
    piece = gather_ring(piece, RING_X)
    attention = gather_ring(piece[:, :, :768], RING_Z)
    feed = gather_ring(piece[:, :, 768:], RING_Y)
    self_all = gather_last(attention[:, :, :, :384], RING_Y)
    cross_all = gather_last(attention[:, :, :, 384:], RING_Y)
    feed_all = gather_last(feed, RING_Z)
    square = functools.partial(square_targets, 384)
    return (
        place(pos, self_all, "y", square, [(768, 3072)])[0],
        place(pos, cross_all, "y", square, [(768, 3072)])[0],
        *place(pos, feed_all, "z", ffn_targets, [(768, 4096), (2048, 768)]),
    )


def sum_pieces(pieces):
    width = pieces.shape[-1]
    halves = jnp.moveaxis(pieces.reshape(64, 2, BLOCK, width), 1, 0)
    core = lax.axis_index("c")
    mine = lax.dynamic_index_in_dim(halves, core, 0, keepdims=False)
    other = lax.dynamic_index_in_dim(halves, 1 - core, 0, keepdims=False)
    both = mine.astype(jnp.float32) + swap_cores(other).astype(jnp.float32)
    got = lax.all_to_all(both.astype(jnp.bfloat16), CHIPS, 0, 0, tiled=True)
    return jnp.sum(got.astype(jnp.float32), axis=0)


def square_pieces(grad):
    return grad.astype(jnp.bfloat16).reshape(16, BLOCK, 8, -1).swapaxes(1, 2)


def rms_norm(hidden, gain):
    scale = lax.rsqrt(jnp.mean(hidden * hidden, axis=-1, keepdims=True) + eps)
    return hidden * scale * gain


def gated_unit(gate, upward):
    return jax.nn.gelu(gate, approximate=True) * upward


def split_heads(rows):
    return rows.reshape(rows.shape[0], rows.shape[1], rows.shape[2] // HEAD_SIZE, HEAD_SIZE)


def scores_of(queries, key_rows, valid):
    raw_scores = (
        jnp.einsum(
            "sqhd,skhd->shqk",
            split_heads(queries),
            split_heads(key_rows),
            preferred_element_type=jnp.float32,
        )
        * 0.125
    )
    return jnp.where(valid[:, None], raw_scores, masked_score)


def attend_forward(queries, key_rows, values, valid):
    scores = scores_of(queries, key_rows, valid)
    row_top = jnp.max(scores, axis=-1, keepdims=True)
    expanded = jnp.exp(scores - row_top)
    row_total = jnp.sum(expanded, axis=-1, keepdims=True)
    weights_low = (expanded / row_total).astype(jnp.bfloat16)
    mixed = jnp.einsum(
        "shqk,skhd->sqhd", weights_low, split_heads(values), preferred_element_type=jnp.float32
    )
    return (mixed.reshape(queries.shape).astype(jnp.bfloat16), row_top, row_total)


def attend_backward(queries, key_rows, values, valid, row_top, row_total, grad_mixed):
    scores = scores_of(queries, key_rows, valid)
    attn_weights = jnp.exp(scores - row_top) / row_total
    split_g = split_heads(grad_mixed)
    grad_weights = jnp.einsum(
        "sqhd,skhd->shqk", split_g, split_heads(values), preferred_element_type=jnp.float32
    )
    row_inner = jnp.sum(grad_weights * attn_weights, axis=-1, keepdims=True)
    grad_scores = (attn_weights * (grad_weights - row_inner)).astype(jnp.bfloat16)
    grad_values = jnp.einsum(
        "shqk,sqhd->skhd",
        attn_weights.astype(jnp.bfloat16),
        split_g,
        preferred_element_type=jnp.float32,
    )
    grad_queries = (
        jnp.einsum(
            "shqk,skhd->sqhd",
            grad_scores,
            split_heads(key_rows),
            preferred_element_type=jnp.float32,
        )
        * 0.125
    )
    grad_keys = (
        jnp.einsum(
            "shqk,sqhd->skhd", grad_scores, split_heads(queries), preferred_element_type=jnp.float32
        )
        * 0.125
    )
    return (
        grad_queries.reshape(queries.shape).astype(jnp.bfloat16),
        grad_keys.reshape(key_rows.shape).astype(jnp.bfloat16),
        grad_values.reshape(values.shape).astype(jnp.bfloat16),
    )


def body(
    target_ids,
    tgt_len,
    mem_len,
    embed_table,
    memory,
    self_qkv,
    self_out,
    gain_self,
    cross_qkv,
    cross_out,
    gain_cross,
    ffn_in,
    ffn_out,
    gain_ffn,
    out_grad,
):
    tgt_count = target_ids.shape[1]
    mem_count, model_width = (memory.shape[1], memory.shape[2])
    own_rows = embed_table.shape[0]
    owner_count = 128
    place_in = [lax.axis_index(ring) for ring in (RING_X, RING_Y, RING_Z, ("c",))]
    pos = jnp.stack(place_in).astype(jnp.int32)

    flat_ids = target_ids.reshape(tgt_count)
    owner_of = flat_ids // own_rows
    local_row = flat_ids - owner_of * own_rows
    owner_hits = (owner_of[:, None] == jnp.arange(owner_count)[None, :]).astype(jnp.int32)
    row_rank = jnp.sum(jnp.cumsum(owner_hits, axis=0) * owner_hits, axis=1) - 1
    slot_index = owner_of * SLOTS + row_rank
    slot_hits = slot_index[:, None] == jnp.arange(owner_count * SLOTS)[None, :]
    wanted = jnp.sum(jnp.where(slot_hits, local_row[:, None] + 1, 0), axis=0)
    gains = jnp.concatenate([gain_self, gain_cross, gain_ffn]).astype(jnp.float32)
    request = jnp.concatenate(
        [
            wanted.astype(jnp.float32).reshape(owner_count, SLOTS),
            jnp.broadcast_to(gains[None], (owner_count, GAINS)),
            jnp.zeros((owner_count, 32 - SLOTS - GAINS), jnp.float32),
        ],
        axis=1,
    )
    arrived = lax.all_to_all(request, AXES, split_axis=0, concat_axis=0, tiled=True)
    gain_self_all, gain_cross_all, gain_ffn_all = (
        arrived[:, SLOTS + 6 * k : SLOTS + 6 * k + 6].reshape(model_width) for k in range(3)
    )
    rows_wanted = arrived[:, :SLOTS].reshape(owner_count * SLOTS).astype(jnp.int32) - 1
    row_hits = (rows_wanted[:, None] == jnp.arange(own_rows)[None, :]).astype(jnp.bfloat16)
    fetched = jnp.dot(row_hits, embed_table, preferred_element_type=jnp.float32)
    fetched = fetched.astype(jnp.bfloat16).reshape(owner_count, SLOTS, model_width)
    returned = lax.all_to_all(fetched, AXES, split_axis=0, concat_axis=0, tiled=True)
    slot_ones = slot_hits.astype(jnp.bfloat16)
    hidden_zero = jnp.dot(
        slot_ones,
        returned.reshape(owner_count * SLOTS, model_width),
        preferred_element_type=jnp.float32,
    )
    self_all, cross_all, ffn_in_all, ffn_out_all = all_weights(
        pos, self_qkv, self_out, cross_qkv, cross_out, ffn_in, ffn_out
    )

    positions = jnp.arange(tgt_count)
    causal = (positions[None, :] <= positions[:, None])[None]
    memory_reach = jnp.broadcast_to(
        jnp.arange(mem_count)[None, None, :] < mem_len[:, None, None], (1, tgt_count, mem_count)
    )
    keep_rows = (positions < tgt_len[0]).astype(jnp.float32).reshape(tgt_count, 1)
    memory_rows = memory.reshape(mem_count, model_width)

    normed_self = rms_norm(hidden_zero, gain_self_all).astype(jnp.bfloat16)
    self_proj = jnp.dot(
        normed_self, self_all[:, :2304], preferred_element_type=jnp.float32
    ).astype(jnp.bfloat16)
    self_proj = [self_proj[None, :, 768 * k : 768 * k + 768] for k in range(3)]
    mixed_self, top_self, total_self = attend_forward(*self_proj, causal)
    mixed_self = mixed_self[0]
    hidden_one = hidden_zero + jnp.dot(
        mixed_self, self_all[:, 2304:], preferred_element_type=jnp.float32
    )
    normed_cross = rms_norm(hidden_one, gain_cross_all).astype(jnp.bfloat16)
    cross_query = jnp.dot(
        normed_cross, cross_all[:, :768], preferred_element_type=jnp.float32
    ).astype(jnp.bfloat16)[None]
    cross_kv = jnp.dot(
        memory_rows, cross_all[:, 768:2304], preferred_element_type=jnp.float32
    ).astype(jnp.bfloat16)
    cross_key, cross_value = cross_kv[None, :, :768], cross_kv[None, :, 768:]
    mixed_cross, top_cross, total_cross = attend_forward(
        cross_query, cross_key, cross_value, memory_reach
    )
    mixed_cross = mixed_cross[0]
    hidden_two = hidden_one + jnp.dot(
        mixed_cross, cross_all[:, 2304:], preferred_element_type=jnp.float32
    )
    normed_ffn = rms_norm(hidden_two, gain_ffn_all).astype(jnp.bfloat16)
    gate_up = jnp.dot(normed_ffn, ffn_in_all, preferred_element_type=jnp.float32)
    gate, upward = gate_up[:, :2048], gate_up[:, 2048:]
    inner_rows, gated_pull = jax.vjp(gated_unit, gate, upward)
    inner_rows = inner_rows.astype(jnp.bfloat16)
    hidden_three = hidden_two + jnp.dot(inner_rows, ffn_out_all, preferred_element_type=jnp.float32)
    result = (hidden_three * keep_rows)[None]

    grad_three = out_grad[0].astype(jnp.float32) * keep_rows
    low_three = grad_three.astype(jnp.bfloat16)
    ffn_out_grad = jnp.einsum("rf,rd->fd", inner_rows, low_three, preferred_element_type=jnp.float32)
    grad_inner = jnp.einsum("rd,fd->rf", low_three, ffn_out_all, preferred_element_type=jnp.float32)
    grad_gate, grad_upward = gated_pull(grad_inner)
    grad_gate_up = jnp.concatenate([grad_gate, grad_upward], axis=1).astype(jnp.bfloat16)
    ffn_in_grad = jnp.einsum("rd,rf->df", normed_ffn, grad_gate_up, preferred_element_type=jnp.float32)
    grad_normed = jnp.einsum("rf,df->rd", grad_gate_up, ffn_in_all, preferred_element_type=jnp.float32)
    unused, norm_pull = jax.vjp(rms_norm, hidden_two, gain_ffn_all)
    grad_hidden, gain_ffn_grad = norm_pull(grad_normed)
    grad_two = grad_three + grad_hidden
    ffn_pieces = jnp.concatenate(
        [
            square_pieces(ffn_in_grad),
            ffn_out_grad.astype(jnp.bfloat16)
            .reshape(16, 8, 16, 3, 256)
            .swapaxes(2, 3)
            .reshape(16, 8, BLOCK, 256),
        ],
        axis=3,
    )
    ffn_sum = sum_pieces(ffn_pieces)

    low_two = grad_two.astype(jnp.bfloat16)
    cross_out_grad = jnp.einsum("rd,re->de", mixed_cross, low_two, preferred_element_type=jnp.float32)
    grad_mixed = jnp.einsum(
        "re,de->rd", low_two, cross_all[:, 2304:], preferred_element_type=jnp.float32
    ).astype(jnp.bfloat16)
    grad_query, grad_key, grad_value = attend_backward(
        cross_query, cross_key, cross_value, memory_reach, top_cross, total_cross, grad_mixed[None]
    )
    grad_query = grad_query[0]
    grad_kv = jnp.concatenate([grad_key[0], grad_value[0]], axis=1)
    cross_q_grad = jnp.einsum("rd,re->de", normed_cross, grad_query, preferred_element_type=jnp.float32)
    cross_kv_grad = jnp.einsum("md,me->de", memory_rows, grad_kv, preferred_element_type=jnp.float32)
    cross_sum = sum_pieces(
        square_pieces(jnp.concatenate([cross_q_grad, cross_kv_grad, cross_out_grad], axis=1))
    )
    memory_grad = jnp.einsum(
        "me,de->md", grad_kv, cross_all[:, 768:2304], preferred_element_type=jnp.float32
    )[None]
    grad_normed = jnp.einsum(
        "re,de->rd", grad_query, cross_all[:, :768], preferred_element_type=jnp.float32
    )
    unused, norm_pull = jax.vjp(rms_norm, hidden_one, gain_cross_all)
    grad_hidden, gain_cross_grad = norm_pull(grad_normed)
    grad_one = grad_two + grad_hidden

    low_one = grad_one.astype(jnp.bfloat16)
    self_out_grad = jnp.einsum("rd,re->de", mixed_self, low_one, preferred_element_type=jnp.float32)
    grad_mixed = jnp.einsum(
        "re,de->rd", low_one, self_all[:, 2304:], preferred_element_type=jnp.float32
    ).astype(jnp.bfloat16)
    grads = attend_backward(*self_proj, causal, top_self, total_self, grad_mixed[None])
    grad_stack = jnp.concatenate([g[0] for g in grads], axis=1)
    self_qkv_grad = jnp.einsum("rd,re->de", normed_self, grad_stack, preferred_element_type=jnp.float32)
    grad_normed = jnp.einsum(
        "re,de->rd", grad_stack, self_all[:, :2304], preferred_element_type=jnp.float32
    )
    unused, norm_pull = jax.vjp(rms_norm, hidden_zero, gain_self_all)
    grad_hidden, gain_self_grad = norm_pull(grad_normed)
    grad_embed = grad_one + grad_hidden
    self_sum = sum_pieces(square_pieces(jnp.concatenate([self_qkv_grad, self_out_grad], axis=1)))

    outgoing = jnp.einsum(
        "rs,rd->sd", slot_ones, grad_embed.astype(jnp.bfloat16), preferred_element_type=jnp.float32
    ).astype(jnp.bfloat16)
    gain_parts = jnp.concatenate(
        [
            g.astype(jnp.bfloat16).reshape(owner_count, 6)
            for g in (gain_self_grad, gain_cross_grad, gain_ffn_grad)
        ],
        axis=1,
    )
    extra = jnp.pad(gain_parts[:, None, :], ((0, 0), (0, SLOTS - 1), (0, 128 - GAINS)))
    outgoing = jnp.concatenate([outgoing.reshape(owner_count, SLOTS, model_width), extra], axis=2)
    incoming = lax.all_to_all(outgoing, AXES, split_axis=0, concat_axis=0, tiled=True)
    gain_sums = jnp.sum(
        incoming[:, 0, model_width : model_width + GAINS].astype(jnp.float32), axis=0
    )
    table_grad = jnp.einsum(
        "sr,sd->rd",
        row_hits,
        incoming[:, :, :model_width].reshape(owner_count * SLOTS, model_width),
        preferred_element_type=jnp.float32,
    )

    turned = jnp.concatenate([self_sum, cross_sum, ffn_sum[:, :512]], axis=1)
    turned = lax.all_to_all(turned.reshape(8, 6, -1), EIGHT, 0, 0, tiled=True)

    def rows_of(v):
        return jnp.swapaxes(v, 0, 1).reshape(6, -1)

    done = []
    for at in (0, 384):
        whole = rows_of(turned[:, :, at : at + 384])
        done.append(jnp.swapaxes(whole[:, :2304].reshape(6, 3, model_width), 0, 1))
        done.append(whole[:, 2304:])
    ffn_in_sum = jnp.swapaxes(rows_of(turned[:, :, 768:]).reshape(6, 2, 2048), 0, 1)
    ffn_out_sum = ffn_sum[:, 512:].reshape(3, 16, 256).swapaxes(0, 1).reshape(16, model_width)
    return (
        result,
        memory_grad,
        table_grad,
        done[0],
        done[1],
        gain_sums[:6],
        done[2],
        done[3],
        gain_sums[6:12],
        ffn_in_sum,
        ffn_out_sum,
        gain_sums[12:18],
    )


def solution(mesh):
    fine = Mesh(mesh.devices.reshape(SIZES), AXES)
    in_specs = (
        P(AXES, None),
        P(AXES),
        P(AXES),
        P(AXES, None),
        P(AXES, None, None),
        P(None, AXES, None),
        P(AXES, None),
        P(AXES),
        P(None, AXES, None),
        P(AXES, None),
        P(AXES),
        P(None, AXES, None),
        P(AXES, None),
        P(AXES),
        P(AXES, None, None),
    )
    out_specs = (
        P(AXES, None, None),
        P(AXES, None, None),
        P(AXES, None),
        P(None, AXES, None),
        P(AXES, None),
        P(AXES),
        P(None, AXES, None),
        P(AXES, None),
        P(AXES),
        P(None, AXES, None),
        P(AXES, None),
        P(AXES),
    )
    return jax.shard_map(body, mesh=fine, in_specs=in_specs, out_specs=out_specs, check_vma=False)
```

```python
import functools

import jax
import jax.numpy as jnp
from jax import lax
from jax.experimental import pallas as pl
from jax.experimental.pallas import tpu as pltpu
from jax.sharding import Mesh, PartitionSpec as P

HEAD_SIZE = 64
D = 768
FF = 2048
TGT = 256
MEM = 1056
KEYS = 1152
PAIRS = 6


eps = 1e-06
masked_score = -1e30

AXES = ("x", "yh", "zh", "zl", "yl", "c")
SIZES = (4, 2, 2, 2, 2, 2)
RING_X, RING_Y, RING_Z = ("x",), ("yh", "yl"), ("zh", "zl")
RINGS = {"x": RING_X, "y": RING_Y, "z": RING_Z}
CHIPS = ("x", "yh", "zh", "zl", "yl")
EIGHT = ("zl", "yl", "c")
BLOCK = 48
SLOTS = 4
GAINS = 18

HBM = pl.BlockSpec(memory_space=pl.ANY)
SCALARS = pl.BlockSpec(memory_space=pltpu.SMEM)


def ring_shift(v, ring, by):
    return lax.ppermute(v, ring, [(i, (i + by) % 4) for i in range(4)])


def ring_pair(v, ring, first):
    perm = []
    for i in range(4):
        for c in range(2):
            perm.append((2 * i + c, 2 * (i ^ (1 if (c == 0) == first else 3)) + c))
    return lax.ppermute(v, ring + ("c",), perm)


def swap_cores(v):
    return lax.ppermute(v, "c", [(0, 1), (1, 0)])


def gather_ring(v, ring):
    return jnp.stack([v] + [ring_shift(v, ring, by) for by in (1, 2, 3)])


def gather_last(v, ring):
    near = ring_pair(v, ring, True)
    other = ring_pair(v, ring, False)
    far = ring_pair(near, ring, False)
    own = [v, near, other, far]
    return own + [swap_cores(b) for b in own]


def add_low(*terms):
    return sum(t.astype(jnp.float32) for t in terms).astype(jnp.bfloat16)


def halve(low, high, ring):
    got = ring_pair(high, ring, False)
    back = ring_pair(add_low(low[1], got[1]), ring, True)
    return low[0], got[0], back


def ring_sum(mine, other, rings):
    got = swap_cores(other)
    low, high = add_low(mine[:2], got[:2]), add_low(mine[2:], got[2:])
    for ring in rings[:-1]:
        terms = halve(low, high, RINGS[ring])
        low, high = (add_low(*(t[at] for t in terms)) for at in (slice(0, 2), slice(2, 4)))
    return sum(t.astype(jnp.float32) for t in halve(low, high, RINGS[rings[-1]]))


def mm(a, b):
    return jnp.dot(a, b, preferred_element_type=jnp.float32)


def mm_nt(a, b):
    return lax.dot_general(a, b, (((1,), (1,)), ((), ())), preferred_element_type=jnp.float32)


def mm_tn(a, b):
    return lax.dot_general(a, b, (((0,), (0,)), ((), ())), preferred_element_type=jnp.float32)


def first_half(shape):
    return lax.broadcasted_iota(jnp.int32, shape, 1) < HEAD_SIZE


def stacked_heads(pair):
    low = first_half(pair.shape)
    zero = jnp.zeros_like(pair)
    return jnp.concatenate([jnp.where(low, pair, zero), jnp.where(low, zero, pair)], axis=0)


def joined_heads(both):
    half = both.shape[0] // 2
    return jnp.where(first_half((half, both.shape[1])), both[:half], both[half:])


def rms_scale(hidden):
    return lax.rsqrt(jnp.mean(hidden * hidden, axis=-1, keepdims=True) + eps)


def rms_back(hidden, gain, grad):
    scale = rms_scale(hidden)
    u = grad * gain
    inner = jnp.mean(u * hidden, axis=-1, keepdims=True)
    grad_hidden = scale * u - hidden * (scale * scale * scale * inner)
    return grad_hidden, jnp.sum(grad * hidden * scale, axis=0, keepdims=True)


def my_place(pos_ref):
    return {"x": pos_ref[0], "y": pos_ref[1], "z": pos_ref[2]}


def group_member(at, core):
    group = at["x"] * 4 + (at["y"] >> 1) * 2 + (at["z"] >> 1)
    return group, (at["z"] & 1) * 4 + (at["y"] & 1) * 2 + core


def partners(core):
    return (0, 1 + 2 * core, 3 - 2 * core, 2)


def square_parts(width, group, member):
    row = pl.multiple_of(group * BLOCK, 16)
    column = pl.multiple_of(member * width, 128)
    return [((slice(None), slice(None)), 0, (pl.ds(row, BLOCK), pl.ds(column, width)))]


def ffn_parts(group, member):
    row = pl.multiple_of(group * BLOCK, 16)
    column = pl.multiple_of(member * 512, 128)
    found = [((slice(None), pl.ds(0, 512)), 0, (pl.ds(row, BLOCK), pl.ds(column, 512)))]
    own = pl.multiple_of((group * 8 + member) * 16, 16)
    for t in range(3):
        found.append(
            ((pl.ds(16 * t, 16), pl.ds(512, 256)), 1, (pl.ds(own, 16), pl.ds(256 * t, 256)))
        )
    return found


def start_place(pos_ref, last, parts, blocks, outs, sem):
    me = my_place(pos_ref)
    middle = "z" if last == "y" else "y"
    at = {}
    for source in range(2):
        core = pos_ref[3] ^ source
        for k, flip in enumerate(partners(core)):
            at[last] = me[last] ^ flip
            for j2 in range(4):
                at[middle] = (me[middle] + 4 - j2) & 3
                for j1 in range(4):
                    at["x"] = (me["x"] + 4 - j1) & 3
                    for src, out, dst in parts(*group_member(at, core)):
                        pltpu.make_async_copy(
                            blocks[4 * source + k].at[(j2, j1) + src], outs[out].at[dst], sem
                        ).start()


def wait_whole(refs, sem):
    for ref in refs:
        pltpu.make_async_copy(ref, ref, sem).wait()


def start_split(pos_ref, rings, parts, wholes, outs, sem):
    me = my_place(pos_ref)
    at = {}
    for source in range(2):
        core = pos_ref[3] ^ source
        flips = partners(core)
        for k3 in range(4):
            at[rings[0]] = me[rings[0]] ^ flips[k3]
            for k2 in range(4):
                at[rings[1]] = me[rings[1]] ^ flips[k2]
                for k1 in range(4):
                    at[rings[2]] = me[rings[2]] ^ flips[k1]
                    for dst, whole, src in parts(*group_member(at, core)):
                        pltpu.make_async_copy(
                            wholes[whole].at[src], outs[source].at[(k3, k2, k1) + dst], sem
                        ).start()


def start_split_whole(pos_ref, whole, outs, sem):
    for source in range(2):
        core = pos_ref[3] ^ source
        for group in range(16):
            for q in range(4):
                for dst, _, src in square_parts(384, group, 2 * q + core):
                    pltpu.make_async_copy(
                        whole.at[src], outs[source].at[(4 * group + q,) + dst], sem
                    ).start()


def softmax_rows(score_ref, weight_ref, rows_at_once, valid_of):
    def step(i, carry):
        at = pl.multiple_of(i * rows_at_once, rows_at_once)
        scores = score_ref[pl.ds(at, rows_at_once), :]
        scores = jnp.where(valid_of(at, scores.shape), scores, masked_score)
        expanded = jnp.exp(scores - jnp.max(scores, axis=-1, keepdims=True))
        total = jnp.sum(expanded, axis=-1, keepdims=True)
        weight_ref[pl.ds(at, rows_at_once), :] = (expanded * (1.0 / total)).astype(jnp.bfloat16)
        return carry

    lax.fori_loop(0, score_ref.shape[0] // rows_at_once, step, 0)


def softmax_back_rows(weight_ref, grad_ref, out_ref, rows_at_once):
    def step(i, carry):
        at = pl.multiple_of(i * rows_at_once, rows_at_once)
        weights = weight_ref[pl.ds(at, rows_at_once), :].astype(jnp.float32)
        grads = grad_ref[pl.ds(at, rows_at_once), :]
        inner = jnp.sum(weights * grads, axis=-1, keepdims=True)
        out_ref[pl.ds(at, rows_at_once), :] = (weights * (grads - inner)).astype(jnp.bfloat16)
        return carry

    lax.fori_loop(0, grad_ref.shape[0] // rows_at_once, step, 0)


def pair_columns(j, offset=0):
    return pl.ds(pl.multiple_of(offset + j * 128, 128), 128)


def self_forward_kernel(pos_ref, rows_ref, slot_ref, gain_ref, *refs):
    blocks, (emb_ref, qkv_ref, p_ref, mixed_ref, h1_ref, w_ref, score, sem) = refs[:8], refs[8:]
    j = pl.program_id(0)

    @pl.when(j == 0)
    def _():
        start_place(pos_ref, "y", functools.partial(square_parts, 384), blocks, [w_ref], sem)
        slots = rows_ref.shape[0]
        hits = slot_ref[...] == lax.broadcasted_iota(jnp.int32, (TGT, slots), 1)
        hidden = mm(hits.astype(jnp.bfloat16), rows_ref[...])
        emb_ref[...] = hidden.astype(jnp.bfloat16)
        normed = (hidden * rms_scale(hidden) * gain_ref[...]).astype(jnp.bfloat16)
        wait_whole([w_ref], sem)
        for k in range(3):
            at = pl.ds(768 * k, 768)
            qkv_ref[:, at] = mm(normed, w_ref[:, at]).astype(jnp.bfloat16)

    queries = stacked_heads(qkv_ref[:, pair_columns(j)]) * jnp.bfloat16(0.125)
    score[...] = mm_nt(queries, qkv_ref[:, pair_columns(j, 768)])

    def causal(at, shape):
        row = (at & (TGT - 1)) + lax.broadcasted_iota(jnp.int32, shape, 0)
        return lax.broadcasted_iota(jnp.int32, shape, 1) <= row

    weights = p_ref.at[0]
    softmax_rows(score, weights, 64, causal)
    mixed = mm(weights[...], qkv_ref[:, pair_columns(j, 1536)])
    mixed_ref[:, pair_columns(j)] = joined_heads(mixed).astype(jnp.bfloat16)

    @pl.when(j == PAIRS - 1)
    def _():
        h1_ref[...] = emb_ref[...].astype(jnp.float32) + mm(mixed_ref[...], w_ref[:, 2304:])


def full(*shape):
    return pl.BlockSpec(shape, lambda j: (0,) * len(shape))


def shaped(dtype, *shape):
    return jax.ShapeDtypeStruct(shape, dtype)


def params(mib=56):
    return pltpu.CompilerParams(vmem_limit_bytes=mib * 2**20)


def cost(gflop, mbytes):
    return pl.CostEstimate(
        flops=int(gflop * 1e9), bytes_accessed=int(mbytes * 1e6), transcendentals=0
    )


def self_forward(pos, rows, slot, gain, blocks):
    bf, f32 = jnp.bfloat16, jnp.float32
    return pl.pallas_call(
        self_forward_kernel,
        grid=(PAIRS,),
        in_specs=[SCALARS, full(512, D), full(TGT, 1), full(1, D)] + [HBM] * 8,
        out_specs=[
            full(TGT, D),
            full(TGT, 3 * D),
            pl.BlockSpec((1, 512, TGT), lambda j: (j, 0, 0)),
            full(TGT, D),
            full(TGT, D),
            full(D, 4 * D),
        ],
        out_shape=[
            shaped(bf, TGT, D),
            shaped(bf, TGT, 3 * D),
            shaped(bf, PAIRS, 512, TGT),
            shaped(bf, TGT, D),
            shaped(f32, TGT, D),
            shaped(bf, D, 4 * D),
        ],
        scratch_shapes=[pltpu.VMEM((512, TGT), f32), pltpu.SemaphoreType.DMA],
        compiler_params=params(),
        cost_estimate=cost(8, 12),
        name="self_forward",
    )(pos, rows, slot, gain, *blocks)


def cross_forward_kernel(pos_ref, len_ref, h1_ref, gain_ref, mem_ref, *refs):
    blocks = refs[:8]
    q_ref, k_ref, v_ref, p_ref, mixed_ref, h2_ref, w_ref, score, sem = refs[8:]
    j = pl.program_id(0)

    @pl.when(j == 0)
    def _():
        start_place(pos_ref, "y", functools.partial(square_parts, 384), blocks, [w_ref], sem)
        hidden = h1_ref[...]
        normed = (hidden * rms_scale(hidden) * gain_ref[...]).astype(jnp.bfloat16)
        wait_whole([w_ref], sem)
        q_ref[...] = mm(normed, w_ref[:, :768]).astype(jnp.bfloat16)
        for out, offset in ((k_ref, 768), (v_ref, 1536)):
            for half in range(2):
                at = pl.ds(384 * half, 384)
                out[:MEM, at] = mm(mem_ref[...], w_ref[:, pl.ds(offset + 384 * half, 384)]).astype(
                    jnp.bfloat16
                )
            out[MEM:, :] = jnp.zeros((KEYS - MEM, D), jnp.bfloat16)

    queries = stacked_heads(q_ref[:, pair_columns(j)]) * jnp.bfloat16(0.125)
    score[...] = mm_nt(queries, k_ref[:, pair_columns(j)])
    reach = len_ref[0]
    weights = p_ref.at[0]
    softmax_rows(
        score, weights, 32, lambda at, shape: lax.broadcasted_iota(jnp.int32, shape, 1) < reach
    )
    mixed = mm(weights[...], v_ref[:, pair_columns(j)])
    mixed_ref[:, pair_columns(j)] = joined_heads(mixed).astype(jnp.bfloat16)

    @pl.when(j == PAIRS - 1)
    def _():
        h2_ref[...] = h1_ref[...] + mm(mixed_ref[...], w_ref[:, 2304:])


def cross_forward(pos, mem_len, h1, gain, memory, blocks):
    bf, f32 = jnp.bfloat16, jnp.float32
    return pl.pallas_call(
        cross_forward_kernel,
        grid=(PAIRS,),
        in_specs=[SCALARS, SCALARS, full(TGT, D), full(1, D), full(MEM, D)] + [HBM] * 8,
        out_specs=[
            full(TGT, D),
            full(KEYS, D),
            full(KEYS, D),
            pl.BlockSpec((1, 512, KEYS), lambda j: (j, 0, 0)),
            full(TGT, D),
            full(TGT, D),
            full(D, 4 * D),
        ],
        out_shape=[
            shaped(bf, TGT, D),
            shaped(bf, KEYS, D),
            shaped(bf, KEYS, D),
            shaped(bf, PAIRS, 512, KEYS),
            shaped(bf, TGT, D),
            shaped(f32, TGT, D),
            shaped(bf, D, 4 * D),
        ],
        scratch_shapes=[pltpu.VMEM((512, KEYS), f32), pltpu.SemaphoreType.DMA],
        compiler_params=params(),
        cost_estimate=cost(20, 20),
        name="cross_forward",
    )(pos, mem_len, h1, gain, memory, *blocks)


def ffn_kernel(rings, pos_ref, len_ref, h2_ref, gain_ref, og_ref, *refs):
    blocks = refs[:8]
    out_ref, g2_ref, dgain_ref, mine_ref, other_ref = refs[8:13]
    w_in, w_out, g_in, g_out, normed, normed_t, low, gate, up, grad, inner, da, sem = refs[13:]
    j = pl.program_id(0)
    bf, f32 = jnp.bfloat16, jnp.float32

    def kept():
        row = lax.broadcasted_iota(jnp.int32, (TGT, 1), 0)
        return row < len_ref[0]

    @pl.when(j == 0)
    def _():
        start_place(pos_ref, "z", ffn_parts, blocks, [w_in, w_out], sem)
        hidden = h2_ref[...]
        a3 = (hidden * rms_scale(hidden) * gain_ref[...]).astype(bf)
        normed[...] = a3
        normed_t[...] = a3.astype(f32).T.astype(bf)
        low[...] = jnp.where(kept(), og_ref[...], jnp.zeros((), bf))
        wait_whole([w_in, w_out], sem)

    width = 512
    gate_at = pl.ds(pl.multiple_of(j * width, width), width)
    up_at = pl.ds(pl.multiple_of(FF + j * width, width), width)
    gate[...] = mm(normed[...], w_in[:, gate_at])
    up[...] = mm(normed[...], w_in[:, up_at])
    grad[...] = mm_nt(low[...], w_out[gate_at, :])

    def unit(i, carry):
        at = pl.ds(pl.multiple_of(i * 32, 32), 32)
        g, u, d = gate[at, :], up[at, :], grad[at, :]
        square = g * g
        t = jnp.tanh(0.7978845608 * (g + 0.044715 * (g * square)))
        half = 0.5 * (1.0 + t)
        gelu = g * half
        slope = half + 0.5 * g * (1.0 - t * t) * (0.7978845608 * (1.0 + 3.0 * 0.044715 * square))
        inner[at, :] = (gelu * u).astype(bf)
        gate[at, :] = d * u * slope
        up[at, :] = d * gelu
        return carry

    lax.fori_loop(0, TGT // 32, unit, 0)
    c_gate, c_up = gate[...].astype(bf), up[...].astype(bf)
    part = mm(inner[...], w_out[gate_at, :])
    da_part = mm_nt(c_gate, w_in[:, gate_at]) + mm_nt(c_up, w_in[:, up_at])

    @pl.when(j == 0)
    def _():
        out_ref[...] = part
        da[...] = da_part

    @pl.when(j > 0)
    def _():
        out_ref[...] += part
        da[...] += da_part

    g_out[gate_at, :] = mm_tn(inner[...], low[...]).astype(bf)
    g_in[:, gate_at] = mm(normed_t[...], c_gate).astype(bf)
    g_in[:, up_at] = mm(normed_t[...], c_up).astype(bf)

    @pl.when(j == FF // width - 1)
    def _():
        start_split(pos_ref, rings, ffn_parts, [g_in, g_out], [mine_ref, other_ref], sem)
        hidden = h2_ref[...]
        out_ref[...] = jnp.where(kept(), hidden + out_ref[...], 0.0)
        back, dgain = rms_back(hidden, gain_ref[...], da[...])
        g2_ref[...] = jnp.where(kept(), og_ref[...].astype(f32), 0.0) + back
        dgain_ref[...] = dgain
        wait_whole([g_in, g_out], sem)


def ffn_both(rings, pos, tgt_len, h2, gain, out_grad, blocks):
    bf, f32 = jnp.bfloat16, jnp.float32
    pieces = shaped(bf, 4, 4, 4, BLOCK, 768)
    return pl.pallas_call(
        functools.partial(ffn_kernel, rings),
        grid=(FF // 512,),
        in_specs=[SCALARS, SCALARS, full(TGT, D), full(1, D), full(TGT, D)] + [HBM] * 8,
        out_specs=[full(TGT, D), full(TGT, D), full(1, D), HBM, HBM],
        out_shape=[shaped(f32, TGT, D), shaped(f32, TGT, D), shaped(f32, 1, D), pieces, pieces],
        scratch_shapes=[
            pltpu.VMEM((D, 2 * FF), bf),
            pltpu.VMEM((FF, D), bf),
            pltpu.VMEM((D, 2 * FF), bf),
            pltpu.VMEM((FF, D), bf),
            pltpu.VMEM((TGT, D), bf),
            pltpu.VMEM((D, TGT), bf),
            pltpu.VMEM((TGT, D), bf),
            pltpu.VMEM((TGT, 512), f32),
            pltpu.VMEM((TGT, 512), f32),
            pltpu.VMEM((TGT, 512), f32),
            pltpu.VMEM((TGT, 512), bf),
            pltpu.VMEM((TGT, D), f32),
            pltpu.SemaphoreType.DMA,
        ],
        compiler_params=params(),
        cost_estimate=cost(15, 25),
        name="ffn_both",
    )(pos, tgt_len, h2, gain, out_grad, *blocks)


def cross_backward_kernel(rings, pos_ref, h1_ref, gain_ref, g2_ref, mem_t_ref, w_ref, *refs):
    q_ref, k_ref, v_ref, p_ref, mixed_ref = refs[:5]
    dkv_ref, g1_ref, dgain_ref, mine_ref, other_ref = refs[5:10]
    grad_low, grad_mixed, grads, low, dq, whole, sem = refs[10:]
    j = pl.program_id(0)
    bf, f32 = jnp.bfloat16, jnp.float32

    @pl.when(j == 0)
    def _():
        low[...] = g2_ref[...].astype(bf)
        grad_mixed[...] = mm_nt(low[...], w_ref[:, 2304:]).astype(bf)
        whole[:, 2304:] = mm_tn(mixed_ref[...], low[...]).astype(bf)

    d_pair = stacked_heads(grad_mixed[:, pair_columns(j)])
    queries = stacked_heads(q_ref[:, pair_columns(j)])
    weights = p_ref.at[0]
    grads[...] = mm_nt(d_pair, v_ref[:, pair_columns(j)])
    softmax_back_rows(weights, grads, grad_low, 32)
    dq[:, pair_columns(j)] = (
        joined_heads(mm(grad_low[...], k_ref[:, pair_columns(j)])) * 0.125
    ).astype(bf)
    dkv_ref[:, pair_columns(j)] = (mm_tn(grad_low[...], queries) * 0.125).astype(bf)
    dkv_ref[:, pair_columns(j, 768)] = mm_tn(weights[...], d_pair).astype(bf)

    @pl.when(j == PAIRS - 1)
    def _():
        hidden = h1_ref[...]
        normed = (hidden * rms_scale(hidden) * gain_ref[...]).astype(bf)
        whole[:, :768] = mm_tn(normed, dq[...]).astype(bf)
        for k in range(4):
            at = pl.ds(768 + 384 * k, 384)
            whole[:, at] = mm(mem_t_ref[...], dkv_ref[:, pl.ds(384 * k, 384)]).astype(bf)
        start_split(
            pos_ref,
            rings,
            functools.partial(square_parts, 384),
            [whole],
            [mine_ref, other_ref],
            sem,
        )
        back, dgain = rms_back(hidden, gain_ref[...], mm_nt(dq[...], w_ref[:, :768]))
        g1_ref[...] = g2_ref[...] + back
        dgain_ref[...] = dgain
        wait_whole([whole], sem)


def cross_backward(rings, pos, h1, gain, g2, mem_t, w, q, k, v, p, mixed):
    bf, f32 = jnp.bfloat16, jnp.float32
    pieces = shaped(bf, 4, 4, 4, BLOCK, 384)
    return pl.pallas_call(
        functools.partial(cross_backward_kernel, rings),
        grid=(PAIRS,),
        in_specs=[
            SCALARS,
            full(TGT, D),
            full(1, D),
            full(TGT, D),
            full(D, KEYS),
            full(D, 4 * D),
            full(TGT, D),
            full(KEYS, D),
            full(KEYS, D),
            pl.BlockSpec((1, 512, KEYS), lambda j: (j, 0, 0)),
            full(TGT, D),
        ],
        out_specs=[full(KEYS, 2 * D), full(TGT, D), full(1, D), HBM, HBM],
        out_shape=[
            shaped(bf, KEYS, 2 * D),
            shaped(f32, TGT, D),
            shaped(f32, 1, D),
            pieces,
            pieces,
        ],
        scratch_shapes=[
            pltpu.VMEM((512, KEYS), bf),
            pltpu.VMEM((TGT, D), bf),
            pltpu.VMEM((512, KEYS), f32),
            pltpu.VMEM((TGT, D), bf),
            pltpu.VMEM((TGT, D), bf),
            pltpu.VMEM((D, 4 * D), bf),
            pltpu.SemaphoreType.DMA,
        ],
        compiler_params=params(),
        cost_estimate=cost(25, 30),
        name="cross_backward",
    )(pos, h1, gain, g2, mem_t, w, q, k, v, p, mixed)


def self_backward_kernel(pos_ref, slot_ref, emb_ref, gain_ref, g1_ref, w_ref, *refs):
    qkv_ref, p_ref, mixed_ref, out_ref, dgain_ref, mine_ref, other_ref = refs[:7]
    grad_low, grad_mixed, grads, low, dqkv, whole, sem = refs[7:]
    j = pl.program_id(0)
    bf, f32 = jnp.bfloat16, jnp.float32

    @pl.when(j == 0)
    def _():
        low[...] = g1_ref[...].astype(bf)
        grad_mixed[...] = mm_nt(low[...], w_ref[:, 2304:]).astype(bf)
        whole[:, 2304:] = mm_tn(mixed_ref[...], low[...]).astype(bf)

    d_pair = stacked_heads(grad_mixed[:, pair_columns(j)])
    queries = stacked_heads(qkv_ref[:, pair_columns(j)])
    weights = p_ref.at[0]
    grads[...] = mm_nt(d_pair, qkv_ref[:, pair_columns(j, 1536)])
    softmax_back_rows(weights, grads, grad_low, 64)
    dqkv[:, pair_columns(j)] = (
        joined_heads(mm(grad_low[...], qkv_ref[:, pair_columns(j, 768)])) * 0.125
    ).astype(bf)
    dqkv[:, pair_columns(j, 768)] = (mm_tn(grad_low[...], queries) * 0.125).astype(bf)
    dqkv[:, pair_columns(j, 1536)] = mm_tn(weights[...], d_pair).astype(bf)

    @pl.when(j == PAIRS - 1)
    def _():
        hidden = emb_ref[...].astype(f32)
        normed = (hidden * rms_scale(hidden) * gain_ref[...]).astype(bf)
        for k in range(3):
            at = pl.ds(768 * k, 768)
            whole[:, at] = mm_tn(normed, dqkv[:, at]).astype(bf)
        start_split_whole(pos_ref, whole, [mine_ref, other_ref], sem)
        back, dgain = rms_back(hidden, gain_ref[...], mm_nt(dqkv[...], w_ref[:, :2304]))
        dgain_ref[...] = dgain
        hits = slot_ref[...] == lax.broadcasted_iota(jnp.int32, (TGT, out_ref.shape[0]), 1)
        out_ref[...] = mm_tn(hits.astype(bf), (g1_ref[...] + back).astype(bf)).astype(bf)
        wait_whole([whole], sem)


def self_backward(pos, slot, emb, gain, g1, w, qkv, p, mixed):
    bf, f32 = jnp.bfloat16, jnp.float32
    pieces = shaped(bf, 64, BLOCK, 384)
    return pl.pallas_call(
        self_backward_kernel,
        grid=(PAIRS,),
        in_specs=[
            SCALARS,
            full(TGT, 1),
            full(TGT, D),
            full(1, D),
            full(TGT, D),
            full(D, 4 * D),
            full(TGT, 3 * D),
            pl.BlockSpec((1, 512, TGT), lambda j: (j, 0, 0)),
            full(TGT, D),
        ],
        out_specs=[full(512, D), full(1, D), HBM, HBM],
        out_shape=[shaped(bf, 512, D), shaped(f32, 1, D), pieces, pieces],
        scratch_shapes=[
            pltpu.VMEM((512, TGT), bf),
            pltpu.VMEM((TGT, D), bf),
            pltpu.VMEM((512, TGT), f32),
            pltpu.VMEM((TGT, D), bf),
            pltpu.VMEM((TGT, 3 * D), bf),
            pltpu.VMEM((D, 4 * D), bf),
            pltpu.SemaphoreType.DMA,
        ],
        compiler_params=params(),
        cost_estimate=cost(10, 15),
        name="self_backward",
    )(pos, slot, emb, gain, g1, w, qkv, p, mixed)


def all_weights(self_qkv, self_out, cross_qkv, cross_out, ffn_in, ffn_out):
    def chunks(v):
        return v.reshape(6, 8, -1).swapaxes(0, 1)

    flat = [
        jnp.concatenate([jnp.swapaxes(qkv, 0, 1).reshape(6, -1), out], axis=1)
        for qkv, out in ((self_qkv, self_out), (cross_qkv, cross_out))
    ]
    flat.append(jnp.swapaxes(ffn_in, 0, 1).reshape(6, -1))
    turned = jnp.concatenate([chunks(v) for v in flat], axis=2)
    turned = lax.all_to_all(turned, EIGHT, 0, 0, tiled=True).reshape(BLOCK, -1)
    tail = ffn_out.reshape(16, 3, 256).swapaxes(0, 1).reshape(BLOCK, 256)
    piece = jnp.concatenate([turned, tail], axis=1)
    piece = gather_ring(piece, RING_X)
    attention = gather_ring(piece[:, :, :768], RING_Z)
    feed = gather_ring(piece[:, :, 768:], RING_Y)
    self_all = gather_last(attention[:, :, :, :384], RING_Y)
    cross_all = gather_last(attention[:, :, :, 384:], RING_Y)
    feed_all = gather_last(feed, RING_Z)
    return self_all, cross_all, feed_all


def body(
    target_ids,
    tgt_len,
    mem_len,
    embed_table,
    memory,
    self_qkv,
    self_out,
    gain_self,
    cross_qkv,
    cross_out,
    gain_cross,
    ffn_in,
    ffn_out,
    gain_ffn,
    out_grad,
):
    tgt_count = target_ids.shape[1]
    model_width = memory.shape[2]
    own_rows = embed_table.shape[0]
    owner_count = 128
    place_in = [lax.axis_index(ring) for ring in (RING_X, RING_Y, RING_Z, ("c",))]
    pos = jnp.stack(place_in).astype(jnp.int32)

    flat_ids = target_ids.reshape(tgt_count)
    owner_of = flat_ids // own_rows
    local_row = flat_ids - owner_of * own_rows
    owner_hits = (owner_of[:, None] == jnp.arange(owner_count)[None, :]).astype(jnp.int32)
    row_rank = jnp.sum(jnp.cumsum(owner_hits, axis=0) * owner_hits, axis=1) - 1
    slot_index = owner_of * SLOTS + row_rank
    slot_hits = slot_index[:, None] == jnp.arange(owner_count * SLOTS)[None, :]
    wanted = jnp.sum(jnp.where(slot_hits, local_row[:, None] + 1, 0), axis=0)
    gains = jnp.concatenate([gain_self, gain_cross, gain_ffn]).astype(jnp.float32)
    request = jnp.concatenate(
        [
            wanted.astype(jnp.float32).reshape(owner_count, SLOTS),
            jnp.broadcast_to(gains[None], (owner_count, GAINS)),
            jnp.zeros((owner_count, 32 - SLOTS - GAINS), jnp.float32),
        ],
        axis=1,
    )
    arrived = lax.all_to_all(request, AXES, split_axis=0, concat_axis=0, tiled=True)
    gain_self_all, gain_cross_all, gain_ffn_all = (
        arrived[:, SLOTS + 6 * k : SLOTS + 6 * k + 6].reshape(1, model_width) for k in range(3)
    )
    rows_wanted = arrived[:, :SLOTS].reshape(owner_count * SLOTS).astype(jnp.int32) - 1
    row_hits = (rows_wanted[:, None] == jnp.arange(own_rows)[None, :]).astype(jnp.bfloat16)
    fetched = jnp.dot(row_hits, embed_table, preferred_element_type=jnp.float32)
    fetched = fetched.astype(jnp.bfloat16).reshape(owner_count, SLOTS, model_width)
    returned = lax.all_to_all(fetched, AXES, split_axis=0, concat_axis=0, tiled=True)
    self_all, cross_all, feed_all = all_weights(
        self_qkv, self_out, cross_qkv, cross_out, ffn_in, ffn_out
    )
    slot = slot_index.reshape(tgt_count, 1)
    memory_rows = memory[0]
    memory_turned = jnp.pad(memory_rows.T, ((0, 0), (0, KEYS - MEM)))

    embedded, self_proj, self_p, self_mixed, hidden_one, self_w = self_forward(
        pos, returned.reshape(owner_count * SLOTS, model_width), slot, gain_self_all, self_all
    )
    query, key, value, cross_p, cross_mixed, hidden_two, cross_w = cross_forward(
        pos, mem_len, hidden_one, gain_cross_all, memory_rows, cross_all
    )
    rings = ("x", "y", "z")
    result, grad_two, gain_ffn_grad, mine, other = ffn_both(
        rings, pos, tgt_len, hidden_two, gain_ffn_all, out_grad[0], feed_all
    )
    ffn_sum = ring_sum(mine, other, rings)
    rings = ("z", "x", "y")
    grad_kv, grad_one, gain_cross_grad, mine, other = cross_backward(
        rings, pos, hidden_one, gain_cross_all, grad_two, memory_turned, cross_w,
        query, key, value, cross_p, cross_mixed,
    )
    cross_sum = ring_sum(mine, other, rings)
    outgoing, gain_self_grad, mine, other = self_backward(
        pos, slot, embedded, gain_self_all, grad_one, self_w, self_proj, self_p, self_mixed
    )
    self_sum = lax.all_to_all(add_low(mine, swap_cores(other)), CHIPS, 0, 0, tiled=True)
    self_sum = jnp.sum(self_sum.astype(jnp.float32), axis=0)
    memory_grad = jnp.einsum(
        "me,de->md", grad_kv[:MEM], cross_w[:, 768:2304], preferred_element_type=jnp.float32
    )[None]

    gain_parts = jnp.concatenate(
        [
            g.astype(jnp.bfloat16).reshape(owner_count, 6)
            for g in (gain_self_grad, gain_cross_grad, gain_ffn_grad)
        ],
        axis=1,
    )
    extra = jnp.pad(gain_parts[:, None, :], ((0, 0), (0, SLOTS - 1), (0, 128 - GAINS)))
    outgoing = jnp.concatenate([outgoing.reshape(owner_count, SLOTS, model_width), extra], axis=2)
    incoming = lax.all_to_all(outgoing, AXES, split_axis=0, concat_axis=0, tiled=True)
    gain_sums = jnp.sum(
        incoming[:, 0, model_width : model_width + GAINS].astype(jnp.float32), axis=0
    )
    table_grad = jnp.einsum(
        "sr,sd->rd",
        row_hits,
        incoming[:, :, :model_width].reshape(owner_count * SLOTS, model_width),
        preferred_element_type=jnp.float32,
    )

    turned = jnp.concatenate([self_sum, cross_sum, ffn_sum[:, :512]], axis=1)
    turned = lax.all_to_all(turned.reshape(8, 6, -1), EIGHT, 0, 0, tiled=True)

    def rows_of(v):
        return jnp.swapaxes(v, 0, 1).reshape(6, -1)

    done = []
    for at in (0, 384):
        whole = rows_of(turned[:, :, at : at + 384])
        done.append(jnp.swapaxes(whole[:, :2304].reshape(6, 3, model_width), 0, 1))
        done.append(whole[:, 2304:])
    ffn_in_sum = jnp.swapaxes(rows_of(turned[:, :, 768:]).reshape(6, 2, 2048), 0, 1)
    ffn_out_sum = ffn_sum[:, 512:].reshape(3, 16, 256).swapaxes(0, 1).reshape(16, model_width)
    return (
        result[None],
        memory_grad,
        table_grad,
        done[0],
        done[1],
        gain_sums[:6],
        done[2],
        done[3],
        gain_sums[6:12],
        ffn_in_sum,
        ffn_out_sum,
        gain_sums[12:18],
    )


def solution(mesh):
    fine = Mesh(mesh.devices.reshape(SIZES), AXES)
    in_specs = (
        P(AXES, None),
        P(AXES),
        P(AXES),
        P(AXES, None),
        P(AXES, None, None),
        P(None, AXES, None),
        P(AXES, None),
        P(AXES),
        P(None, AXES, None),
        P(AXES, None),
        P(AXES),
        P(None, AXES, None),
        P(AXES, None),
        P(AXES),
        P(AXES, None, None),
    )
    out_specs = (
        P(AXES, None, None),
        P(AXES, None, None),
        P(AXES, None),
        P(None, AXES, None),
        P(AXES, None),
        P(AXES),
        P(None, AXES, None),
        P(AXES, None),
        P(AXES),
        P(None, AXES, None),
        P(AXES, None),
        P(AXES),
    )
    return jax.shard_map(body, mesh=fine, in_specs=in_specs, out_specs=out_specs, check_vma=False)
```

```python
import functools

import jax
import jax.numpy as jnp
from jax import lax
from jax.experimental import pallas as pl
from jax.experimental.pallas import tpu as pltpu
from jax.sharding import Mesh, PartitionSpec as P

HEAD_SIZE = 64
D = 768
FF = 2048
TGT = 256
MEM = 1056
KEYS = 1152
PAIRS = 6
SELF_FORWARD, CROSS_FORWARD, CROSS_BACKWARD, SELF_BACKWARD = 6, 6, 2, 3


eps = 1e-06
masked_score = -1e30

AXES = ("x", "yh", "zh", "zl", "yl", "c")
SIZES = (4, 2, 2, 2, 2, 2)
RING_X, RING_Y, RING_Z = ("x",), ("yh", "yl"), ("zh", "zl")
RINGS = {"x": RING_X, "y": RING_Y, "z": RING_Z}
TORUS = RING_X + RING_Y + RING_Z + ("c",)
CHIPS = ("x", "yh", "zh", "zl", "yl")
EIGHT = ("zl", "yl", "c")
BLOCK = 48
SLOTS = 4
GAINS = 18

HBM = pl.BlockSpec(memory_space=pl.ANY)
SCALARS = pl.BlockSpec(memory_space=pltpu.SMEM)


def ring_pair(v, ring, first):
    perm = []
    for i in range(4):
        for c in range(2):
            perm.append((2 * i + c, 2 * (i ^ (1 if (c == 0) == first else 3)) + c))
    return lax.ppermute(v, ring + ("c",), perm)


def swap_cores(v):
    return lax.ppermute(v, "c", [(0, 1), (1, 0)])


def then(v, *tokens):
    return lax.optimization_barrier((v, *tokens))[0]


def add_low(*terms):
    return sum(t.astype(jnp.float32) for t in terms).astype(jnp.bfloat16)


def halve(low, high, ring):
    got = ring_pair(high, ring, False)
    back = ring_pair(add_low(low[1], got[1]), ring, True)
    return low[0], got[0], back


def ring_sum(mine, other, rings):
    got = swap_cores(other)
    low, high = add_low(mine[:2], got[:2]), add_low(mine[2:], got[2:])
    for ring in rings[:-1]:
        terms = halve(low, high, RINGS[ring])
        low, high = (add_low(*(t[at] for t in terms)) for at in (slice(0, 2), slice(2, 4)))
    return sum(t.astype(jnp.float32) for t in halve(low, high, RINGS[rings[-1]]))


def mm(a, b):
    return jnp.dot(a, b, preferred_element_type=jnp.float32)


def mm_nt(a, b):
    return lax.dot_general(a, b, (((1,), (1,)), ((), ())), preferred_element_type=jnp.float32)


def mm_tn(a, b):
    return lax.dot_general(a, b, (((0,), (0,)), ((), ())), preferred_element_type=jnp.float32)


def turned(v):
    return v.astype(jnp.float32).T.astype(v.dtype)


def first_half(shape):
    return lax.broadcasted_iota(jnp.int32, shape, 1) < HEAD_SIZE


def stacked_heads(pair):
    low = first_half(pair.shape)
    zero = jnp.zeros_like(pair)
    return jnp.concatenate([jnp.where(low, pair, zero), jnp.where(low, zero, pair)], axis=0)


def joined_heads(both):
    half = both.shape[0] // 2
    return jnp.where(first_half((half, both.shape[1])), both[:half], both[half:])


def rms_scale(hidden):
    return lax.rsqrt(jnp.mean(hidden * hidden, axis=-1, keepdims=True) + eps)


def rms_back(hidden, gain, grad):
    scale = rms_scale(hidden)
    u = grad * gain
    inner = jnp.mean(u * hidden, axis=-1, keepdims=True)
    grad_hidden = scale * u - hidden * (scale * scale * scale * inner)
    return grad_hidden, jnp.sum(grad * hidden * scale, axis=0, keepdims=True)


def my_place(pos_ref):
    return {"x": pos_ref[0], "y": pos_ref[1], "z": pos_ref[2]}


def group_member(at, core):
    group = at["x"] * 4 + (at["y"] >> 1) * 2 + (at["z"] >> 1)
    return group, (at["z"] & 1) * 4 + (at["y"] & 1) * 2 + core


def partners(core):
    return (0, 1 + 2 * core, 3 - 2 * core, 2)


def square_parts(width, group, member):
    row = pl.multiple_of(group * BLOCK, 16)
    column = pl.multiple_of(member * width, 128)
    return [((slice(None), slice(None)), 0, (pl.ds(row, BLOCK), pl.ds(column, width)))]


def torus():
    return [(x, y, z, c) for x in range(4) for y in range(4) for z in range(4) for c in range(2)]


def block_place(x, y, z, c):
    return x * 4 + (y // 2) * 2 + z // 2, (z % 2) * 4 + (y % 2) * 2 + c


def start_place(blocks, first, out, sem):
    for at in torus():
        group, member = block_place(*at)
        pltpu.make_async_copy(
            blocks.at[at + (slice(None), pl.ds(first, 384))],
            out.at[pl.ds(BLOCK * group, BLOCK), pl.ds(384 * member, 384)],
            sem,
        ).start()


def ffn_copies(j, whole_in, whole_out, block_of):
    found = []
    for at in torus():
        group, member = block_place(*at)
        block = block_of(at)
        if member % 4 == j:
            rows, columns = pl.ds(BLOCK * group, BLOCK), pl.ds(512 * member, 512)
            found.append((whole_in.at[rows, columns], block.at[:, pl.ds(768, 512)]))
        if at[0] == j:
            rows = pl.ds(16 * (8 * group + member), 16)
            for s in range(3):
                part = block.at[pl.ds(16 * s, 16), pl.ds(1280, 256)]
                found.append((whole_out.at[rows, pl.ds(256 * s, 256)], part))
    return found


def start_split(pos_ref, rings, parts, wholes, outs, sem):
    me = my_place(pos_ref)
    at = {}
    for source in range(2):
        core = pos_ref[3] ^ source
        flips = partners(core)
        for k3 in range(4):
            at[rings[0]] = me[rings[0]] ^ flips[k3]
            for k2 in range(4):
                at[rings[1]] = me[rings[1]] ^ flips[k2]
                for k1 in range(4):
                    at[rings[2]] = me[rings[2]] ^ flips[k1]
                    for dst, whole, src in parts(*group_member(at, core)):
                        pltpu.make_async_copy(
                            wholes[whole].at[src], outs[source].at[(k3, k2, k1) + dst], sem
                        ).start()


def start_split_whole(pos_ref, whole, outs, sem):
    for source in range(2):
        core = pos_ref[3] ^ source
        for group in range(16):
            for q in range(4):
                for dst, _, src in square_parts(384, group, 2 * q + core):
                    pltpu.make_async_copy(
                        whole.at[src], outs[source].at[(4 * group + q,) + dst], sem
                    ).start()


def wait_whole(refs, sem):
    for ref in refs:
        pltpu.make_async_copy(ref, ref, sem).wait()


def start_split(pos_ref, rings, parts, wholes, outs, sem):
    me = my_place(pos_ref)
    at = {}
    for source in range(2):
        core = pos_ref[3] ^ source
        flips = partners(core)
        for k3 in range(4):
            at[rings[0]] = me[rings[0]] ^ flips[k3]
            for k2 in range(4):
                at[rings[1]] = me[rings[1]] ^ flips[k2]
                for k1 in range(4):
                    at[rings[2]] = me[rings[2]] ^ flips[k1]
                    for dst, whole, src in parts(*group_member(at, core)):
                        pltpu.make_async_copy(
                            wholes[whole].at[src], outs[source].at[(k3, k2, k1) + dst], sem
                        ).start()


def start_split_whole(pos_ref, whole, outs, sem):
    for source in range(2):
        core = pos_ref[3] ^ source
        for group in range(16):
            for q in range(4):
                for dst, _, src in square_parts(384, group, 2 * q + core):
                    pltpu.make_async_copy(
                        whole.at[src], outs[source].at[(4 * group + q,) + dst], sem
                    ).start()


def softmax_low(scores, valid):
    scores = jnp.where(valid, scores, masked_score)
    expanded = jnp.exp(scores - jnp.max(scores, axis=-1, keepdims=True))
    total = jnp.sum(expanded, axis=-1, keepdims=True)
    return (expanded * (1.0 / total)).astype(jnp.bfloat16)


def softmax_back(weights, grads):
    weights = weights.astype(jnp.float32)
    inner = jnp.sum(weights * grads, axis=-1, keepdims=True)
    return (weights * (grads - inner)).astype(jnp.bfloat16)


def pair_columns(j, offset=0):
    return pl.ds(pl.multiple_of(offset + j * 128, 128), 128)


def pairs_here(together):
    j = pl.program_id(0)
    return [(s, j * together + s) for s in range(together)]


def self_forward_kernel(rows_ref, slot_ref, gain_ref, early_ref, blocks, *refs):
    emb_ref, qkv_ref, p_ref, mixed_ref, h1_ref, w_ref, sem = refs
    j = pl.program_id(0)

    @pl.when(j == 0)
    def _():
        start_place(blocks, 0, w_ref, sem)
        slots = rows_ref.shape[0]
        hits = slot_ref[...] == lax.broadcasted_iota(jnp.int32, (TGT, slots), 1)
        hidden = mm(hits.astype(jnp.bfloat16), rows_ref[...])
        emb_ref[...] = hidden.astype(jnp.bfloat16)
        normed = (hidden * rms_scale(hidden) * gain_ref[...]).astype(jnp.bfloat16)
        wait_whole([w_ref], sem)
        for k in range(3):
            at = pl.ds(768 * k, 768)
            qkv_ref[:, at] = mm(normed, w_ref[:, at]).astype(jnp.bfloat16)

    row = lax.broadcasted_iota(jnp.int32, (2 * TGT, TGT), 0) & (TGT - 1)
    causal = lax.broadcasted_iota(jnp.int32, (2 * TGT, TGT), 1) <= row
    for s, pair in pairs_here(SELF_FORWARD):
        queries = stacked_heads(qkv_ref[:, pair_columns(pair)]) * jnp.bfloat16(0.125)
        weights = softmax_low(mm_nt(queries, qkv_ref[:, pair_columns(pair, 768)]), causal)
        p_ref[s] = weights
        mixed = mm(weights, qkv_ref[:, pair_columns(pair, 1536)])
        mixed_ref[:, pair_columns(pair)] = joined_heads(mixed).astype(jnp.bfloat16)

    @pl.when(j == PAIRS // SELF_FORWARD - 1)
    def _():
        h1_ref[...] = emb_ref[...].astype(jnp.float32) + mm(mixed_ref[...], w_ref[:, 2304:])


def full(*shape):
    return pl.BlockSpec(shape, lambda j: (0,) * len(shape))


def shaped(dtype, *shape):
    return jax.ShapeDtypeStruct(shape, dtype)


def params(mib=56):
    return pltpu.CompilerParams(vmem_limit_bytes=mib * 2**20)


def cost(gflop, mbytes):
    return pl.CostEstimate(
        flops=int(gflop * 1e9), bytes_accessed=int(mbytes * 1e6), transcendentals=0
    )


def self_forward(rows, slot, gain, early, blocks):
    bf, f32 = jnp.bfloat16, jnp.float32
    return pl.pallas_call(
        self_forward_kernel,
        grid=(PAIRS // SELF_FORWARD,),
        in_specs=[full(512, D), full(TGT, 1), full(1, D), HBM, HBM],
        out_specs=[
            full(TGT, D),
            full(TGT, 3 * D),
            pl.BlockSpec((SELF_FORWARD, 512, TGT), lambda j: (j, 0, 0)),
            full(TGT, D),
            full(TGT, D),
            full(D, 4 * D),
        ],
        out_shape=[
            shaped(bf, TGT, D),
            shaped(bf, TGT, 3 * D),
            shaped(bf, PAIRS, 512, TGT),
            shaped(bf, TGT, D),
            shaped(f32, TGT, D),
            shaped(bf, D, 4 * D),
        ],
        scratch_shapes=[pltpu.SemaphoreType.DMA],
        compiler_params=params(),
        cost_estimate=cost(8, 12),
        name="self_forward",
    )(rows, slot, gain, early, blocks)


def cross_forward_kernel(len_ref, h1_ref, gain_ref, mem_ref, blocks, *refs):
    q_ref, k_ref, v_ref, p_ref, mixed_ref, h2_ref, w_ref, sem = refs
    j = pl.program_id(0)

    @pl.when(j == 0)
    def _():
        start_place(blocks, 384, w_ref, sem)
        hidden = h1_ref[...]
        normed = (hidden * rms_scale(hidden) * gain_ref[...]).astype(jnp.bfloat16)
        wait_whole([w_ref], sem)
        q_ref[...] = mm(normed, w_ref[:, :768]).astype(jnp.bfloat16)
        for out, offset in ((k_ref, 768), (v_ref, 1536)):
            for half in range(2):
                at = pl.ds(384 * half, 384)
                out[:MEM, at] = mm(mem_ref[...], w_ref[:, pl.ds(offset + 384 * half, 384)]).astype(
                    jnp.bfloat16
                )
            out[MEM:, :] = jnp.zeros((KEYS - MEM, D), jnp.bfloat16)

    reach = lax.broadcasted_iota(jnp.int32, (2 * TGT, KEYS), 1) < len_ref[0]
    for s, pair in pairs_here(CROSS_FORWARD):
        queries = stacked_heads(q_ref[:, pair_columns(pair)]) * jnp.bfloat16(0.125)
        weights = softmax_low(mm_nt(queries, k_ref[:, pair_columns(pair)]), reach)
        p_ref[s] = weights
        mixed = mm(weights, v_ref[:, pair_columns(pair)])
        mixed_ref[:, pair_columns(pair)] = joined_heads(mixed).astype(jnp.bfloat16)

    @pl.when(j == PAIRS // CROSS_FORWARD - 1)
    def _():
        h2_ref[...] = h1_ref[...] + mm(mixed_ref[...], w_ref[:, 2304:])


def cross_forward(mem_len, h1, gain, memory, blocks):
    bf, f32 = jnp.bfloat16, jnp.float32
    return pl.pallas_call(
        cross_forward_kernel,
        grid=(PAIRS // CROSS_FORWARD,),
        in_specs=[SCALARS, full(TGT, D), full(1, D), full(MEM, D), HBM],
        out_specs=[
            full(TGT, D),
            full(KEYS, D),
            full(KEYS, D),
            pl.BlockSpec((CROSS_FORWARD, 512, KEYS), lambda j: (j, 0, 0)),
            full(TGT, D),
            full(TGT, D),
            full(D, 4 * D),
        ],
        out_shape=[
            shaped(bf, TGT, D),
            shaped(bf, KEYS, D),
            shaped(bf, KEYS, D),
            shaped(bf, PAIRS, 512, KEYS),
            shaped(bf, TGT, D),
            shaped(f32, TGT, D),
            shaped(bf, D, 4 * D),
        ],
        scratch_shapes=[pltpu.SemaphoreType.DMA],
        compiler_params=params(),
        cost_estimate=cost(20, 20),
        name="cross_forward",
    )(mem_len, h1, gain, memory, blocks)


class piece_of:
    def __init__(self, ref):
        self.ref = ref

    @property
    def at(self):
        return self

    def __getitem__(self, place):
        rows, columns = place
        return self.ref.at[rows, pl.ds(columns.start - 768, columns.size)]


def ffn_kernel(len_ref, h2_ref, gain_ref, og_ref, blocks, *refs):
    out_ref, g2_ref, dgain_ref, pieces = refs[:4]
    w_in, w_out, g_in, g_out, normed, normed_t, low, gate, up, grad, inner, da, sems, sem = refs[4:]
    j = pl.program_id(0)
    bf, f32 = jnp.bfloat16, jnp.float32

    def kept():
        row = lax.broadcasted_iota(jnp.int32, (TGT, 1), 0)
        return row < len_ref[0]

    @pl.when(j == 0)
    def _():
        for quarter in range(FF // 512):
            for whole, block in ffn_copies(quarter, w_in, w_out, lambda at: blocks.at[at]):
                pltpu.make_async_copy(block, whole, sems.at[quarter]).start()
        hidden = h2_ref[...]
        a3 = (hidden * rms_scale(hidden) * gain_ref[...]).astype(bf)
        normed[...] = a3
        normed_t[...] = a3.astype(f32).T.astype(bf)
        low[...] = jnp.where(kept(), og_ref[...], jnp.zeros((), bf))

    width = 512
    gate_at = pl.ds(pl.multiple_of(j * width, width), width)
    up_at = pl.ds(pl.multiple_of(FF + j * width, width), width)
    wait_whole([w_in.at[:, gate_at], w_in.at[:, up_at], w_out.at[gate_at, :]], sems.at[j])
    gate[...] = mm(normed[...], w_in[:, gate_at])
    up[...] = mm(normed[...], w_in[:, up_at])
    grad[...] = mm_nt(low[...], w_out[gate_at, :])

    def unit(i, carry):
        at = pl.ds(pl.multiple_of(i * 32, 32), 32)
        g, u, d = gate[at, :], up[at, :], grad[at, :]
        square = g * g
        t = jnp.tanh(0.7978845608 * (g + 0.044715 * (g * square)))
        half = 0.5 * (1.0 + t)
        gelu = g * half
        slope = half + 0.5 * g * (1.0 - t * t) * (0.7978845608 * (1.0 + 3.0 * 0.044715 * square))
        inner[at, :] = (gelu * u).astype(bf)
        gate[at, :] = d * u * slope
        up[at, :] = d * gelu
        return carry

    lax.fori_loop(0, TGT // 32, unit, 0, unroll=True)
    c_gate, c_up = gate[...].astype(bf), up[...].astype(bf)
    part = mm(inner[...], w_out[gate_at, :])
    da_part = mm_nt(c_gate, w_in[:, gate_at]) + mm_nt(c_up, w_in[:, up_at])

    @pl.when(j == 0)
    def _():
        out_ref[...] = part
        da[...] = da_part

    @pl.when(j > 0)
    def _():
        out_ref[...] += part
        da[...] += da_part

    g_out[gate_at, :] = mm_tn(inner[...], low[...]).astype(bf)
    g_in[:, gate_at] = mm(normed_t[...], c_gate).astype(bf)
    g_in[:, up_at] = mm(normed_t[...], c_up).astype(bf)

    for quarter in range(FF // width):

        @pl.when(j == quarter)
        def _():
            for whole, block in ffn_copies(
                quarter, g_in, g_out, lambda at: piece_of(pieces.at[at[0], at[3], at[1], at[2]])
            ):
                pltpu.make_async_copy(whole, block, sem).start()

    @pl.when(j == FF // width - 1)
    def _():
        hidden = h2_ref[...]
        out_ref[...] = jnp.where(kept(), hidden + out_ref[...], 0.0)
        back, dgain = rms_back(hidden, gain_ref[...], da[...])
        g2_ref[...] = jnp.where(kept(), og_ref[...].astype(f32), 0.0) + back
        dgain_ref[...] = dgain
        wait_whole([g_in, g_out], sem)


def ffn_both(tgt_len, h2, gain, out_grad, blocks):
    bf, f32 = jnp.bfloat16, jnp.float32
    pieces = shaped(bf, 4, 2, 4, 4, BLOCK, 768)
    return pl.pallas_call(
        ffn_kernel,
        grid=(FF // 512,),
        in_specs=[SCALARS, full(TGT, D), full(1, D), full(TGT, D), HBM],
        out_specs=[full(TGT, D), full(TGT, D), full(1, D), HBM],
        out_shape=[shaped(f32, TGT, D), shaped(f32, TGT, D), shaped(f32, 1, D), pieces],
        scratch_shapes=[
            pltpu.VMEM((D, 2 * FF), bf),
            pltpu.VMEM((FF, D), bf),
            pltpu.VMEM((D, 2 * FF), bf),
            pltpu.VMEM((FF, D), bf),
            pltpu.VMEM((TGT, D), bf),
            pltpu.VMEM((D, TGT), bf),
            pltpu.VMEM((TGT, D), bf),
            pltpu.VMEM((TGT, 512), f32),
            pltpu.VMEM((TGT, 512), f32),
            pltpu.VMEM((TGT, 512), f32),
            pltpu.VMEM((TGT, 512), bf),
            pltpu.VMEM((TGT, D), f32),
            pltpu.SemaphoreType.DMA((FF // 512,)),
            pltpu.SemaphoreType.DMA,
        ],
        compiler_params=params(),
        cost_estimate=cost(15, 25),
        name="ffn_both",
    )(tgt_len, h2, gain, out_grad, blocks)


def cross_backward_kernel(h1_ref, gain_ref, g2_ref, w_ref, q_ref, k_ref, v_ref, p_ref, *refs):
    dq, dkv_ref, g1_ref, dgain_ref, grad_mixed = refs
    j = pl.program_id(0)
    bf = jnp.bfloat16

    @pl.when(j == 0)
    def _():
        grad_mixed[...] = mm_nt(g2_ref[...].astype(bf), w_ref[:, 2304:]).astype(bf)

    for s, pair in pairs_here(CROSS_BACKWARD):
        at = pair_columns(pair)
        d_pair = stacked_heads(grad_mixed[:, at])
        queries = stacked_heads(q_ref[:, at])
        weights = p_ref[s]
        grads = softmax_back(weights, mm_nt(d_pair, v_ref[:, at]))
        dq[:, at] = (joined_heads(mm(grads, k_ref[:, at])) * 0.125).astype(bf)
        dkv_ref[:, at] = (mm(turned(queries), grads) * 0.125).T.astype(bf)
        dkv_ref[:, pair_columns(pair, 768)] = mm(turned(d_pair), weights).T.astype(bf)

    @pl.when(j == PAIRS // CROSS_BACKWARD - 1)
    def _():
        back, dgain = rms_back(h1_ref[...], gain_ref[...], mm_nt(dq[...], w_ref[:, :768]))
        g1_ref[...] = g2_ref[...] + back
        dgain_ref[...] = dgain


def cross_backward(h1, gain, g2, w, q, k, v, p):
    bf, f32 = jnp.bfloat16, jnp.float32
    return pl.pallas_call(
        cross_backward_kernel,
        grid=(PAIRS // CROSS_BACKWARD,),
        in_specs=[
            full(TGT, D),
            full(1, D),
            full(TGT, D),
            full(D, 4 * D),
            full(TGT, D),
            full(KEYS, D),
            full(KEYS, D),
            pl.BlockSpec((CROSS_BACKWARD, 512, KEYS), lambda j: (j, 0, 0)),
        ],
        out_specs=[full(TGT, D), full(KEYS, 2 * D), full(TGT, D), full(1, D)],
        out_shape=[
            shaped(bf, TGT, D),
            shaped(bf, KEYS, 2 * D),
            shaped(f32, TGT, D),
            shaped(f32, 1, D),
        ],
        scratch_shapes=[pltpu.VMEM((TGT, D), bf)],
        compiler_params=params(),
        cost_estimate=cost(16, 20),
        name="cross_backward",
    )(h1, gain, g2, w, q, k, v, p)


def cross_grads_kernel(
    rings, pos_ref, h1_ref, gain_ref, g2_ref, mem_t_ref, mixed_ref, dq_ref, dkv_ref, *refs
):
    mine_ref, other_ref, whole, sem = refs
    bf = jnp.bfloat16
    hidden = h1_ref[...]
    normed = (hidden * rms_scale(hidden) * gain_ref[...]).astype(bf)
    whole[:, :768] = mm_tn(normed, dq_ref[...]).astype(bf)
    whole[:, 2304:] = mm_tn(mixed_ref[...], g2_ref[...].astype(bf)).astype(bf)
    for k in range(4):
        at = pl.ds(768 + 384 * k, 384)
        whole[:, at] = mm(mem_t_ref[...], dkv_ref[:, pl.ds(384 * k, 384)]).astype(bf)
    parts = functools.partial(square_parts, 384)
    start_split(pos_ref, rings, parts, [whole], [mine_ref, other_ref], sem)
    wait_whole([whole], sem)


def cross_grads(rings, pos, h1, gain, g2, mem_t, mixed, dq, dkv):
    bf = jnp.bfloat16
    pieces = shaped(bf, 4, 4, 4, BLOCK, 384)
    return pl.pallas_call(
        functools.partial(cross_grads_kernel, rings),
        in_specs=[SCALARS] + [pl.BlockSpec(memory_space=pltpu.VMEM)] * 7,
        out_specs=[HBM, HBM],
        out_shape=[pieces, pieces],
        scratch_shapes=[pltpu.VMEM((D, 4 * D), bf), pltpu.SemaphoreType.DMA],
        compiler_params=params(),
        cost_estimate=cost(6, 12),
        name="cross_grads",
    )(pos, h1, gain, g2, mem_t, mixed, dq, dkv)


def self_backward_kernel(slot_ref, emb_ref, gain_ref, g1_ref, w_ref, qkv_ref, p_ref, *refs):
    dg2_ref, dg3_ref, dqkv, out_ref, grad_mixed = refs
    j = pl.program_id(0)
    bf, f32 = jnp.bfloat16, jnp.float32

    @pl.when(j == 0)
    def _():
        grad_mixed[...] = mm_nt(g1_ref[...].astype(bf), w_ref[:, 2304:]).astype(bf)

    for s, pair in pairs_here(SELF_BACKWARD):
        at = pair_columns(pair)
        d_pair = stacked_heads(grad_mixed[:, at])
        queries = stacked_heads(qkv_ref[:, at])
        weights = p_ref[s]
        grads = softmax_back(weights, mm_nt(d_pair, qkv_ref[:, pair_columns(pair, 1536)]))
        dqkv[:, at] = (joined_heads(mm(grads, qkv_ref[:, pair_columns(pair, 768)])) * 0.125).astype(bf)
        dqkv[:, pair_columns(pair, 768)] = (mm_tn(grads, queries) * 0.125).astype(bf)
        dqkv[:, pair_columns(pair, 1536)] = mm_tn(weights, d_pair).astype(bf)

    @pl.when(j == PAIRS // SELF_BACKWARD - 1)
    def _():
        hidden = emb_ref[...].astype(f32)
        back, dgain = rms_back(hidden, gain_ref[...], mm_nt(dqkv[...], w_ref[:, :2304]))
        slots = out_ref.shape[0]
        hits = slot_ref[...] == lax.broadcasted_iota(jnp.int32, (TGT, slots), 1)
        out_ref[:, :D] = mm_tn(hits.astype(bf), (g1_ref[...] + back).astype(bf)).astype(bf)
        row = lax.broadcasted_iota(jnp.int32, (slots, D), 0)
        feature = lax.broadcasted_iota(jnp.int32, (slots, D), 1)
        first = (row // SLOTS) * 6
        owned = (row % SLOTS == 0) & (feature >= first) & (feature < first + 6)
        lane = lax.broadcasted_iota(jnp.int32, (D, 128), 1)
        place = lax.broadcasted_iota(jnp.int32, (D, 128), 0) % 6
        extra = jnp.zeros((slots, 128), f32)
        for k, grad in enumerate((dgain, dg2_ref[...], dg3_ref[...])):
            spread = jnp.where(owned, grad, 0.0).astype(bf)
            extra += mm(spread, (lane == place + 6 * k).astype(bf))
        out_ref[:, D:] = extra.astype(bf)


def self_backward(slot, emb, gain, g1, w, qkv, p, dg2, dg3):
    bf = jnp.bfloat16
    return pl.pallas_call(
        self_backward_kernel,
        grid=(PAIRS // SELF_BACKWARD,),
        in_specs=[
            full(TGT, 1),
            full(TGT, D),
            full(1, D),
            full(TGT, D),
            full(D, 4 * D),
            full(TGT, 3 * D),
            pl.BlockSpec((SELF_BACKWARD, 512, TGT), lambda j: (j, 0, 0)),
            full(1, D),
            full(1, D),
        ],
        out_specs=[full(TGT, 3 * D), full(512, D + 128)],
        out_shape=[shaped(bf, TGT, 3 * D), shaped(bf, 512, D + 128)],
        scratch_shapes=[pltpu.VMEM((TGT, D), bf)],
        compiler_params=params(),
        cost_estimate=cost(8, 10),
        name="self_backward",
    )(slot, emb, gain, g1, w, qkv, p, dg2, dg3)


def self_grads_kernel(pos_ref, emb_ref, gain_ref, g1_ref, mixed_ref, dqkv_ref, *refs):
    mine_ref, other_ref, whole, sem = refs
    bf, f32 = jnp.bfloat16, jnp.float32
    hidden = emb_ref[...].astype(f32)
    normed = turned((hidden * rms_scale(hidden) * gain_ref[...]).astype(bf))
    for k in range(3):
        at = pl.ds(768 * k, 768)
        whole[:, at] = mm(normed, dqkv_ref[:, at]).astype(bf)
    whole[:, 2304:] = mm_tn(mixed_ref[...], g1_ref[...].astype(bf)).astype(bf)
    start_split_whole(pos_ref, whole, [mine_ref, other_ref], sem)
    wait_whole([whole], sem)


def self_grads(pos, emb, gain, g1, mixed, dqkv):
    bf = jnp.bfloat16
    pieces = shaped(bf, 64, BLOCK, 384)
    return pl.pallas_call(
        self_grads_kernel,
        in_specs=[SCALARS] + [pl.BlockSpec(memory_space=pltpu.VMEM)] * 5,
        out_specs=[HBM, HBM],
        out_shape=[pieces, pieces],
        scratch_shapes=[pltpu.VMEM((D, 4 * D), bf), pltpu.SemaphoreType.DMA],
        compiler_params=params(),
        cost_estimate=cost(3, 8),
        name="self_grads",
    )(pos, emb, gain, g1, mixed, dqkv)


def after(v, token):
    return v + (token * 0).astype(v.dtype)


def column_blocks(self_qkv, self_out, cross_qkv, cross_out, ffn_in):
    def chunks(v):
        return v.reshape(6, 8, -1).swapaxes(0, 1)

    flat = [
        jnp.concatenate([jnp.swapaxes(qkv, 0, 1).reshape(6, -1), out], axis=1)
        for qkv, out in ((self_qkv, self_out), (cross_qkv, cross_out))
    ]
    flat.append(jnp.swapaxes(ffn_in, 0, 1).reshape(6, -1))
    whole = jnp.concatenate([chunks(v) for v in flat], axis=2)
    return lax.all_to_all(whole, EIGHT, 0, 0, tiled=True).reshape(BLOCK, -1)


def all_weights(whole, ffn_out):
    tail = ffn_out.reshape(16, 3, 256).swapaxes(0, 1).reshape(BLOCK, 256)
    piece = jnp.concatenate([whole, tail], axis=1)
    return lax.all_gather(piece, TORUS).reshape(4, 4, 4, 2, BLOCK, -1)


def body(
    target_ids,
    tgt_len,
    mem_len,
    embed_table,
    memory,
    self_qkv,
    self_out,
    gain_self,
    cross_qkv,
    cross_out,
    gain_cross,
    ffn_in,
    ffn_out,
    gain_ffn,
    out_grad,
):
    tgt_count = target_ids.shape[1]
    model_width = memory.shape[2]
    own_rows = embed_table.shape[0]
    owner_count = 128
    place_in = [lax.axis_index(ring) for ring in (RING_X, RING_Y, RING_Z, ("c",))]
    pos = jnp.stack(place_in).astype(jnp.int32)

    flat_ids = target_ids.reshape(tgt_count)
    owner_of = flat_ids // own_rows
    local_row = flat_ids - owner_of * own_rows
    owner_hits = (owner_of[:, None] == jnp.arange(owner_count)[None, :]).astype(jnp.int32)
    row_rank = jnp.sum(jnp.cumsum(owner_hits, axis=0) * owner_hits, axis=1) - 1
    slot_index = owner_of * SLOTS + row_rank
    slot_hits = slot_index[:, None] == jnp.arange(owner_count * SLOTS)[None, :]
    wanted = jnp.sum(jnp.where(slot_hits, local_row[:, None] + 1, 0), axis=0)
    gains = jnp.concatenate([gain_self, gain_cross, gain_ffn]).astype(jnp.float32)
    request = jnp.concatenate(
        [
            wanted.astype(jnp.float32).reshape(owner_count, SLOTS),
            jnp.broadcast_to(gains[None], (owner_count, GAINS)),
            jnp.zeros((owner_count, 32 - SLOTS - GAINS), jnp.float32),
        ],
        axis=1,
    )
    whole = column_blocks(self_qkv, self_out, cross_qkv, cross_out, ffn_in)
    arrived = lax.all_to_all(then(request, whole), AXES, split_axis=0, concat_axis=0, tiled=True)
    gain_self_all, gain_cross_all, gain_ffn_all = (
        arrived[:, SLOTS + 6 * k : SLOTS + 6 * k + 6].reshape(1, model_width) for k in range(3)
    )
    rows_wanted = arrived[:, :SLOTS].reshape(owner_count * SLOTS).astype(jnp.int32) - 1
    row_hits = (rows_wanted[:, None] == jnp.arange(own_rows)[None, :]).astype(jnp.bfloat16)
    fetched = jnp.dot(row_hits, embed_table, preferred_element_type=jnp.float32)
    fetched = fetched.astype(jnp.bfloat16).reshape(owner_count, SLOTS, model_width)
    returned = lax.all_to_all(fetched, AXES, split_axis=0, concat_axis=0, tiled=True)
    memory_rows = memory[0]
    memory_turned = jnp.pad(memory_rows.T, ((0, 0), (0, KEYS - MEM)))
    blocks = all_weights(whole, ffn_out)
    slot = slot_index.reshape(tgt_count, 1)

    embedded, self_proj, self_p, self_mixed, hidden_one, self_w = self_forward(
        returned.reshape(owner_count * SLOTS, model_width), slot, gain_self_all, memory_turned,
        blocks,
    )
    query, key, value, cross_p, cross_mixed, hidden_two, cross_w = cross_forward(
        mem_len, hidden_one, gain_cross_all, memory_rows, blocks
    )
    result, grad_two, gain_ffn_grad, pieces = ffn_both(
        tgt_len, hidden_two, gain_ffn_all, out_grad[0], blocks
    )
    ffn_sum = pieces.reshape(8, 4, 4, BLOCK, 768)
    for ring in (("x", "c"), RING_Y, RING_Z):
        ffn_sum = lax.psum_scatter(ffn_sum, ring)
    rings = ("z", "x", "y")
    grad_query, grad_kv, grad_one, gain_cross_grad = cross_backward(
        hidden_one, gain_cross_all, grad_two, cross_w, query, key, value, cross_p
    )
    mine, other = cross_grads(
        rings, pos, hidden_one, gain_cross_all, grad_two, memory_turned, cross_mixed,
        grad_query, grad_kv,
    )
    cross_sum = ring_sum(mine, other, rings)
    grad_proj, outgoing = self_backward(
        slot, embedded, gain_self_all, grad_one, self_w, self_proj, self_p,
        gain_cross_grad, gain_ffn_grad,
    )
    mine, other = self_grads(
        pos, embedded, gain_self_all, grad_one, self_mixed, grad_proj
    )
    self_sum = lax.all_to_all(add_low(mine, swap_cores(other)), CHIPS, 0, 0, tiled=True)
    self_sum = jnp.sum(self_sum.astype(jnp.float32), axis=0)
    memory_grad = jnp.einsum(
        "me,de->md", grad_kv[:MEM], cross_w[:, 768:2304], preferred_element_type=jnp.float32
    )[None]

    outgoing = outgoing.reshape(owner_count, SLOTS, model_width + 128)
    incoming = lax.all_to_all(outgoing, AXES, split_axis=0, concat_axis=0, tiled=True)
    incoming = incoming.reshape(owner_count * SLOTS, model_width + 128)
    gain_sums = jnp.sum(incoming[:, model_width : model_width + GAINS].astype(jnp.float32), axis=0)
    table_grad = jnp.einsum(
        "sr,sd->rd", row_hits, incoming[:, :model_width], preferred_element_type=jnp.float32
    )

    sums = jnp.concatenate([self_sum, cross_sum, ffn_sum[:, :512].astype(jnp.float32)], axis=1)
    sums = lax.all_to_all(sums.reshape(8, 6, -1), EIGHT, 0, 0, tiled=True)

    def rows_of(v):
        return jnp.swapaxes(v, 0, 1).reshape(6, -1)

    done = []
    for at in (0, 384):
        whole = rows_of(sums[:, :, at : at + 384])
        done.append(jnp.swapaxes(whole[:, :2304].reshape(6, 3, model_width), 0, 1))
        done.append(whole[:, 2304:])
    ffn_in_sum = jnp.swapaxes(rows_of(sums[:, :, 768:]).reshape(6, 2, 2048), 0, 1)
    ffn_out_sum = ffn_sum[:, 512:].astype(jnp.float32).reshape(3, 16, 256).swapaxes(0, 1).reshape(16, model_width)
    return (
        result[None],
        memory_grad,
        table_grad,
        done[0],
        done[1],
        gain_sums[:6],
        done[2],
        done[3],
        gain_sums[6:12],
        ffn_in_sum,
        ffn_out_sum,
        gain_sums[12:18],
    )


def solution(mesh):
    fine = Mesh(mesh.devices.reshape(SIZES), AXES)
    in_specs = (
        P(AXES, None),
        P(AXES),
        P(AXES),
        P(AXES, None),
        P(AXES, None, None),
        P(None, AXES, None),
        P(AXES, None),
        P(AXES),
        P(None, AXES, None),
        P(AXES, None),
        P(AXES),
        P(None, AXES, None),
        P(AXES, None),
        P(AXES),
        P(AXES, None, None),
    )
    out_specs = (
        P(AXES, None, None),
        P(AXES, None, None),
        P(AXES, None),
        P(None, AXES, None),
        P(AXES, None),
        P(AXES),
        P(None, AXES, None),
        P(AXES, None),
        P(AXES),
        P(None, AXES, None),
        P(AXES, None),
        P(AXES),
    )
    return jax.shard_map(body, mesh=fine, in_specs=in_specs, out_specs=out_specs, check_vma=False)
```

```python
import functools

import jax
import jax.numpy as jnp
from jax import lax
from jax.experimental import pallas as pl
from jax.experimental.pallas import tpu as pltpu
from jax.sharding import Mesh, PartitionSpec as P

HEAD_SIZE = 64
D = 768
FF = 2048
TGT = 256
MEM = 1056
KEYS = 1152
PAIRS = 6
SELF_FORWARD, CROSS_FORWARD, CROSS_BACKWARD, SELF_BACKWARD = 6, 6, 2, 3


eps = 1e-06
masked_score = -1e30

AXES = ("x", "yh", "zh", "zl", "yl", "c")
SIZES = (4, 2, 2, 2, 2, 2)
RING_X, RING_Y, RING_Z = ("x",), ("yh", "yl"), ("zh", "zl")
RINGS = {"x": RING_X, "y": RING_Y, "z": RING_Z}
TORUS = RING_X + RING_Y + RING_Z + ("c",)
CHIPS = ("x", "yh", "zh", "zl", "yl")
EIGHT = ("zl", "yl", "c")
BLOCK = 48
SLOTS = 4
GAINS = 18

HBM = pl.BlockSpec(memory_space=pl.ANY)
SCALARS = pl.BlockSpec(memory_space=pltpu.SMEM)


def ring_pair(v, ring, first):
    perm = []
    for i in range(4):
        for c in range(2):
            perm.append((2 * i + c, 2 * (i ^ (1 if (c == 0) == first else 3)) + c))
    return lax.ppermute(v, ring + ("c",), perm)


def swap_cores(v):
    return lax.ppermute(v, "c", [(0, 1), (1, 0)])


def then(v, *tokens):
    return lax.optimization_barrier((v, *tokens))[0]


def add_low(*terms):
    return sum(t.astype(jnp.float32) for t in terms).astype(jnp.bfloat16)


def ring_sum_start(mine, got):
    return add_low(mine[:2], got[:2]), add_low(mine[2:], got[2:])


def ring_first(low, high, ring):
    got = ring_pair(high, RINGS[ring], False)
    return low[0], got[0], add_low(low[1], got[1])


def ring_second(terms, ring):
    return terms[0], terms[1], ring_pair(terms[2], RINGS[ring], True)


def ring_halves(terms):
    return tuple(add_low(*(t[at] for t in terms)) for at in (slice(0, 2), slice(2, 4)))


def ring_total(low, high, ring):
    return sum(t.astype(jnp.float32) for t in ring_second(ring_first(low, high, ring), ring))


def mm(a, b):
    return jnp.dot(a, b, preferred_element_type=jnp.float32)


def mm_nt(a, b):
    return lax.dot_general(a, b, (((1,), (1,)), ((), ())), preferred_element_type=jnp.float32)


def mm_tn(a, b):
    return lax.dot_general(a, b, (((0,), (0,)), ((), ())), preferred_element_type=jnp.float32)


def turned(v):
    return v.astype(jnp.float32).T.astype(v.dtype)


def first_half(shape):
    return lax.broadcasted_iota(jnp.int32, shape, 1) < HEAD_SIZE


def stacked_heads(pair):
    low = first_half(pair.shape)
    zero = jnp.zeros_like(pair)
    return jnp.concatenate([jnp.where(low, pair, zero), jnp.where(low, zero, pair)], axis=0)


def joined_heads(both):
    half = both.shape[0] // 2
    return jnp.where(first_half((half, both.shape[1])), both[:half], both[half:])


def rms_scale(hidden):
    return lax.rsqrt(jnp.mean(hidden * hidden, axis=-1, keepdims=True) + eps)


def rms_back(hidden, gain, grad):
    scale = rms_scale(hidden)
    u = grad * gain
    inner = jnp.mean(u * hidden, axis=-1, keepdims=True)
    grad_hidden = scale * u - hidden * (scale * scale * scale * inner)
    return grad_hidden, jnp.sum(grad * hidden * scale, axis=0, keepdims=True)


def my_place(pos_ref):
    return {"x": pos_ref[0], "y": pos_ref[1], "z": pos_ref[2]}


def group_member(at, core):
    group = at["x"] * 4 + (at["y"] >> 1) * 2 + (at["z"] >> 1)
    return group, (at["z"] & 1) * 4 + (at["y"] & 1) * 2 + core


def partners(core):
    return (0, 1 + 2 * core, 3 - 2 * core, 2)


def square_parts(width, group, member):
    row = pl.multiple_of(group * BLOCK, 16)
    column = pl.multiple_of(member * width, 128)
    return [((slice(None), slice(None)), 0, (pl.ds(row, BLOCK), pl.ds(column, width)))]


def torus():
    return [(x, y, z, c) for x in range(4) for y in range(4) for z in range(4) for c in range(2)]


def block_place(x, y, z, c):
    return x * 4 + (y // 2) * 2 + z // 2, (z % 2) * 4 + (y % 2) * 2 + c


def start_place(blocks, first, out, sem):
    for at in torus():
        group, member = block_place(*at)
        pltpu.make_async_copy(
            blocks.at[at + (slice(None), pl.ds(first, 384))],
            out.at[pl.ds(BLOCK * group, BLOCK), pl.ds(384 * member, 384)],
            sem,
        ).start()


def ffn_copies(j, whole_in, whole_out, block_of):
    found = []
    for at in torus():
        group, member = block_place(*at)
        block = block_of(at)
        if member % 4 == j:
            rows, columns = pl.ds(BLOCK * group, BLOCK), pl.ds(512 * member, 512)
            found.append((whole_in.at[rows, columns], block.at[:, pl.ds(768, 512)]))
        if at[0] == j:
            rows = pl.ds(16 * (8 * group + member), 16)
            for s in range(3):
                part = block.at[pl.ds(16 * s, 16), pl.ds(1280, 256)]
                found.append((whole_out.at[rows, pl.ds(256 * s, 256)], part))
    return found


def start_split(pos_ref, rings, parts, wholes, outs, sem):
    me = my_place(pos_ref)
    at = {}
    for source in range(2):
        core = pos_ref[3] ^ source
        flips = partners(core)
        for k3 in range(4):
            at[rings[0]] = me[rings[0]] ^ flips[k3]
            for k2 in range(4):
                at[rings[1]] = me[rings[1]] ^ flips[k2]
                for k1 in range(4):
                    at[rings[2]] = me[rings[2]] ^ flips[k1]
                    for dst, whole, src in parts(*group_member(at, core)):
                        pltpu.make_async_copy(
                            wholes[whole].at[src], outs[source].at[(k3, k2, k1) + dst], sem
                        ).start()


def wait_whole(refs, sem):
    for ref in refs:
        pltpu.make_async_copy(ref, ref, sem).wait()


def start_split(pos_ref, rings, parts, wholes, outs, sem):
    me = my_place(pos_ref)
    at = {}
    for source in range(2):
        core = pos_ref[3] ^ source
        flips = partners(core)
        for k3 in range(4):
            at[rings[0]] = me[rings[0]] ^ flips[k3]
            for k2 in range(4):
                at[rings[1]] = me[rings[1]] ^ flips[k2]
                for k1 in range(4):
                    at[rings[2]] = me[rings[2]] ^ flips[k1]
                    for dst, whole, src in parts(*group_member(at, core)):
                        pltpu.make_async_copy(
                            wholes[whole].at[src], outs[source].at[(k3, k2, k1) + dst], sem
                        ).start()


def start_split_whole(pos_ref, whole, outs, sem):
    for source in range(2):
        core = pos_ref[3] ^ source
        for group in range(16):
            for q in range(4):
                for dst, _, src in square_parts(384, group, 2 * q + core):
                    pltpu.make_async_copy(
                        whole.at[src], outs[source].at[(4 * group + q,) + dst], sem
                    ).start()


def softmax_low(scores, valid):
    scores = jnp.where(valid, scores, masked_score)
    expanded = jnp.exp(scores - jnp.max(scores, axis=-1, keepdims=True))
    total = jnp.sum(expanded, axis=-1, keepdims=True)
    return (expanded * (1.0 / total)).astype(jnp.bfloat16)


def softmax_back(weights, grads):
    weights = weights.astype(jnp.float32)
    inner = jnp.sum(weights * grads, axis=-1, keepdims=True)
    return (weights * (grads - inner)).astype(jnp.bfloat16)


def pair_columns(j, offset=0):
    return pl.ds(pl.multiple_of(offset + j * 128, 128), 128)


def pairs_here(together):
    j = pl.program_id(0)
    return [(s, j * together + s) for s in range(together)]


def self_forward_kernel(rows_ref, slot_ref, gain_ref, early_ref, blocks, *refs):
    kept_ref, qkv_ref, p_ref, h1_ref, w_ref, sem = refs
    emb_ref, mixed_ref = kept_ref.at[:, :D], kept_ref.at[:, D:]
    j = pl.program_id(0)

    @pl.when(j == 0)
    def _():
        start_place(blocks, 0, w_ref, sem)
        slots = rows_ref.shape[0]
        hits = slot_ref[...] == lax.broadcasted_iota(jnp.int32, (TGT, slots), 1)
        hidden = mm(hits.astype(jnp.bfloat16), rows_ref[...])
        emb_ref[...] = hidden.astype(jnp.bfloat16)
        normed = (hidden * rms_scale(hidden) * gain_ref[...]).astype(jnp.bfloat16)
        wait_whole([w_ref], sem)
        for k in range(3):
            at = pl.ds(768 * k, 768)
            qkv_ref[:, at] = mm(normed, w_ref[:, at]).astype(jnp.bfloat16)

    row = lax.broadcasted_iota(jnp.int32, (2 * TGT, TGT), 0) & (TGT - 1)
    causal = lax.broadcasted_iota(jnp.int32, (2 * TGT, TGT), 1) <= row
    for s, pair in pairs_here(SELF_FORWARD):
        queries = stacked_heads(qkv_ref[:, pair_columns(pair)]) * jnp.bfloat16(0.125)
        weights = softmax_low(mm_nt(queries, qkv_ref[:, pair_columns(pair, 768)]), causal)
        p_ref[s] = weights
        mixed = mm(weights, qkv_ref[:, pair_columns(pair, 1536)])
        mixed_ref[:, pair_columns(pair)] = joined_heads(mixed).astype(jnp.bfloat16)

    @pl.when(j == PAIRS // SELF_FORWARD - 1)
    def _():
        h1_ref[...] = emb_ref[...].astype(jnp.float32) + mm(mixed_ref[...], w_ref[:, 2304:])


def full(*shape):
    return pl.BlockSpec(shape, lambda j: (0,) * len(shape))


def shaped(dtype, *shape):
    return jax.ShapeDtypeStruct(shape, dtype)


def params(mib=56):
    return pltpu.CompilerParams(vmem_limit_bytes=mib * 2**20)


def cost(gflop, mbytes):
    return pl.CostEstimate(
        flops=int(gflop * 1e9), bytes_accessed=int(mbytes * 1e6), transcendentals=0
    )


def self_forward(rows, slot, gain, early, blocks):
    bf, f32 = jnp.bfloat16, jnp.float32
    return pl.pallas_call(
        self_forward_kernel,
        grid=(PAIRS // SELF_FORWARD,),
        in_specs=[full(512, D), full(TGT, 1), full(1, D), HBM, HBM],
        out_specs=[
            full(TGT, 2 * D),
            full(TGT, 3 * D),
            pl.BlockSpec((SELF_FORWARD, 512, TGT), lambda j: (j, 0, 0)),
            full(TGT, D),
            full(D, 4 * D),
        ],
        out_shape=[
            shaped(bf, TGT, 2 * D),
            shaped(bf, TGT, 3 * D),
            shaped(bf, PAIRS, 512, TGT),
            shaped(f32, TGT, D),
            shaped(bf, D, 4 * D),
        ],
        scratch_shapes=[pltpu.SemaphoreType.DMA],
        compiler_params=params(),
        cost_estimate=cost(8, 12),
        name="self_forward",
    )(rows, slot, gain, early, blocks)


def cross_forward_kernel(len_ref, h1_ref, gain_ref, mem_ref, blocks, *refs):
    q_ref, k_ref, v_ref, p_ref, mixed_ref, h2_ref, w_ref, sem = refs
    j = pl.program_id(0)

    @pl.when(j == 0)
    def _():
        start_place(blocks, 384, w_ref, sem)
        hidden = h1_ref[...]
        normed = (hidden * rms_scale(hidden) * gain_ref[...]).astype(jnp.bfloat16)
        wait_whole([w_ref], sem)
        q_ref[...] = mm(normed, w_ref[:, :768]).astype(jnp.bfloat16)
        for out, offset in ((k_ref, 768), (v_ref, 1536)):
            for half in range(2):
                at = pl.ds(384 * half, 384)
                out[:MEM, at] = mm(mem_ref[...], w_ref[:, pl.ds(offset + 384 * half, 384)]).astype(
                    jnp.bfloat16
                )
            out[MEM:, :] = jnp.zeros((KEYS - MEM, D), jnp.bfloat16)

    reach = lax.broadcasted_iota(jnp.int32, (2 * TGT, KEYS), 1) < len_ref[0]
    for s, pair in pairs_here(CROSS_FORWARD):
        queries = stacked_heads(q_ref[:, pair_columns(pair)]) * jnp.bfloat16(0.125)
        weights = softmax_low(mm_nt(queries, k_ref[:, pair_columns(pair)]), reach)
        p_ref[s] = weights
        mixed = mm(weights, v_ref[:, pair_columns(pair)])
        mixed_ref[:, pair_columns(pair)] = joined_heads(mixed).astype(jnp.bfloat16)

    @pl.when(j == PAIRS // CROSS_FORWARD - 1)
    def _():
        h2_ref[...] = h1_ref[...] + mm(mixed_ref[...], w_ref[:, 2304:])


def cross_forward(mem_len, h1, gain, memory, blocks):
    bf, f32 = jnp.bfloat16, jnp.float32
    return pl.pallas_call(
        cross_forward_kernel,
        grid=(PAIRS // CROSS_FORWARD,),
        in_specs=[SCALARS, full(TGT, D), full(1, D), full(MEM, D), HBM],
        out_specs=[
            full(TGT, D),
            full(KEYS, D),
            full(KEYS, D),
            pl.BlockSpec((CROSS_FORWARD, 512, KEYS), lambda j: (j, 0, 0)),
            full(TGT, D),
            full(TGT, D),
            full(D, 4 * D),
        ],
        out_shape=[
            shaped(bf, TGT, D),
            shaped(bf, KEYS, D),
            shaped(bf, KEYS, D),
            shaped(bf, PAIRS, 512, KEYS),
            shaped(bf, TGT, D),
            shaped(f32, TGT, D),
            shaped(bf, D, 4 * D),
        ],
        scratch_shapes=[pltpu.SemaphoreType.DMA],
        compiler_params=params(),
        cost_estimate=cost(20, 20),
        name="cross_forward",
    )(mem_len, h1, gain, memory, blocks)


class piece_of:
    def __init__(self, ref):
        self.ref = ref

    @property
    def at(self):
        return self

    def __getitem__(self, place):
        rows, columns = place
        return self.ref.at[rows, pl.ds(columns.start - 768, columns.size)]


def ffn_kernel(len_ref, h2_ref, gain_ref, og_ref, blocks, *refs):
    out_ref, g2_ref, dgain_ref, pieces = refs[:4]
    w_in, w_out, g_in, g_out, normed, normed_t, low, gate, up, grad, inner, da, sems, sem = refs[4:]
    j = pl.program_id(0)
    bf, f32 = jnp.bfloat16, jnp.float32

    def kept():
        row = lax.broadcasted_iota(jnp.int32, (TGT, 1), 0)
        return row < len_ref[0]

    @pl.when(j == 0)
    def _():
        for quarter in range(FF // 512):
            for whole, block in ffn_copies(quarter, w_in, w_out, lambda at: blocks.at[at]):
                pltpu.make_async_copy(block, whole, sems.at[quarter]).start()
        hidden = h2_ref[...]
        a3 = (hidden * rms_scale(hidden) * gain_ref[...]).astype(bf)
        normed[...] = a3
        normed_t[...] = a3.astype(f32).T.astype(bf)
        low[...] = jnp.where(kept(), og_ref[...], jnp.zeros((), bf))

    width = 512
    gate_at = pl.ds(pl.multiple_of(j * width, width), width)
    up_at = pl.ds(pl.multiple_of(FF + j * width, width), width)
    wait_whole([w_in.at[:, gate_at], w_in.at[:, up_at], w_out.at[gate_at, :]], sems.at[j])
    gate[...] = mm(normed[...], w_in[:, gate_at])
    up[...] = mm(normed[...], w_in[:, up_at])
    grad[...] = mm_nt(low[...], w_out[gate_at, :])

    def unit(i, carry):
        at = pl.ds(pl.multiple_of(i * 32, 32), 32)
        g, u, d = gate[at, :], up[at, :], grad[at, :]
        square = g * g
        t = jnp.tanh(0.7978845608 * (g + 0.044715 * (g * square)))
        half = 0.5 * (1.0 + t)
        gelu = g * half
        slope = half + 0.5 * g * (1.0 - t * t) * (0.7978845608 * (1.0 + 3.0 * 0.044715 * square))
        inner[at, :] = (gelu * u).astype(bf)
        gate[at, :] = d * u * slope
        up[at, :] = d * gelu
        return carry

    lax.fori_loop(0, TGT // 32, unit, 0, unroll=True)
    c_gate, c_up = gate[...].astype(bf), up[...].astype(bf)
    part = mm(inner[...], w_out[gate_at, :])
    da_part = mm_nt(c_gate, w_in[:, gate_at]) + mm_nt(c_up, w_in[:, up_at])

    @pl.when(j == 0)
    def _():
        out_ref[...] = part
        da[...] = da_part

    @pl.when(j > 0)
    def _():
        out_ref[...] += part
        da[...] += da_part

    g_out[gate_at, :] = mm_tn(inner[...], low[...]).astype(bf)
    g_in[:, gate_at] = mm(normed_t[...], c_gate).astype(bf)
    g_in[:, up_at] = mm(normed_t[...], c_up).astype(bf)

    for quarter in range(FF // width):

        @pl.when(j == quarter)
        def _():
            for whole, block in ffn_copies(
                quarter, g_in, g_out, lambda at: piece_of(pieces.at[at[0], at[3], at[1], at[2]])
            ):
                pltpu.make_async_copy(whole, block, sem).start()

    @pl.when(j == FF // width - 1)
    def _():
        hidden = h2_ref[...]
        out_ref[...] = jnp.where(kept(), hidden + out_ref[...], 0.0)
        back, dgain = rms_back(hidden, gain_ref[...], da[...])
        g2_ref[...] = jnp.where(kept(), og_ref[...].astype(f32), 0.0) + back
        dgain_ref[...] = dgain
        wait_whole([g_in, g_out], sem)


def ffn_both(tgt_len, h2, gain, out_grad, blocks):
    bf, f32 = jnp.bfloat16, jnp.float32
    pieces = shaped(bf, 4, 2, 4, 4, BLOCK, 768)
    return pl.pallas_call(
        ffn_kernel,
        grid=(FF // 512,),
        in_specs=[SCALARS, full(TGT, D), full(1, D), full(TGT, D), HBM],
        out_specs=[full(TGT, D), full(TGT, D), full(1, D), HBM],
        out_shape=[shaped(f32, TGT, D), shaped(f32, TGT, D), shaped(f32, 1, D), pieces],
        scratch_shapes=[
            pltpu.VMEM((D, 2 * FF), bf),
            pltpu.VMEM((FF, D), bf),
            pltpu.VMEM((D, 2 * FF), bf),
            pltpu.VMEM((FF, D), bf),
            pltpu.VMEM((TGT, D), bf),
            pltpu.VMEM((D, TGT), bf),
            pltpu.VMEM((TGT, D), bf),
            pltpu.VMEM((TGT, 512), f32),
            pltpu.VMEM((TGT, 512), f32),
            pltpu.VMEM((TGT, 512), f32),
            pltpu.VMEM((TGT, 512), bf),
            pltpu.VMEM((TGT, D), f32),
            pltpu.SemaphoreType.DMA((FF // 512,)),
            pltpu.SemaphoreType.DMA,
        ],
        compiler_params=params(),
        cost_estimate=cost(15, 25),
        name="ffn_both",
    )(tgt_len, h2, gain, out_grad, blocks)


def cross_backward_kernel(h1_ref, gain_ref, g2_ref, w_ref, q_ref, k_ref, v_ref, p_ref, *refs):
    dq, dkv_ref, g1_ref, dgain_ref, grad_mixed = refs
    j = pl.program_id(0)
    bf = jnp.bfloat16

    @pl.when(j == 0)
    def _():
        grad_mixed[...] = mm_nt(g2_ref[...].astype(bf), w_ref[:, 2304:]).astype(bf)

    for s, pair in pairs_here(CROSS_BACKWARD):
        at = pair_columns(pair)
        d_pair = stacked_heads(grad_mixed[:, at])
        queries = stacked_heads(q_ref[:, at])
        weights = p_ref[s]
        grads = softmax_back(weights, mm_nt(d_pair, v_ref[:, at]))
        dq[:, at] = (joined_heads(mm(grads, k_ref[:, at])) * 0.125).astype(bf)
        dkv_ref[:, at] = (mm(turned(queries), grads) * 0.125).T.astype(bf)
        dkv_ref[:, pair_columns(pair, 768)] = mm(turned(d_pair), weights).T.astype(bf)

    @pl.when(j == PAIRS // CROSS_BACKWARD - 1)
    def _():
        back, dgain = rms_back(h1_ref[...], gain_ref[...], mm_nt(dq[...], w_ref[:, :768]))
        g1_ref[...] = g2_ref[...] + back
        dgain_ref[...] = dgain


def cross_backward(h1, gain, g2, w, q, k, v, p):
    bf, f32 = jnp.bfloat16, jnp.float32
    return pl.pallas_call(
        cross_backward_kernel,
        grid=(PAIRS // CROSS_BACKWARD,),
        in_specs=[
            full(TGT, D),
            full(1, D),
            full(TGT, D),
            full(D, 4 * D),
            full(TGT, D),
            full(KEYS, D),
            full(KEYS, D),
            pl.BlockSpec((CROSS_BACKWARD, 512, KEYS), lambda j: (j, 0, 0)),
        ],
        out_specs=[full(TGT, D), full(KEYS, 2 * D), full(TGT, D), full(1, D)],
        out_shape=[
            shaped(bf, TGT, D),
            shaped(bf, KEYS, 2 * D),
            shaped(f32, TGT, D),
            shaped(f32, 1, D),
        ],
        scratch_shapes=[pltpu.VMEM((TGT, D), bf)],
        compiler_params=params(),
        cost_estimate=cost(16, 20),
        name="cross_backward",
    )(h1, gain, g2, w, q, k, v, p)


def cross_grads_kernel(
    rings, pos_ref, h1_ref, gain_ref, g2_ref, mem_t_ref, mixed_ref, dq_ref, dkv_ref, *refs
):
    mine_ref, other_ref, whole, sem = refs
    bf = jnp.bfloat16
    hidden = h1_ref[...]
    normed = (hidden * rms_scale(hidden) * gain_ref[...]).astype(bf)
    whole[:, :768] = mm_tn(normed, dq_ref[...]).astype(bf)
    whole[:, 2304:] = mm_tn(mixed_ref[...], g2_ref[...].astype(bf)).astype(bf)
    for k in range(4):
        at = pl.ds(768 + 384 * k, 384)
        whole[:, at] = mm(mem_t_ref[...], dkv_ref[:, pl.ds(384 * k, 384)]).astype(bf)
    parts = functools.partial(square_parts, 384)
    start_split(pos_ref, rings, parts, [whole], [mine_ref, other_ref], sem)
    wait_whole([whole], sem)


def cross_grads(rings, pos, h1, gain, g2, mem_t, mixed, dq, dkv):
    bf = jnp.bfloat16
    pieces = shaped(bf, 4, 4, 4, BLOCK, 384)
    return pl.pallas_call(
        functools.partial(cross_grads_kernel, rings),
        in_specs=[SCALARS] + [pl.BlockSpec(memory_space=pltpu.VMEM)] * 7,
        out_specs=[HBM, HBM],
        out_shape=[pieces, pieces],
        scratch_shapes=[pltpu.VMEM((D, 4 * D), bf), pltpu.SemaphoreType.DMA],
        compiler_params=params(),
        cost_estimate=cost(6, 12),
        name="cross_grads",
    )(pos, h1, gain, g2, mem_t, mixed, dq, dkv)


def self_backward_kernel(
    pos_ref, slot_ref, kept_ref, gain_ref, g1_ref, w_ref, qkv_ref, p_ref, *refs
):
    dg2_ref, dg3_ref, mine_ref, other_ref, out_ref, grad_mixed, dqkv = refs
    j = pl.program_id(0)
    bf, f32 = jnp.bfloat16, jnp.float32

    @pl.when(j == 0)
    def _():
        grad_mixed[...] = mm_nt(g1_ref[...].astype(bf), w_ref[:, 2304:]).astype(bf)

    for s, pair in pairs_here(SELF_BACKWARD):
        at = pair_columns(pair)
        d_pair = stacked_heads(grad_mixed[:, at])
        queries = stacked_heads(qkv_ref[:, at])
        weights = p_ref[s]
        grads = softmax_back(weights, mm_nt(d_pair, qkv_ref[:, pair_columns(pair, 1536)]))
        dqkv[:, at] = (joined_heads(mm(grads, qkv_ref[:, pair_columns(pair, 768)])) * 0.125).astype(bf)
        dqkv[:, pair_columns(pair, 768)] = (mm_tn(grads, queries) * 0.125).astype(bf)
        dqkv[:, pair_columns(pair, 1536)] = mm_tn(weights, d_pair).astype(bf)

    @pl.when(j == PAIRS // SELF_BACKWARD - 1)
    def _():
        for source, half_ref in enumerate((mine_ref, other_ref)):
            first = pl.multiple_of((pos_ref[3] ^ source) * 384, 128)
            for k in range(3):
                half_ref[:, 384 * k : 384 * k + 384] = dqkv[:, pl.ds(768 * k + first, 384)]
            half_ref[:, 1152:] = g1_ref[:, pl.ds(first, 384)].astype(bf)
        hidden = kept_ref[:, :D].astype(f32)
        back, dgain = rms_back(hidden, gain_ref[...], mm_nt(dqkv[...], w_ref[:, :2304]))
        slots = out_ref.shape[0]
        hits = slot_ref[...] == lax.broadcasted_iota(jnp.int32, (TGT, slots), 1)
        out_ref[:, :D] = mm_tn(hits.astype(bf), (g1_ref[...] + back).astype(bf)).astype(bf)
        row = lax.broadcasted_iota(jnp.int32, (slots, D), 0)
        feature = lax.broadcasted_iota(jnp.int32, (slots, D), 1)
        first = (row // SLOTS) * 6
        owned = (row % SLOTS == 0) & (feature >= first) & (feature < first + 6)
        lane = lax.broadcasted_iota(jnp.int32, (D, 128), 1)
        place = lax.broadcasted_iota(jnp.int32, (D, 128), 0) % 6
        extra = jnp.zeros((slots, 128), f32)
        for k, grad in enumerate((dgain, dg2_ref[...], dg3_ref[...])):
            spread = jnp.where(owned, grad, 0.0).astype(bf)
            extra += mm(spread, (lane == place + 6 * k).astype(bf))
        out_ref[:, D:] = extra.astype(bf)


def self_backward(pos, slot, kept, gain, g1, w, qkv, p, dg2, dg3):
    bf = jnp.bfloat16
    return pl.pallas_call(
        self_backward_kernel,
        grid=(PAIRS // SELF_BACKWARD,),
        in_specs=[
            SCALARS,
            full(TGT, 1),
            full(TGT, 2 * D),
            full(1, D),
            full(TGT, D),
            full(D, 4 * D),
            full(TGT, 3 * D),
            pl.BlockSpec((SELF_BACKWARD, 512, TGT), lambda j: (j, 0, 0)),
            full(1, D),
            full(1, D),
        ],
        out_specs=[full(TGT, 2 * D), full(TGT, 2 * D), full(512, D + 128)],
        out_shape=[shaped(bf, TGT, 2 * D), shaped(bf, TGT, 2 * D), shaped(bf, 512, D + 128)],
        scratch_shapes=[pltpu.VMEM((TGT, D), bf), pltpu.VMEM((TGT, 3 * D), bf)],
        compiler_params=params(),
        cost_estimate=cost(8, 10),
        name="self_backward",
    )(pos, slot, kept, gain, g1, w, qkv, p, dg2, dg3)


def self_grads_kernel(rings, pos_ref, gain_ref, kept_ref, kept_other_ref, half_ref, half_other_ref, *refs):
    *outs, whole, sem = refs
    bf, f32 = jnp.bfloat16, jnp.float32

    def normed(kept):
        hidden = kept[:, :D].astype(f32)
        return turned((hidden * rms_scale(hidden) * gain_ref[...]).astype(bf))

    whole[:, :1152] = (
        mm(normed(kept_ref), half_ref[:, :1152])
        + mm(normed(kept_other_ref), half_other_ref[:, :1152])
    ).astype(bf)
    whole[:, 1152:] = (
        mm_tn(kept_ref[:, D:], half_ref[:, 1152:])
        + mm_tn(kept_other_ref[:, D:], half_other_ref[:, 1152:])
    ).astype(bf)
    me, at = my_place(pos_ref), {}
    flips = partners(pos_ref[3])
    for k3 in range(4):
        at[rings[0]] = me[rings[0]] ^ flips[k3]
        for k2 in range(4):
            at[rings[1]] = me[rings[1]] ^ flips[k2]
            for k1 in range(4):
                at[rings[2]] = me[rings[2]] ^ flips[k1]
                group, member = group_member(at, 0)
                row = pl.multiple_of(group * BLOCK, 16)
                column = pl.multiple_of((member >> 1) * 384, 128)
                pltpu.make_async_copy(
                    whole.at[pl.ds(row, BLOCK), pl.ds(column, 384)],
                    outs[k3 // 2].at[k3 % 2, k2, k1],
                    sem,
                ).start()
    wait_whole([whole], sem)


def self_grads(rings, pos, gain, kept, kept_other, half, half_other):
    bf = jnp.bfloat16
    return pl.pallas_call(
        functools.partial(self_grads_kernel, rings),
        in_specs=[SCALARS] + [pl.BlockSpec(memory_space=pltpu.VMEM)] * 5,
        out_specs=[HBM, HBM],
        out_shape=[shaped(bf, 2, 4, 4, BLOCK, 384)] * 2,
        scratch_shapes=[pltpu.VMEM((D, 2 * D), bf), pltpu.SemaphoreType.DMA],
        compiler_params=params(),
        cost_estimate=cost(3, 8),
        name="self_grads",
    )(pos, gain, kept, kept_other, half, half_other)


def after(v, token):
    return v + (token * 0).astype(v.dtype)


def column_blocks(self_qkv, self_out, cross_qkv, cross_out, ffn_in):
    def chunks(v):
        return v.reshape(6, 8, -1).swapaxes(0, 1)

    flat = [
        jnp.concatenate([jnp.swapaxes(qkv, 0, 1).reshape(6, -1), out], axis=1)
        for qkv, out in ((self_qkv, self_out), (cross_qkv, cross_out))
    ]
    flat.append(jnp.swapaxes(ffn_in, 0, 1).reshape(6, -1))
    whole = jnp.concatenate([chunks(v) for v in flat], axis=2)
    return lax.all_to_all(whole, EIGHT, 0, 0, tiled=True).reshape(BLOCK, -1)


def all_weights(whole, ffn_out):
    tail = ffn_out.reshape(16, 3, 256).swapaxes(0, 1).reshape(BLOCK, 256)
    piece = jnp.concatenate([whole, tail], axis=1)
    return lax.all_gather(piece, TORUS).reshape(4, 4, 4, 2, BLOCK, -1)


def body(
    target_ids,
    tgt_len,
    mem_len,
    embed_table,
    memory,
    self_qkv,
    self_out,
    gain_self,
    cross_qkv,
    cross_out,
    gain_cross,
    ffn_in,
    ffn_out,
    gain_ffn,
    out_grad,
):
    tgt_count = target_ids.shape[1]
    model_width = memory.shape[2]
    own_rows = embed_table.shape[0]
    owner_count = 128
    place_in = [lax.axis_index(ring) for ring in (RING_X, RING_Y, RING_Z, ("c",))]
    pos = jnp.stack(place_in).astype(jnp.int32)

    flat_ids = target_ids.reshape(tgt_count)
    owner_of = flat_ids // own_rows
    local_row = flat_ids - owner_of * own_rows
    owner_hits = (owner_of[:, None] == jnp.arange(owner_count)[None, :]).astype(jnp.int32)
    row_rank = jnp.sum(jnp.cumsum(owner_hits, axis=0) * owner_hits, axis=1) - 1
    slot_index = owner_of * SLOTS + row_rank
    slot_hits = slot_index[:, None] == jnp.arange(owner_count * SLOTS)[None, :]
    wanted = jnp.sum(jnp.where(slot_hits, local_row[:, None] + 1, 0), axis=0)
    gains = jnp.concatenate([gain_self, gain_cross, gain_ffn]).astype(jnp.float32)
    request = jnp.concatenate(
        [
            wanted.astype(jnp.float32).reshape(owner_count, SLOTS),
            jnp.broadcast_to(gains[None], (owner_count, GAINS)),
            jnp.zeros((owner_count, 32 - SLOTS - GAINS), jnp.float32),
        ],
        axis=1,
    )
    whole = column_blocks(self_qkv, self_out, cross_qkv, cross_out, ffn_in)
    arrived = lax.all_to_all(then(request, whole), AXES, split_axis=0, concat_axis=0, tiled=True)
    gain_self_all, gain_cross_all, gain_ffn_all = (
        arrived[:, SLOTS + 6 * k : SLOTS + 6 * k + 6].reshape(1, model_width) for k in range(3)
    )
    rows_wanted = arrived[:, :SLOTS].reshape(owner_count * SLOTS).astype(jnp.int32) - 1
    row_hits = (rows_wanted[:, None] == jnp.arange(own_rows)[None, :]).astype(jnp.bfloat16)
    fetched = jnp.dot(row_hits, embed_table, preferred_element_type=jnp.float32)
    fetched = fetched.astype(jnp.bfloat16).reshape(owner_count, SLOTS, model_width)
    returned = lax.all_to_all(fetched, AXES, split_axis=0, concat_axis=0, tiled=True)
    memory_rows = memory[0]
    memory_turned = jnp.pad(memory_rows.T, ((0, 0), (0, KEYS - MEM)))
    blocks = all_weights(whole, ffn_out)
    slot = slot_index.reshape(tgt_count, 1)

    kept, self_proj, self_p, hidden_one, self_w = self_forward(
        returned.reshape(owner_count * SLOTS, model_width), slot, gain_self_all, memory_turned,
        blocks,
    )
    query, key, value, cross_p, cross_mixed, hidden_two, cross_w = cross_forward(
        mem_len, hidden_one, gain_cross_all, memory_rows, blocks
    )
    result, grad_two, gain_ffn_grad, pieces = ffn_both(
        tgt_len, hidden_two, gain_ffn_all, out_grad[0], blocks
    )
    kept_other = swap_cores(kept)
    ffn_x = lax.psum_scatter(pieces.reshape(8, 4, 4, BLOCK, 768), ("x", "c"))
    ffn_y = lax.psum_scatter(ffn_x, RING_Y)
    ffn_sum = lax.psum_scatter(ffn_y, RING_Z)
    grad_query, grad_kv, grad_one, gain_cross_grad = cross_backward(
        hidden_one, gain_cross_all, grad_two, cross_w, query, key, value, cross_p
    )
    rings = ("z", "y", "x")
    mine, other = cross_grads(
        rings, pos, hidden_one, gain_cross_all, grad_two, memory_turned, cross_mixed,
        grad_query, grad_kv,
    )
    other = swap_cores(other)
    half, half_other, outgoing = self_backward(
        pos, slot, kept, gain_self_all, then(grad_one, mine), self_w, self_proj, self_p,
        gain_cross_grad, gain_ffn_grad,
    )
    cross_start = ring_sum_start(then(mine, half), other)
    outgoing = then(outgoing, cross_start).reshape(owner_count, SLOTS, model_width + 128)
    incoming = lax.all_to_all(outgoing, AXES, split_axis=0, concat_axis=0, tiled=True)
    self_rings = ("x", "z", "y")
    self_low, self_high = self_grads(
        self_rings, pos, then(gain_self_all, outgoing), kept, kept_other, half,
        swap_cores(half_other),
    )
    cross_low, cross_high = cross_start
    cross_terms = ring_first(then(cross_low, self_low), cross_high, rings[0])
    memory_grad = jnp.einsum(
        "me,de->md", then(grad_kv, cross_terms[2], ffn_x)[:MEM], cross_w[:, 768:2304],
        preferred_element_type=jnp.float32,
    )[None]
    self_terms = ring_first(then(self_low, memory_grad, incoming), self_high, self_rings[0])
    cross_terms = ring_second(cross_terms, rings[0])
    cross_low, cross_high = ring_halves((then(cross_terms[0], self_terms[2]), *cross_terms[1:]))
    self_terms = ring_second(self_terms, self_rings[0])
    self_low, self_high = ring_halves((then(self_terms[0], cross_low), *self_terms[1:]))
    cross_terms = ring_first(then(cross_low, self_low), cross_high, rings[1])
    incoming = then(incoming, cross_terms[2]).reshape(
        owner_count * SLOTS, model_width + 128
    )
    gain_sums = jnp.sum(incoming[:, model_width : model_width + GAINS].astype(jnp.float32), axis=0)
    table_grad = jnp.einsum(
        "sr,sd->rd", row_hits, incoming[:, :model_width], preferred_element_type=jnp.float32
    )
    cross_terms = ring_second(cross_terms, rings[1])
    cross_low, cross_high = ring_halves((then(cross_terms[0], ffn_y), *cross_terms[1:]))
    self_terms = ring_first(self_low, self_high, self_rings[1])
    self_low, self_high = ring_halves(ring_second(self_terms, self_rings[1]))
    cross_sum = ring_total(cross_low, cross_high, rings[2])
    self_sum = ring_total(then(self_low, ffn_sum), self_high, self_rings[2])

    sums = jnp.concatenate([self_sum, cross_sum, ffn_sum[:, :512].astype(jnp.float32)], axis=1)
    sums = lax.all_to_all(sums.reshape(8, 6, -1), EIGHT, 0, 0, tiled=True)

    def rows_of(v):
        return jnp.swapaxes(v, 0, 1).reshape(6, -1)

    done = []
    for at in (0, 384):
        whole = rows_of(sums[:, :, at : at + 384])
        done.append(jnp.swapaxes(whole[:, :2304].reshape(6, 3, model_width), 0, 1))
        done.append(whole[:, 2304:])
    ffn_in_sum = jnp.swapaxes(rows_of(sums[:, :, 768:]).reshape(6, 2, 2048), 0, 1)
    ffn_out_sum = ffn_sum[:, 512:].astype(jnp.float32).reshape(3, 16, 256).swapaxes(0, 1).reshape(16, model_width)
    return (
        result[None],
        memory_grad,
        table_grad,
        done[0],
        done[1],
        gain_sums[:6],
        done[2],
        done[3],
        gain_sums[6:12],
        ffn_in_sum,
        ffn_out_sum,
        gain_sums[12:18],
    )


def solution(mesh):
    fine = Mesh(mesh.devices.reshape(SIZES), AXES)
    in_specs = (
        P(AXES, None),
        P(AXES),
        P(AXES),
        P(AXES, None),
        P(AXES, None, None),
        P(None, AXES, None),
        P(AXES, None),
        P(AXES),
        P(None, AXES, None),
        P(AXES, None),
        P(AXES),
        P(None, AXES, None),
        P(AXES, None),
        P(AXES),
        P(AXES, None, None),
    )
    out_specs = (
        P(AXES, None, None),
        P(AXES, None, None),
        P(AXES, None),
        P(None, AXES, None),
        P(AXES, None),
        P(AXES),
        P(None, AXES, None),
        P(AXES, None),
        P(AXES),
        P(None, AXES, None),
        P(AXES, None),
        P(AXES),
    )
    return jax.shard_map(body, mesh=fine, in_specs=in_specs, out_specs=out_specs, check_vma=False)
```

```python
import functools

import jax
import jax.numpy as jnp
from jax import lax
from jax.experimental import pallas as pl
from jax.experimental.pallas import tpu as pltpu
from jax.sharding import Mesh, PartitionSpec as P

HEAD_SIZE = 64
D = 768
FF = 2048
TGT = 256
MEM = 1056
KEYS = 1152
PAIRS = 6
SELF_FORWARD, CROSS_FORWARD, CROSS_BACKWARD, SELF_BACKWARD = 6, 6, 2, 3


eps = 1e-06
masked_score = -1e30

AXES = ("x", "yh", "zh", "zl", "yl", "c")
SIZES = (4, 2, 2, 2, 2, 2)
RING_X, RING_Y, RING_Z = ("x",), ("yh", "yl"), ("zh", "zl")
RINGS = {"x": RING_X, "y": RING_Y, "z": RING_Z}
TORUS = RING_X + RING_Y + RING_Z + ("c",)
CHIPS = ("x", "yh", "zh", "zl", "yl")
EIGHT = ("zl", "yl", "c")
BLOCK = 48
SLOTS = 4
GAINS = 18

HBM = pl.BlockSpec(memory_space=pl.ANY)
SCALARS = pl.BlockSpec(memory_space=pltpu.SMEM)


def ring_pair(v, ring, first):
    perm = []
    for i in range(4):
        for c in range(2):
            perm.append((2 * i + c, 2 * (i ^ (1 if (c == 0) == first else 3)) + c))
    return lax.ppermute(v, ring + ("c",), perm)


def swap_cores(v):
    return lax.ppermute(v, "c", [(0, 1), (1, 0)])


def then(v, *tokens):
    return lax.optimization_barrier((v, *tokens))[0]


def add_low(*terms):
    return sum(t.astype(jnp.float32) for t in terms).astype(jnp.bfloat16)


def ring_sum_start(mine, got):
    return add_low(mine[:2], got[:2]), add_low(mine[2:], got[2:])


def ring_first(low, high, ring):
    got = ring_pair(high, RINGS[ring], False)
    return low[0], got[0], add_low(low[1], got[1])


def ring_second(terms, ring):
    return terms[0], terms[1], ring_pair(terms[2], RINGS[ring], True)


def ring_halves(terms):
    return tuple(add_low(*(t[at] for t in terms)) for at in (slice(0, 2), slice(2, 4)))


def ring_total(low, high, ring):
    return sum(t.astype(jnp.float32) for t in ring_second(ring_first(low, high, ring), ring))


def mm(a, b):
    return jnp.dot(a, b, preferred_element_type=jnp.float32)


def mm_nt(a, b):
    return lax.dot_general(a, b, (((1,), (1,)), ((), ())), preferred_element_type=jnp.float32)


def mm_tn(a, b):
    return lax.dot_general(a, b, (((0,), (0,)), ((), ())), preferred_element_type=jnp.float32)


def turned(v):
    return v.astype(jnp.float32).T.astype(v.dtype)


def first_half(shape):
    return lax.broadcasted_iota(jnp.int32, shape, 1) < HEAD_SIZE


def stacked_heads(pair):
    low = first_half(pair.shape)
    zero = jnp.zeros_like(pair)
    return jnp.concatenate([jnp.where(low, pair, zero), jnp.where(low, zero, pair)], axis=0)


def joined_heads(both):
    half = both.shape[0] // 2
    return jnp.where(first_half((half, both.shape[1])), both[:half], both[half:])


def rms_scale(hidden):
    return lax.rsqrt(jnp.mean(hidden * hidden, axis=-1, keepdims=True) + eps)


def rms_back(hidden, gain, grad):
    scale = rms_scale(hidden)
    u = grad * gain
    inner = jnp.mean(u * hidden, axis=-1, keepdims=True)
    grad_hidden = scale * u - hidden * (scale * scale * scale * inner)
    return grad_hidden, jnp.sum(grad * hidden * scale, axis=0, keepdims=True)


def my_place(pos_ref):
    return {"x": pos_ref[0], "y": pos_ref[1], "z": pos_ref[2]}


def group_member(at, core):
    group = at["x"] * 4 + (at["y"] >> 1) * 2 + (at["z"] >> 1)
    return group, (at["z"] & 1) * 4 + (at["y"] & 1) * 2 + core


def partners(core):
    return (0, 1 + 2 * core, 3 - 2 * core, 2)


def torus():
    return [(x, y, z, c) for x in range(4) for y in range(4) for z in range(4) for c in range(2)]


def block_place(x, y, z, c):
    return x * 4 + (y // 2) * 2 + z // 2, (z % 2) * 4 + (y % 2) * 2 + c


def start_place(blocks, first, out, sems):
    for matrix in range(4):
        for at in torus():
            group, member = block_place(*at)
            if member // 2 == matrix:
                pltpu.make_async_copy(
                    blocks.at[at + (slice(None), pl.ds(first, 384))],
                    out.at[pl.ds(BLOCK * group, BLOCK), pl.ds(384 * member, 384)],
                    sems.at[matrix],
                ).start()


def wait_matrix(out, matrix, sems):
    wait_whole([out.at[:, pl.ds(D * matrix, D)]], sems.at[matrix])


def ffn_copies(j, whole_in, whole_out, block_of):
    found = []
    for at in torus():
        group, member = block_place(*at)
        block = block_of(at)
        if member % 4 == j:
            rows, columns = pl.ds(BLOCK * group, BLOCK), pl.ds(512 * member, 512)
            found.append((whole_in.at[rows, columns], block.at[:, pl.ds(768, 512)]))
        if at[0] == j:
            rows = pl.ds(16 * (8 * group + member), 16)
            for s in range(3):
                part = block.at[pl.ds(16 * s, 16), pl.ds(1280, 256)]
                found.append((whole_out.at[rows, pl.ds(256 * s, 256)], part))
    return found


def ring_place(me, to, core):
    distance = me ^ to
    straight = distance ^ (distance >> 1)
    turned_round = ((straight & 1) << 1) | (straight >> 1)
    return jnp.where(core == 0, straight, turned_round)


def start_split(pos_ref, rings, matrix, column_of, whole, out_of, core, sem):
    me = my_place(pos_ref)
    for x, y, z, c in torus():
        group, member = block_place(x, y, z, 0)
        if c == 0 and member // 2 == matrix:
            to = {"x": x, "y": y, "z": z}
            places = [ring_place(me[ring], to[ring], core) for ring in rings]
            pltpu.make_async_copy(
                whole.at[pl.ds(BLOCK * group, BLOCK), pl.ds(column_of(matrix), 384)],
                out_of(*places),
                sem,
            ).start()


def wait_whole(refs, sem):
    for ref in refs:
        pltpu.make_async_copy(ref, ref, sem).wait()


def softmax_low(scores, valid):
    scores = jnp.where(valid, scores, masked_score)
    expanded = jnp.exp(scores - jnp.max(scores, axis=-1, keepdims=True))
    total = jnp.sum(expanded, axis=-1, keepdims=True)
    return (expanded * (1.0 / total)).astype(jnp.bfloat16)


def softmax_back(weights, grads):
    weights = weights.astype(jnp.float32)
    inner = jnp.sum(weights * grads, axis=-1, keepdims=True)
    return (weights * (grads - inner)).astype(jnp.bfloat16)


def pair_columns(j, offset=0):
    return pl.ds(pl.multiple_of(offset + j * 128, 128), 128)


def pairs_here(together):
    j = pl.program_id(0)
    return [(s, j * together + s) for s in range(together)]


def self_forward_kernel(rows_ref, slot_ref, gain_ref, early_ref, blocks, *refs):
    kept_ref, qkv_ref, p_out, h1_ref, w_out, p_ref, w_ref, sem, sent = refs
    emb_ref, mixed_ref = kept_ref.at[:, :D], kept_ref.at[:, D:]
    j = pl.program_id(0)

    @pl.when(j == 0)
    def _():
        start_place(blocks, 0, w_ref, sem)
        slots = rows_ref.shape[0]
        hits = slot_ref[...] == lax.broadcasted_iota(jnp.int32, (TGT, slots), 1)
        hidden = mm(hits.astype(jnp.bfloat16), rows_ref[...])
        emb_ref[...] = hidden.astype(jnp.bfloat16)
        normed = (hidden * rms_scale(hidden) * gain_ref[...]).astype(jnp.bfloat16)
        for k in range(3):
            at = pl.ds(768 * k, 768)
            wait_matrix(w_ref, k, sem)
            qkv_ref[:, at] = mm(normed, w_ref[:, at]).astype(jnp.bfloat16)
        wait_matrix(w_ref, 3, sem)
        pltpu.make_async_copy(w_ref, w_out, sent).start()

    row = lax.broadcasted_iota(jnp.int32, (2 * TGT, TGT), 0) & (TGT - 1)
    causal = lax.broadcasted_iota(jnp.int32, (2 * TGT, TGT), 1) <= row
    for s, pair in pairs_here(SELF_FORWARD):
        queries = stacked_heads(qkv_ref[:, pair_columns(pair)]) * jnp.bfloat16(0.125)
        weights = softmax_low(mm_nt(queries, qkv_ref[:, pair_columns(pair, 768)]), causal)
        p_ref[s] = weights
        pltpu.make_async_copy(p_ref.at[s], p_out.at[s], sent).start()
        mixed = mm(weights, qkv_ref[:, pair_columns(pair, 1536)])
        mixed_ref[:, pair_columns(pair)] = joined_heads(mixed).astype(jnp.bfloat16)

    @pl.when(j == PAIRS // SELF_FORWARD - 1)
    def _():
        h1_ref[...] = emb_ref[...].astype(jnp.float32) + mm(mixed_ref[...], w_ref[:, 2304:])
        wait_whole([w_ref, p_ref], sent)


def full(*shape):
    return pl.BlockSpec(shape, lambda j: (0,) * len(shape))


def shaped(dtype, *shape):
    return jax.ShapeDtypeStruct(shape, dtype)


def params(mib=56):
    return pltpu.CompilerParams(vmem_limit_bytes=mib * 2**20)


def cost(gflop, mbytes):
    return pl.CostEstimate(
        flops=int(gflop * 1e9), bytes_accessed=int(mbytes * 1e6), transcendentals=0
    )


def self_forward(rows, slot, gain, early, blocks):
    bf, f32 = jnp.bfloat16, jnp.float32
    return pl.pallas_call(
        self_forward_kernel,
        grid=(PAIRS // SELF_FORWARD,),
        in_specs=[full(512, D), full(TGT, 1), full(1, D), HBM, HBM],
        out_specs=[
            full(TGT, 2 * D),
            full(TGT, 3 * D),
            HBM,
            full(TGT, D),
            HBM,
        ],
        out_shape=[
            shaped(bf, TGT, 2 * D),
            shaped(bf, TGT, 3 * D),
            shaped(bf, PAIRS, 512, TGT),
            shaped(f32, TGT, D),
            shaped(bf, D, 4 * D),
        ],
        scratch_shapes=[
            pltpu.VMEM((PAIRS, 512, TGT), bf),
            pltpu.VMEM((D, 4 * D), bf),
            pltpu.SemaphoreType.DMA((4,)),
            pltpu.SemaphoreType.DMA,
        ],
        compiler_params=params(),
        cost_estimate=cost(8, 12),
        name="self_forward",
    )(rows, slot, gain, early, blocks)


def cross_forward_kernel(len_ref, h1_ref, gain_ref, mem_ref, blocks, *refs):
    q_ref, k_out, v_out, p_out, mixed_ref, h2_ref, w_out = refs[:7]
    k_ref, v_ref, p_ref, w_ref, sem, sent = refs[7:]
    j = pl.program_id(0)

    @pl.when(j == 0)
    def _():
        start_place(blocks, 384, w_ref, sem)
        hidden = h1_ref[...]
        normed = (hidden * rms_scale(hidden) * gain_ref[...]).astype(jnp.bfloat16)
        wait_matrix(w_ref, 0, sem)
        q_ref[...] = mm(normed, w_ref[:, :768]).astype(jnp.bfloat16)
        for out, sent_to, offset in ((k_ref, k_out, 768), (v_ref, v_out, 1536)):
            wait_matrix(w_ref, offset // D, sem)
            for half in range(2):
                at = pl.ds(384 * half, 384)
                out[:MEM, at] = mm(mem_ref[...], w_ref[:, pl.ds(offset + 384 * half, 384)]).astype(
                    jnp.bfloat16
                )
            out[MEM:, :] = jnp.zeros((KEYS - MEM, D), jnp.bfloat16)
            pltpu.make_async_copy(out, sent_to, sent).start()
        wait_matrix(w_ref, 3, sem)
        pltpu.make_async_copy(w_ref, w_out, sent).start()

    reach = lax.broadcasted_iota(jnp.int32, (2 * TGT, KEYS), 1) < len_ref[0]
    for s, pair in pairs_here(CROSS_FORWARD):
        queries = stacked_heads(q_ref[:, pair_columns(pair)]) * jnp.bfloat16(0.125)
        weights = softmax_low(mm_nt(queries, k_ref[:, pair_columns(pair)]), reach)
        p_ref[s] = weights
        pltpu.make_async_copy(p_ref.at[s], p_out.at[s], sent).start()
        mixed = mm(weights, v_ref[:, pair_columns(pair)])
        mixed_ref[:, pair_columns(pair)] = joined_heads(mixed).astype(jnp.bfloat16)

    @pl.when(j == PAIRS // CROSS_FORWARD - 1)
    def _():
        h2_ref[...] = h1_ref[...] + mm(mixed_ref[...], w_ref[:, 2304:])
        wait_whole([w_ref, k_ref, v_ref, p_ref], sent)


def cross_forward(mem_len, h1, gain, memory, blocks):
    bf, f32 = jnp.bfloat16, jnp.float32
    return pl.pallas_call(
        cross_forward_kernel,
        grid=(PAIRS // CROSS_FORWARD,),
        in_specs=[SCALARS, full(TGT, D), full(1, D), full(MEM, D), HBM],
        out_specs=[
            full(TGT, D),
            HBM,
            HBM,
            HBM,
            full(TGT, D),
            full(TGT, D),
            HBM,
        ],
        out_shape=[
            shaped(bf, TGT, D),
            shaped(bf, KEYS, D),
            shaped(bf, KEYS, D),
            shaped(bf, PAIRS, 512, KEYS),
            shaped(bf, TGT, D),
            shaped(f32, TGT, D),
            shaped(bf, D, 4 * D),
        ],
        scratch_shapes=[
            pltpu.VMEM((KEYS, D), bf),
            pltpu.VMEM((KEYS, D), bf),
            pltpu.VMEM((PAIRS, 512, KEYS), bf),
            pltpu.VMEM((D, 4 * D), bf),
            pltpu.SemaphoreType.DMA((4,)),
            pltpu.SemaphoreType.DMA,
        ],
        compiler_params=params(),
        cost_estimate=cost(20, 20),
        name="cross_forward",
    )(mem_len, h1, gain, memory, blocks)


class piece_of:
    def __init__(self, ref):
        self.ref = ref

    @property
    def at(self):
        return self

    def __getitem__(self, place):
        rows, columns = place
        return self.ref.at[rows, pl.ds(columns.start - 768, columns.size)]


def ffn_kernel(len_ref, h2_ref, gain_ref, og_ref, blocks, *refs):
    out_ref, g2_ref, dgain_ref, pieces = refs[:4]
    w_in, w_out, g_in, g_out, normed, normed_t, low, gate, up, grad, inner, da, sems, sem = refs[4:]
    j = pl.program_id(0)
    bf, f32 = jnp.bfloat16, jnp.float32

    def kept():
        row = lax.broadcasted_iota(jnp.int32, (TGT, 1), 0)
        return row < len_ref[0]

    @pl.when(j == 0)
    def _():
        for quarter in range(FF // 512):
            for whole, block in ffn_copies(quarter, w_in, w_out, lambda at: blocks.at[at]):
                pltpu.make_async_copy(block, whole, sems.at[quarter]).start()
        hidden = h2_ref[...]
        a3 = (hidden * rms_scale(hidden) * gain_ref[...]).astype(bf)
        normed[...] = a3
        normed_t[...] = a3.astype(f32).T.astype(bf)
        low[...] = jnp.where(kept(), og_ref[...], jnp.zeros((), bf))

    width = 512
    gate_at = pl.ds(pl.multiple_of(j * width, width), width)
    up_at = pl.ds(pl.multiple_of(FF + j * width, width), width)
    wait_whole([w_in.at[:, gate_at], w_in.at[:, up_at], w_out.at[gate_at, :]], sems.at[j])
    gate[...] = mm(normed[...], w_in[:, gate_at])
    up[...] = mm(normed[...], w_in[:, up_at])
    grad[...] = mm_nt(low[...], w_out[gate_at, :])

    def unit(i, carry):
        at = pl.ds(pl.multiple_of(i * 32, 32), 32)
        g, u, d = gate[at, :], up[at, :], grad[at, :]
        square = g * g
        t = jnp.tanh(0.7978845608 * (g + 0.044715 * (g * square)))
        half = 0.5 * (1.0 + t)
        gelu = g * half
        slope = half + 0.5 * g * (1.0 - t * t) * (0.7978845608 * (1.0 + 3.0 * 0.044715 * square))
        inner[at, :] = (gelu * u).astype(bf)
        gate[at, :] = d * u * slope
        up[at, :] = d * gelu
        return carry

    lax.fori_loop(0, TGT // 32, unit, 0, unroll=True)
    c_gate, c_up = gate[...].astype(bf), up[...].astype(bf)
    part = mm(inner[...], w_out[gate_at, :])
    da_part = mm_nt(c_gate, w_in[:, gate_at]) + mm_nt(c_up, w_in[:, up_at])

    @pl.when(j == 0)
    def _():
        out_ref[...] = part
        da[...] = da_part

    @pl.when(j > 0)
    def _():
        out_ref[...] += part
        da[...] += da_part

    g_out[gate_at, :] = mm_tn(inner[...], low[...]).astype(bf)
    g_in[:, gate_at] = mm(normed_t[...], c_gate).astype(bf)
    g_in[:, up_at] = mm(normed_t[...], c_up).astype(bf)

    for quarter in range(FF // width):

        @pl.when(j == quarter)
        def _():
            for whole, block in ffn_copies(
                quarter, g_in, g_out, lambda at: piece_of(pieces.at[at[0], at[3], at[1], at[2]])
            ):
                pltpu.make_async_copy(whole, block, sem).start()

    @pl.when(j == FF // width - 1)
    def _():
        hidden = h2_ref[...]
        out_ref[...] = jnp.where(kept(), hidden + out_ref[...], 0.0)
        back, dgain = rms_back(hidden, gain_ref[...], da[...])
        g2_ref[...] = jnp.where(kept(), og_ref[...].astype(f32), 0.0) + back
        dgain_ref[...] = dgain
        wait_whole([g_in, g_out], sem)


def ffn_both(tgt_len, h2, gain, out_grad, blocks):
    bf, f32 = jnp.bfloat16, jnp.float32
    pieces = shaped(bf, 4, 2, 4, 4, BLOCK, 768)
    return pl.pallas_call(
        ffn_kernel,
        grid=(FF // 512,),
        in_specs=[SCALARS, full(TGT, D), full(1, D), full(TGT, D), HBM],
        out_specs=[full(TGT, D), full(TGT, D), full(1, D), HBM],
        out_shape=[shaped(f32, TGT, D), shaped(f32, TGT, D), shaped(f32, 1, D), pieces],
        scratch_shapes=[
            pltpu.VMEM((D, 2 * FF), bf),
            pltpu.VMEM((FF, D), bf),
            pltpu.VMEM((D, 2 * FF), bf),
            pltpu.VMEM((FF, D), bf),
            pltpu.VMEM((TGT, D), bf),
            pltpu.VMEM((D, TGT), bf),
            pltpu.VMEM((TGT, D), bf),
            pltpu.VMEM((TGT, 512), f32),
            pltpu.VMEM((TGT, 512), f32),
            pltpu.VMEM((TGT, 512), f32),
            pltpu.VMEM((TGT, 512), bf),
            pltpu.VMEM((TGT, D), f32),
            pltpu.SemaphoreType.DMA((FF // 512,)),
            pltpu.SemaphoreType.DMA,
        ],
        compiler_params=params(),
        cost_estimate=cost(15, 25),
        name="ffn_both",
    )(tgt_len, h2, gain, out_grad, blocks)


def cross_backward_kernel(h1_ref, gain_ref, g2_ref, wq_ref, wo_ref, q_ref, k_ref, v_ref, p_ref, *refs):
    dq, dkv_ref, g1_ref, dgain_ref, grad_mixed = refs
    j = pl.program_id(0)
    bf = jnp.bfloat16

    @pl.when(j == 0)
    def _():
        grad_mixed[...] = mm_nt(g2_ref[...].astype(bf), wo_ref[...]).astype(bf)

    for s, pair in pairs_here(CROSS_BACKWARD):
        at = pair_columns(pair)
        d_pair = stacked_heads(grad_mixed[:, at])
        queries = stacked_heads(q_ref[:, at])
        weights = p_ref[s]
        grads = softmax_back(weights, mm_nt(d_pair, v_ref[:, at]))
        dq[:, at] = (joined_heads(mm(grads, k_ref[:, at])) * 0.125).astype(bf)
        dkv_ref[:, at] = (mm(turned(queries), grads) * 0.125).T.astype(bf)
        dkv_ref[:, pair_columns(pair, 768)] = mm(turned(d_pair), weights).T.astype(bf)

    @pl.when(j == PAIRS // CROSS_BACKWARD - 1)
    def _():
        back, dgain = rms_back(h1_ref[...], gain_ref[...], mm_nt(dq[...], wq_ref[...]))
        g1_ref[...] = g2_ref[...] + back
        dgain_ref[...] = dgain


def cross_backward(h1, gain, g2, w, q, k, v, p):
    bf, f32 = jnp.bfloat16, jnp.float32
    return pl.pallas_call(
        cross_backward_kernel,
        grid=(PAIRS // CROSS_BACKWARD,),
        in_specs=[
            full(TGT, D),
            full(1, D),
            full(TGT, D),
            pl.BlockSpec((D, D), lambda j: (0, 0)),
            pl.BlockSpec((D, D), lambda j: (0, 3)),
            full(TGT, D),
            full(KEYS, D),
            full(KEYS, D),
            pl.BlockSpec((CROSS_BACKWARD, 512, KEYS), lambda j: (j, 0, 0)),
        ],
        out_specs=[full(TGT, D), full(KEYS, 2 * D), full(TGT, D), full(1, D)],
        out_shape=[
            shaped(bf, TGT, D),
            shaped(bf, KEYS, 2 * D),
            shaped(f32, TGT, D),
            shaped(f32, 1, D),
        ],
        scratch_shapes=[pltpu.VMEM((TGT, D), bf)],
        compiler_params=params(),
        cost_estimate=cost(16, 20),
        name="cross_backward",
    )(h1, gain, g2, w, w, q, k, v, p)


def cross_grads_kernel(
    rings, pos_ref, h1_ref, gain_ref, g2_ref, mem_t_ref, mixed_ref, dq_ref, dkv_ref, *refs
):
    mine_ref, other_ref, whole, sem = refs
    bf = jnp.bfloat16
    hidden = h1_ref[...]
    normed = (hidden * rms_scale(hidden) * gain_ref[...]).astype(bf)

    def send(matrix):
        for source, out_ref in enumerate((mine_ref, other_ref)):
            core = pos_ref[3] ^ source
            start_split(
                pos_ref,
                rings,
                matrix,
                lambda m: pl.multiple_of(m * D + core * 384, 128),
                whole,
                lambda *places: out_ref.at[places],
                core,
                sem,
            )

    whole[:, :768] = mm_tn(normed, dq_ref[...]).astype(bf)
    send(0)
    whole[:, 2304:] = mm_tn(mixed_ref[...], g2_ref[...].astype(bf)).astype(bf)
    send(3)
    for k in range(4):
        at = pl.ds(768 + 384 * k, 384)
        whole[:, at] = mm(mem_t_ref[...], dkv_ref[:, pl.ds(384 * k, 384)]).astype(bf)
        if k % 2:
            send(1 + k // 2)
    wait_whole([whole], sem)


def cross_grads(rings, pos, h1, gain, g2, mem_t, mixed, dq, dkv):
    bf = jnp.bfloat16
    pieces = shaped(bf, 4, 4, 4, BLOCK, 384)
    return pl.pallas_call(
        functools.partial(cross_grads_kernel, rings),
        in_specs=[SCALARS] + [pl.BlockSpec(memory_space=pltpu.VMEM)] * 7,
        out_specs=[HBM, HBM],
        out_shape=[pieces, pieces],
        scratch_shapes=[pltpu.VMEM((D, 4 * D), bf), pltpu.SemaphoreType.DMA],
        compiler_params=params(),
        cost_estimate=cost(6, 12),
        name="cross_grads",
    )(pos, h1, gain, g2, mem_t, mixed, dq, dkv)


def self_backward_kernel(
    pos_ref, slot_ref, kept_ref, gain_ref, g1_ref, w_ref, qkv_ref, p_ref, *refs
):
    dg2_ref, dg3_ref, mine_ref, other_ref, out_ref, grad_mixed, dqkv = refs
    j = pl.program_id(0)
    bf, f32 = jnp.bfloat16, jnp.float32

    @pl.when(j == 0)
    def _():
        grad_mixed[...] = mm_nt(g1_ref[...].astype(bf), w_ref[:, 2304:]).astype(bf)

    for s, pair in pairs_here(SELF_BACKWARD):
        at = pair_columns(pair)
        d_pair = stacked_heads(grad_mixed[:, at])
        queries = stacked_heads(qkv_ref[:, at])
        weights = p_ref[s]
        grads = softmax_back(weights, mm_nt(d_pair, qkv_ref[:, pair_columns(pair, 1536)]))
        dqkv[:, at] = (joined_heads(mm(grads, qkv_ref[:, pair_columns(pair, 768)])) * 0.125).astype(bf)
        dqkv[:, pair_columns(pair, 768)] = (mm_tn(grads, queries) * 0.125).astype(bf)
        dqkv[:, pair_columns(pair, 1536)] = mm_tn(weights, d_pair).astype(bf)

    @pl.when(j == PAIRS // SELF_BACKWARD - 1)
    def _():
        for source, half_ref in enumerate((mine_ref, other_ref)):
            first = pl.multiple_of((pos_ref[3] ^ source) * 384, 128)
            for k in range(3):
                half_ref[:, 384 * k : 384 * k + 384] = dqkv[:, pl.ds(768 * k + first, 384)]
            half_ref[:, 1152:] = g1_ref[:, pl.ds(first, 384)].astype(bf)
        hidden = kept_ref[:, :D].astype(f32)
        back, dgain = rms_back(hidden, gain_ref[...], mm_nt(dqkv[...], w_ref[:, :2304]))
        slots = out_ref.shape[0]
        hits = slot_ref[...] == lax.broadcasted_iota(jnp.int32, (TGT, slots), 1)
        out_ref[:, :D] = mm_tn(hits.astype(bf), (g1_ref[...] + back).astype(bf)).astype(bf)
        row = lax.broadcasted_iota(jnp.int32, (slots, D), 0)
        feature = lax.broadcasted_iota(jnp.int32, (slots, D), 1)
        first = (row // SLOTS) * 6
        owned = (row % SLOTS == 0) & (feature >= first) & (feature < first + 6)
        lane = lax.broadcasted_iota(jnp.int32, (D, 128), 1)
        place = lax.broadcasted_iota(jnp.int32, (D, 128), 0) % 6
        extra = jnp.zeros((slots, 128), f32)
        for k, grad in enumerate((dgain, dg2_ref[...], dg3_ref[...])):
            spread = jnp.where(owned, grad, 0.0).astype(bf)
            extra += mm(spread, (lane == place + 6 * k).astype(bf))
        out_ref[:, D:] = extra.astype(bf)


def self_backward(pos, slot, kept, gain, g1, w, qkv, p, dg2, dg3):
    bf = jnp.bfloat16
    return pl.pallas_call(
        self_backward_kernel,
        grid=(PAIRS // SELF_BACKWARD,),
        in_specs=[
            SCALARS,
            full(TGT, 1),
            full(TGT, 2 * D),
            full(1, D),
            full(TGT, D),
            full(D, 4 * D),
            full(TGT, 3 * D),
            pl.BlockSpec((SELF_BACKWARD, 512, TGT), lambda j: (j, 0, 0)),
            full(1, D),
            full(1, D),
        ],
        out_specs=[full(TGT, 2 * D), full(TGT, 2 * D), full(512, D + 128)],
        out_shape=[shaped(bf, TGT, 2 * D), shaped(bf, TGT, 2 * D), shaped(bf, 512, D + 128)],
        scratch_shapes=[pltpu.VMEM((TGT, D), bf), pltpu.VMEM((TGT, 3 * D), bf)],
        compiler_params=params(),
        cost_estimate=cost(8, 10),
        name="self_backward",
    )(pos, slot, kept, gain, g1, w, qkv, p, dg2, dg3)


def self_grads_kernel(rings, pos_ref, gain_ref, kept_ref, kept_other_ref, half_ref, half_other_ref, *refs):
    *outs, whole, sem = refs
    bf, f32 = jnp.bfloat16, jnp.float32

    def normed(kept):
        hidden = kept[:, :D].astype(f32)
        return turned((hidden * rms_scale(hidden) * gain_ref[...]).astype(bf))

    whole[:, :1152] = (
        mm(normed(kept_ref), half_ref[:, :1152])
        + mm(normed(kept_other_ref), half_other_ref[:, :1152])
    ).astype(bf)
    whole[:, 1152:] = (
        mm_tn(kept_ref[:, D:], half_ref[:, 1152:])
        + mm_tn(kept_other_ref[:, D:], half_other_ref[:, 1152:])
    ).astype(bf)
    me, at = my_place(pos_ref), {}
    flips = partners(pos_ref[3])
    for k3 in range(4):
        at[rings[0]] = me[rings[0]] ^ flips[k3]
        for k2 in range(4):
            at[rings[1]] = me[rings[1]] ^ flips[k2]
            for k1 in range(4):
                at[rings[2]] = me[rings[2]] ^ flips[k1]
                group, member = group_member(at, 0)
                row = pl.multiple_of(group * BLOCK, 16)
                column = pl.multiple_of((member >> 1) * 384, 128)
                pltpu.make_async_copy(
                    whole.at[pl.ds(row, BLOCK), pl.ds(column, 384)],
                    outs[k3 // 2].at[k3 % 2, k2, k1],
                    sem,
                ).start()
    wait_whole([whole], sem)


def self_grads(rings, pos, gain, kept, kept_other, half, half_other):
    bf = jnp.bfloat16
    return pl.pallas_call(
        functools.partial(self_grads_kernel, rings),
        in_specs=[SCALARS] + [pl.BlockSpec(memory_space=pltpu.VMEM)] * 5,
        out_specs=[HBM, HBM],
        out_shape=[shaped(bf, 2, 4, 4, BLOCK, 384)] * 2,
        scratch_shapes=[pltpu.VMEM((D, 2 * D), bf), pltpu.SemaphoreType.DMA],
        compiler_params=params(),
        cost_estimate=cost(3, 8),
        name="self_grads",
    )(pos, gain, kept, kept_other, half, half_other)


def column_blocks(self_qkv, self_out, cross_qkv, cross_out, ffn_in):
    def chunks(v):
        return v.reshape(6, 8, -1).swapaxes(0, 1)

    flat = [
        jnp.concatenate([jnp.swapaxes(qkv, 0, 1).reshape(6, -1), out], axis=1)
        for qkv, out in ((self_qkv, self_out), (cross_qkv, cross_out))
    ]
    flat.append(jnp.swapaxes(ffn_in, 0, 1).reshape(6, -1))
    whole = jnp.concatenate([chunks(v) for v in flat], axis=2)
    return lax.all_to_all(whole, EIGHT, 0, 0, tiled=True).reshape(BLOCK, -1)


def all_weights(whole, ffn_out):
    tail = ffn_out.reshape(16, 3, 256).swapaxes(0, 1).reshape(BLOCK, 256)
    piece = jnp.concatenate([whole, tail], axis=1)
    return lax.all_gather(piece, TORUS).reshape(4, 4, 4, 2, BLOCK, -1)


def body(
    target_ids,
    tgt_len,
    mem_len,
    embed_table,
    memory,
    self_qkv,
    self_out,
    gain_self,
    cross_qkv,
    cross_out,
    gain_cross,
    ffn_in,
    ffn_out,
    gain_ffn,
    out_grad,
):
    tgt_count = target_ids.shape[1]
    model_width = memory.shape[2]
    own_rows = embed_table.shape[0]
    owner_count = 128
    place_in = [lax.axis_index(ring) for ring in (RING_X, RING_Y, RING_Z, ("c",))]
    pos = jnp.stack(place_in).astype(jnp.int32)

    flat_ids = target_ids.reshape(tgt_count)
    owner_of = flat_ids // own_rows
    local_row = flat_ids - owner_of * own_rows
    owner_hits = (owner_of[:, None] == jnp.arange(owner_count)[None, :]).astype(jnp.int32)
    row_rank = jnp.sum(jnp.cumsum(owner_hits, axis=0) * owner_hits, axis=1) - 1
    slot_index = owner_of * SLOTS + row_rank
    slot_hits = slot_index[:, None] == jnp.arange(owner_count * SLOTS)[None, :]
    wanted = jnp.sum(jnp.where(slot_hits, local_row[:, None] + 1, 0), axis=0)
    gains = jnp.concatenate([gain_self, gain_cross, gain_ffn]).astype(jnp.float32)
    request = jnp.concatenate(
        [
            wanted.astype(jnp.float32).reshape(owner_count, SLOTS),
            jnp.broadcast_to(gains[None], (owner_count, GAINS)),
            jnp.zeros((owner_count, 32 - SLOTS - GAINS), jnp.float32),
        ],
        axis=1,
    )
    whole = column_blocks(self_qkv, self_out, cross_qkv, cross_out, ffn_in)
    arrived = lax.all_to_all(then(request, whole), AXES, split_axis=0, concat_axis=0, tiled=True)
    gain_self_all, gain_cross_all, gain_ffn_all = (
        arrived[:, SLOTS + 6 * k : SLOTS + 6 * k + 6].reshape(1, model_width) for k in range(3)
    )
    rows_wanted = arrived[:, :SLOTS].reshape(owner_count * SLOTS).astype(jnp.int32) - 1
    row_hits = (rows_wanted[:, None] == jnp.arange(own_rows)[None, :]).astype(jnp.bfloat16)
    fetched = jnp.dot(row_hits, embed_table, preferred_element_type=jnp.float32)
    fetched = fetched.astype(jnp.bfloat16).reshape(owner_count, SLOTS, model_width)
    returned = lax.all_to_all(fetched, AXES, split_axis=0, concat_axis=0, tiled=True)
    memory_rows = memory[0]
    memory_turned = jnp.pad(memory_rows.T, ((0, 0), (0, KEYS - MEM)))
    blocks = all_weights(whole, ffn_out)
    slot = slot_index.reshape(tgt_count, 1)

    kept, self_proj, self_p, hidden_one, self_w = self_forward(
        returned.reshape(owner_count * SLOTS, model_width), slot, gain_self_all, memory_turned,
        blocks,
    )
    query, key, value, cross_p, cross_mixed, hidden_two, cross_w = cross_forward(
        mem_len, hidden_one, gain_cross_all, memory_rows, blocks
    )
    result, grad_two, gain_ffn_grad, pieces = ffn_both(
        tgt_len, hidden_two, gain_ffn_all, out_grad[0], blocks
    )
    kept_other = swap_cores(kept)
    ffn_x = lax.psum_scatter(pieces.reshape(8, 4, 4, BLOCK, 768), ("x", "c"))
    ffn_y = lax.psum_scatter(ffn_x, RING_Y)
    ffn_sum = lax.psum_scatter(ffn_y, RING_Z)
    grad_query, grad_kv, grad_one, gain_cross_grad = cross_backward(
        hidden_one, gain_cross_all, grad_two, cross_w, query, key, value, cross_p
    )
    rings = ("z", "y", "x")
    mine, other = cross_grads(
        rings, pos, hidden_one, gain_cross_all, grad_two, memory_turned, cross_mixed,
        grad_query, grad_kv,
    )
    other = swap_cores(other)
    half, half_other, outgoing = self_backward(
        pos, slot, kept, gain_self_all, then(grad_one, mine), self_w, self_proj, self_p,
        gain_cross_grad, gain_ffn_grad,
    )
    cross_start = ring_sum_start(then(mine, half), other)
    outgoing = then(outgoing, cross_start).reshape(owner_count, SLOTS, model_width + 128)
    incoming = lax.all_to_all(outgoing, AXES, split_axis=0, concat_axis=0, tiled=True)
    self_rings = ("x", "z", "y")
    self_low, self_high = self_grads(
        self_rings, pos, then(gain_self_all, outgoing), kept, kept_other, half,
        swap_cores(half_other),
    )
    cross_low, cross_high = cross_start
    cross_terms = ring_first(then(cross_low, self_low), cross_high, rings[0])
    memory_grad = jnp.einsum(
        "me,de->md", then(grad_kv, cross_terms[2], ffn_x)[:MEM], cross_w[:, 768:2304],
        preferred_element_type=jnp.float32,
    )[None]
    self_terms = ring_first(then(self_low, memory_grad), self_high, self_rings[0])
    cross_terms = ring_second(cross_terms, rings[0])
    cross_low, cross_high = ring_halves((then(cross_terms[0], self_terms[2]), *cross_terms[1:]))
    self_terms = ring_second(self_terms, self_rings[0])
    self_low, self_high = ring_halves((then(self_terms[0], cross_low, incoming), *self_terms[1:]))
    cross_terms = ring_first(then(cross_low, self_low), cross_high, rings[1])
    incoming = then(incoming, cross_terms[2]).reshape(
        owner_count * SLOTS, model_width + 128
    )
    gain_sums = jnp.sum(incoming[:, model_width : model_width + GAINS].astype(jnp.float32), axis=0)
    table_grad = jnp.einsum(
        "sr,sd->rd", row_hits, incoming[:, :model_width], preferred_element_type=jnp.float32
    )
    cross_terms = ring_second(cross_terms, rings[1])
    cross_low, cross_high = ring_halves((then(cross_terms[0], ffn_y), *cross_terms[1:]))
    self_terms = ring_first(self_low, self_high, self_rings[1])
    self_low, self_high = ring_halves(ring_second(self_terms, self_rings[1]))
    cross_sum = ring_total(cross_low, cross_high, rings[2])
    self_sum = ring_total(then(self_low, ffn_sum), self_high, self_rings[2])

    sums = jnp.concatenate([self_sum, cross_sum, ffn_sum[:, :512].astype(jnp.float32)], axis=1)
    sums = lax.all_to_all(sums.reshape(8, 6, -1), EIGHT, 0, 0, tiled=True)

    def rows_of(v):
        return jnp.swapaxes(v, 0, 1).reshape(6, -1)

    done = []
    for at in (0, 384):
        whole = rows_of(sums[:, :, at : at + 384])
        done.append(jnp.swapaxes(whole[:, :2304].reshape(6, 3, model_width), 0, 1))
        done.append(whole[:, 2304:])
    ffn_in_sum = jnp.swapaxes(rows_of(sums[:, :, 768:]).reshape(6, 2, 2048), 0, 1)
    ffn_out_sum = ffn_sum[:, 512:].astype(jnp.float32).reshape(3, 16, 256).swapaxes(0, 1).reshape(16, model_width)
    return (
        result[None],
        memory_grad,
        table_grad,
        done[0],
        done[1],
        gain_sums[:6],
        done[2],
        done[3],
        gain_sums[6:12],
        ffn_in_sum,
        ffn_out_sum,
        gain_sums[12:18],
    )


def solution(mesh):
    fine = Mesh(mesh.devices.reshape(SIZES), AXES)
    in_specs = (
        P(AXES, None),
        P(AXES),
        P(AXES),
        P(AXES, None),
        P(AXES, None, None),
        P(None, AXES, None),
        P(AXES, None),
        P(AXES),
        P(None, AXES, None),
        P(AXES, None),
        P(AXES),
        P(None, AXES, None),
        P(AXES, None),
        P(AXES),
        P(AXES, None, None),
    )
    out_specs = (
        P(AXES, None, None),
        P(AXES, None, None),
        P(AXES, None),
        P(None, AXES, None),
        P(AXES, None),
        P(AXES),
        P(None, AXES, None),
        P(AXES, None),
        P(AXES),
        P(None, AXES, None),
        P(AXES, None),
        P(AXES),
    )
    return jax.shard_map(body, mesh=fine, in_specs=in_specs, out_specs=out_specs, check_vma=False)
```

```python
import functools

import jax
import jax.numpy as jnp
from jax import lax
from jax.experimental import pallas as pl
from jax.experimental.pallas import tpu as pltpu
from jax.sharding import Mesh, PartitionSpec as P

HEAD_SIZE = 64
D = 768
FF = 2048
TGT = 256
MEM = 1056
KEYS = 1152
PAIRS = 6
SELF_FORWARD, CROSS_FORWARD, CROSS_BACKWARD, SELF_BACKWARD = 6, 6, 2, 3


eps = 1e-06
masked_score = -1e30

AXES = ("x", "yh", "zh", "zl", "yl", "c")
SIZES = (4, 2, 2, 2, 2, 2)
RING_X, RING_Y, RING_Z = ("x",), ("yh", "yl"), ("zh", "zl")
RINGS = {"x": RING_X, "y": RING_Y, "z": RING_Z}
TORUS = RING_X + RING_Y + RING_Z + ("c",)
CHIPS = ("x", "yh", "zh", "zl", "yl")
EIGHT = ("zl", "yl", "c")
BLOCK = 48
SLOTS = 4
GAINS = 18

HBM = pl.BlockSpec(memory_space=pl.ANY)
SCALARS = pl.BlockSpec(memory_space=pltpu.SMEM)


def ring_pair(v, ring, first):
    perm = []
    for i in range(4):
        for c in range(2):
            perm.append((2 * i + c, 2 * (i ^ (1 if (c == 0) == first else 3)) + c))
    return lax.ppermute(v, ring + ("c",), perm)


def swap_cores(v):
    return lax.ppermute(v, "c", [(0, 1), (1, 0)])


def then(v, *tokens):
    return lax.optimization_barrier((v, *tokens))[0]


def add_low(*terms):
    return sum(t.astype(jnp.float32) for t in terms).astype(jnp.bfloat16)


def ring_sum_start(mine, got):
    return add_low(mine[:2], got[:2]), add_low(mine[2:], got[2:])


def ring_first(low, high, ring):
    got = ring_pair(high, RINGS[ring], False)
    return low[0], got[0], add_low(low[1], got[1])


def ring_second(terms, ring):
    return terms[0], terms[1], ring_pair(terms[2], RINGS[ring], True)


def ring_halves(terms):
    return tuple(add_low(*(t[at] for t in terms)) for at in (slice(0, 2), slice(2, 4)))


def ring_total(low, high, ring):
    return sum(t.astype(jnp.float32) for t in ring_second(ring_first(low, high, ring), ring))


def mm(a, b):
    return jnp.dot(a, b, preferred_element_type=jnp.float32)


def mm_nt(a, b):
    return lax.dot_general(a, b, (((1,), (1,)), ((), ())), preferred_element_type=jnp.float32)


def mm_tn(a, b):
    return lax.dot_general(a, b, (((0,), (0,)), ((), ())), preferred_element_type=jnp.float32)


def turned(v):
    return v.astype(jnp.float32).T.astype(v.dtype)


def first_half(shape):
    return lax.broadcasted_iota(jnp.int32, shape, 1) < HEAD_SIZE


def stacked_heads(pair):
    low = first_half(pair.shape)
    zero = jnp.zeros_like(pair)
    return jnp.concatenate([jnp.where(low, pair, zero), jnp.where(low, zero, pair)], axis=0)


def joined_heads(both):
    half = both.shape[0] // 2
    return jnp.where(first_half((half, both.shape[1])), both[:half], both[half:])


def rms_scale(hidden):
    return lax.rsqrt(jnp.mean(hidden * hidden, axis=-1, keepdims=True) + eps)


def rms_back(hidden, gain, grad):
    scale = rms_scale(hidden)
    u = grad * gain
    inner = jnp.mean(u * hidden, axis=-1, keepdims=True)
    grad_hidden = scale * u - hidden * (scale * scale * scale * inner)
    return grad_hidden, jnp.sum(grad * hidden * scale, axis=0, keepdims=True)


def my_place(pos_ref):
    return {"x": pos_ref[0], "y": pos_ref[1], "z": pos_ref[2]}


def group_member(at, core):
    group = at["x"] * 4 + (at["y"] >> 1) * 2 + (at["z"] >> 1)
    return group, (at["z"] & 1) * 4 + (at["y"] & 1) * 2 + core


def partners(core):
    return (0, 1 + 2 * core, 3 - 2 * core, 2)


def torus():
    return [(x, y, z, c) for x in range(4) for y in range(4) for z in range(4) for c in range(2)]


def block_place(x, y, z, c):
    return x * 4 + (y // 2) * 2 + z // 2, (z % 2) * 4 + (y % 2) * 2 + c


def start_place(blocks, first, out, sems):
    for matrix in range(4):
        for at in torus():
            group, member = block_place(*at)
            if member // 2 == matrix:
                pltpu.make_async_copy(
                    blocks.at[at + (slice(None), pl.ds(first, 384))],
                    out.at[pl.ds(BLOCK * group, BLOCK), pl.ds(384 * member, 384)],
                    sems.at[matrix],
                ).start()


def wait_matrix(out, matrix, sems):
    wait_whole([out.at[:, pl.ds(D * matrix, D)]], sems.at[matrix])


def ffn_copies(j, whole_in, whole_out, block_of):
    found = []
    for at in torus():
        group, member = block_place(*at)
        block = block_of(at)
        if member % 4 == j:
            rows, columns = pl.ds(BLOCK * group, BLOCK), pl.ds(512 * member, 512)
            found.append((whole_in.at[rows, columns], block.at[:, pl.ds(768, 512)]))
        if at[0] == j:
            rows = pl.ds(16 * (8 * group + member), 16)
            for s in range(3):
                part = block.at[pl.ds(16 * s, 16), pl.ds(1280, 256)]
                found.append((whole_out.at[rows, pl.ds(256 * s, 256)], part))
    return found


def ring_place(me, to, core):
    distance = me ^ to
    straight = distance ^ (distance >> 1)
    turned_round = ((straight & 1) << 1) | (straight >> 1)
    return jnp.where(core == 0, straight, turned_round)


def start_split(pos_ref, rings, matrix, column_of, whole, out_of, core, sem):
    me = my_place(pos_ref)
    for x, y, z, c in torus():
        group, member = block_place(x, y, z, 0)
        if c == 0 and member // 2 == matrix:
            to = {"x": x, "y": y, "z": z}
            places = [ring_place(me[ring], to[ring], core) for ring in rings]
            pltpu.make_async_copy(
                whole.at[pl.ds(BLOCK * group, BLOCK), pl.ds(column_of(matrix), 384)],
                out_of(*places),
                sem,
            ).start()


def wait_whole(refs, sem):
    for ref in refs:
        pltpu.make_async_copy(ref, ref, sem).wait()


def softmax_low(scores, valid):
    scores = jnp.where(valid, scores, masked_score)
    expanded = jnp.exp(scores - jnp.max(scores, axis=-1, keepdims=True))
    total = jnp.sum(expanded, axis=-1, keepdims=True)
    return (expanded * (1.0 / total)).astype(jnp.bfloat16)


def softmax_back(weights, grads):
    weights = weights.astype(jnp.float32)
    inner = jnp.sum(weights * grads, axis=-1, keepdims=True)
    return (weights * (grads - inner)).astype(jnp.bfloat16)


def pair_columns(j, offset=0):
    return pl.ds(pl.multiple_of(offset + j * 128, 128), 128)


def pairs_here(together):
    j = pl.program_id(0)
    return [(s, j * together + s) for s in range(together)]


def self_forward_kernel(rows_ref, slot_ref, gain_ref, early_ref, blocks, *refs):
    kept_ref, qkv_ref, p_out, h1_ref, w_out, p_ref, w_ref, sem, sent = refs
    emb_ref, mixed_ref = kept_ref.at[:, :D], kept_ref.at[:, D:]
    j = pl.program_id(0)

    @pl.when(j == 0)
    def _():
        start_place(blocks, 0, w_ref, sem)
        slots = rows_ref.shape[0]
        hits = slot_ref[...] == lax.broadcasted_iota(jnp.int32, (TGT, slots), 1)
        hidden = mm(hits.astype(jnp.bfloat16), rows_ref[...])
        emb_ref[...] = hidden.astype(jnp.bfloat16)
        normed = (hidden * rms_scale(hidden) * gain_ref[...]).astype(jnp.bfloat16)
        for k in range(3):
            at = pl.ds(768 * k, 768)
            wait_matrix(w_ref, k, sem)
            qkv_ref[:, at] = mm(normed, w_ref[:, at]).astype(jnp.bfloat16)
        wait_matrix(w_ref, 3, sem)
        pltpu.make_async_copy(w_ref, w_out, sent).start()

    row = lax.broadcasted_iota(jnp.int32, (2 * TGT, TGT), 0) & (TGT - 1)
    causal = lax.broadcasted_iota(jnp.int32, (2 * TGT, TGT), 1) <= row
    for s, pair in pairs_here(SELF_FORWARD):
        queries = stacked_heads(qkv_ref[:, pair_columns(pair)]) * jnp.bfloat16(0.125)
        weights = softmax_low(mm_nt(queries, qkv_ref[:, pair_columns(pair, 768)]), causal)
        p_ref[s] = weights
        pltpu.make_async_copy(p_ref.at[s], p_out.at[s], sent).start()
        mixed = mm(weights, qkv_ref[:, pair_columns(pair, 1536)])
        mixed_ref[:, pair_columns(pair)] = joined_heads(mixed).astype(jnp.bfloat16)

    @pl.when(j == PAIRS // SELF_FORWARD - 1)
    def _():
        h1_ref[...] = emb_ref[...].astype(jnp.float32) + mm(mixed_ref[...], w_ref[:, 2304:])
        wait_whole([w_ref, p_ref], sent)


def full(*shape):
    return pl.BlockSpec(shape, lambda j: (0,) * len(shape))


def shaped(dtype, *shape):
    return jax.ShapeDtypeStruct(shape, dtype)


def params(mib=56):
    return pltpu.CompilerParams(vmem_limit_bytes=mib * 2**20)


def cost(gflop, mbytes):
    return pl.CostEstimate(
        flops=int(gflop * 1e9), bytes_accessed=int(mbytes * 1e6), transcendentals=0
    )


def self_forward(rows, slot, gain, early, blocks):
    bf, f32 = jnp.bfloat16, jnp.float32
    return pl.pallas_call(
        self_forward_kernel,
        grid=(PAIRS // SELF_FORWARD,),
        in_specs=[full(512, D), full(TGT, 1), full(1, D), HBM, HBM],
        out_specs=[
            full(TGT, 2 * D),
            full(TGT, 3 * D),
            HBM,
            full(TGT, D),
            HBM,
        ],
        out_shape=[
            shaped(bf, TGT, 2 * D),
            shaped(bf, TGT, 3 * D),
            shaped(bf, PAIRS, 512, TGT),
            shaped(f32, TGT, D),
            shaped(bf, D, 4 * D),
        ],
        scratch_shapes=[
            pltpu.VMEM((PAIRS, 512, TGT), bf),
            pltpu.VMEM((D, 4 * D), bf),
            pltpu.SemaphoreType.DMA((4,)),
            pltpu.SemaphoreType.DMA,
        ],
        compiler_params=params(),
        cost_estimate=cost(8, 12),
        name="self_forward",
    )(rows, slot, gain, early, blocks)


def cross_forward_kernel(len_ref, h1_ref, gain_ref, mem_ref, blocks, *refs):
    q_ref, k_out, v_out, p_out, mixed_ref, h2_ref, w_out = refs[:7]
    k_ref, v_ref, p_ref, w_ref, sem, sent = refs[7:]
    j = pl.program_id(0)

    @pl.when(j == 0)
    def _():
        start_place(blocks, 384, w_ref, sem)
        hidden = h1_ref[...]
        normed = (hidden * rms_scale(hidden) * gain_ref[...]).astype(jnp.bfloat16)
        wait_matrix(w_ref, 0, sem)
        q_ref[...] = mm(normed, w_ref[:, :768]).astype(jnp.bfloat16)
        for out, sent_to, offset in ((k_ref, k_out, 768), (v_ref, v_out, 1536)):
            wait_matrix(w_ref, offset // D, sem)
            for half in range(2):
                at = pl.ds(384 * half, 384)
                out[:MEM, at] = mm(mem_ref[...], w_ref[:, pl.ds(offset + 384 * half, 384)]).astype(
                    jnp.bfloat16
                )
            out[MEM:, :] = jnp.zeros((KEYS - MEM, D), jnp.bfloat16)
            pltpu.make_async_copy(out, sent_to, sent).start()
        wait_matrix(w_ref, 3, sem)
        pltpu.make_async_copy(w_ref, w_out, sent).start()

    reach = lax.broadcasted_iota(jnp.int32, (2 * TGT, KEYS), 1) < len_ref[0]
    for s, pair in pairs_here(CROSS_FORWARD):
        queries = stacked_heads(q_ref[:, pair_columns(pair)]) * jnp.bfloat16(0.125)
        weights = softmax_low(mm_nt(queries, k_ref[:, pair_columns(pair)]), reach)
        p_ref[s] = weights
        pltpu.make_async_copy(p_ref.at[s], p_out.at[s], sent).start()
        mixed = mm(weights, v_ref[:, pair_columns(pair)])
        mixed_ref[:, pair_columns(pair)] = joined_heads(mixed).astype(jnp.bfloat16)

    @pl.when(j == PAIRS // CROSS_FORWARD - 1)
    def _():
        h2_ref[...] = h1_ref[...] + mm(mixed_ref[...], w_ref[:, 2304:])
        wait_whole([w_ref, k_ref, v_ref, p_ref], sent)


def cross_forward(mem_len, h1, gain, memory, blocks):
    bf, f32 = jnp.bfloat16, jnp.float32
    return pl.pallas_call(
        cross_forward_kernel,
        grid=(PAIRS // CROSS_FORWARD,),
        in_specs=[SCALARS, full(TGT, D), full(1, D), full(MEM, D), HBM],
        out_specs=[
            full(TGT, D),
            HBM,
            HBM,
            HBM,
            full(TGT, D),
            full(TGT, D),
            HBM,
        ],
        out_shape=[
            shaped(bf, TGT, D),
            shaped(bf, KEYS, D),
            shaped(bf, KEYS, D),
            shaped(bf, PAIRS, 512, KEYS),
            shaped(bf, TGT, D),
            shaped(f32, TGT, D),
            shaped(bf, D, 4 * D),
        ],
        scratch_shapes=[
            pltpu.VMEM((KEYS, D), bf),
            pltpu.VMEM((KEYS, D), bf),
            pltpu.VMEM((PAIRS, 512, KEYS), bf),
            pltpu.VMEM((D, 4 * D), bf),
            pltpu.SemaphoreType.DMA((4,)),
            pltpu.SemaphoreType.DMA,
        ],
        compiler_params=params(),
        cost_estimate=cost(20, 20),
        name="cross_forward",
    )(mem_len, h1, gain, memory, blocks)


class piece_of:
    def __init__(self, ref):
        self.ref = ref

    @property
    def at(self):
        return self

    def __getitem__(self, place):
        rows, columns = place
        return self.ref.at[rows, pl.ds(columns.start - 768, columns.size)]


def ffn_kernel(len_ref, h2_ref, gain_ref, og_ref, blocks, *refs):
    out_ref, g2_ref, dgain_ref, pieces = refs[:4]
    w_in, w_out, g_in, g_out, normed, normed_t, low, gate, up, grad, inner, da, sems, sem = refs[4:]
    j = pl.program_id(0)
    bf, f32 = jnp.bfloat16, jnp.float32

    def kept():
        row = lax.broadcasted_iota(jnp.int32, (TGT, 1), 0)
        return row < len_ref[0]

    @pl.when(j == 0)
    def _():
        for quarter in range(FF // 512):
            for whole, block in ffn_copies(quarter, w_in, w_out, lambda at: blocks.at[at]):
                pltpu.make_async_copy(block, whole, sems.at[quarter]).start()
        hidden = h2_ref[...]
        a3 = (hidden * rms_scale(hidden) * gain_ref[...]).astype(bf)
        normed[...] = a3
        normed_t[...] = a3.astype(f32).T.astype(bf)
        low[...] = jnp.where(kept(), og_ref[...], jnp.zeros((), bf))

    width = 512
    gate_at = pl.ds(pl.multiple_of(j * width, width), width)
    up_at = pl.ds(pl.multiple_of(FF + j * width, width), width)
    wait_whole([w_in.at[:, gate_at], w_in.at[:, up_at], w_out.at[gate_at, :]], sems.at[j])
    gate[...] = mm(normed[...], w_in[:, gate_at])
    up[...] = mm(normed[...], w_in[:, up_at])
    grad[...] = mm_nt(low[...], w_out[gate_at, :])

    def unit(i, carry):
        at = pl.ds(pl.multiple_of(i * 32, 32), 32)
        g, u, d = gate[at, :], up[at, :], grad[at, :]
        square = g * g
        t = jnp.tanh(0.7978845608 * (g + 0.044715 * (g * square)))
        half = 0.5 * (1.0 + t)
        gelu = g * half
        slope = half + 0.5 * g * (1.0 - t * t) * (0.7978845608 * (1.0 + 3.0 * 0.044715 * square))
        inner[at, :] = (gelu * u).astype(bf)
        gate[at, :] = d * u * slope
        up[at, :] = d * gelu
        return carry

    lax.fori_loop(0, TGT // 32, unit, 0, unroll=True)
    c_gate, c_up = gate[...].astype(bf), up[...].astype(bf)
    part = mm(inner[...], w_out[gate_at, :])
    da_part = mm_nt(c_gate, w_in[:, gate_at]) + mm_nt(c_up, w_in[:, up_at])

    @pl.when(j == 0)
    def _():
        out_ref[...] = part
        da[...] = da_part

    @pl.when(j > 0)
    def _():
        out_ref[...] += part
        da[...] += da_part

    g_out[gate_at, :] = mm_tn(inner[...], low[...]).astype(bf)
    g_in[:, gate_at] = mm(normed_t[...], c_gate).astype(bf)
    g_in[:, up_at] = mm(normed_t[...], c_up).astype(bf)

    for quarter in range(FF // width):

        @pl.when(j == quarter)
        def _():
            for whole, block in ffn_copies(
                quarter, g_in, g_out, lambda at: piece_of(pieces.at[at[0], at[3], at[1], at[2]])
            ):
                pltpu.make_async_copy(whole, block, sem).start()

    @pl.when(j == FF // width - 1)
    def _():
        hidden = h2_ref[...]
        out_ref[...] = jnp.where(kept(), hidden + out_ref[...], 0.0)
        back, dgain = rms_back(hidden, gain_ref[...], da[...])
        g2_ref[...] = jnp.where(kept(), og_ref[...].astype(f32), 0.0) + back
        dgain_ref[...] = dgain
        wait_whole([g_in, g_out], sem)


def ffn_both(tgt_len, h2, gain, out_grad, blocks):
    bf, f32 = jnp.bfloat16, jnp.float32
    pieces = shaped(bf, 4, 2, 4, 4, BLOCK, 768)
    return pl.pallas_call(
        ffn_kernel,
        grid=(FF // 512,),
        in_specs=[SCALARS, full(TGT, D), full(1, D), full(TGT, D), HBM],
        out_specs=[full(TGT, D), full(TGT, D), full(1, D), HBM],
        out_shape=[shaped(f32, TGT, D), shaped(f32, TGT, D), shaped(f32, 1, D), pieces],
        scratch_shapes=[
            pltpu.VMEM((D, 2 * FF), bf),
            pltpu.VMEM((FF, D), bf),
            pltpu.VMEM((D, 2 * FF), bf),
            pltpu.VMEM((FF, D), bf),
            pltpu.VMEM((TGT, D), bf),
            pltpu.VMEM((D, TGT), bf),
            pltpu.VMEM((TGT, D), bf),
            pltpu.VMEM((TGT, 512), f32),
            pltpu.VMEM((TGT, 512), f32),
            pltpu.VMEM((TGT, 512), f32),
            pltpu.VMEM((TGT, 512), bf),
            pltpu.VMEM((TGT, D), f32),
            pltpu.SemaphoreType.DMA((FF // 512,)),
            pltpu.SemaphoreType.DMA,
        ],
        compiler_params=params(),
        cost_estimate=cost(15, 25),
        name="ffn_both",
    )(tgt_len, h2, gain, out_grad, blocks)


def cross_backward_kernel(h1_ref, gain_ref, g2_ref, wq_ref, wo_ref, q_ref, k_ref, v_ref, p_ref, *refs):
    dq, dkv_ref, g1_ref, dgain_ref, grad_mixed = refs
    j = pl.program_id(0)
    bf = jnp.bfloat16

    @pl.when(j == 0)
    def _():
        grad_mixed[...] = mm_nt(g2_ref[...].astype(bf), wo_ref[...]).astype(bf)

    for s, pair in pairs_here(CROSS_BACKWARD):
        at = pair_columns(pair)
        d_pair = stacked_heads(grad_mixed[:, at])
        queries = stacked_heads(q_ref[:, at])
        weights = p_ref[s]
        grads = softmax_back(weights, mm_nt(d_pair, v_ref[:, at]))
        dq[:, at] = (joined_heads(mm(grads, k_ref[:, at])) * 0.125).astype(bf)
        dkv_ref[:, at] = (mm(turned(queries), grads) * 0.125).T.astype(bf)
        dkv_ref[:, pair_columns(pair, 768)] = mm(turned(d_pair), weights).T.astype(bf)

    @pl.when(j == PAIRS // CROSS_BACKWARD - 1)
    def _():
        back, dgain = rms_back(h1_ref[...], gain_ref[...], mm_nt(dq[...], wq_ref[...]))
        g1_ref[...] = g2_ref[...] + back
        dgain_ref[...] = dgain


def cross_backward(h1, gain, g2, w, q, k, v, p):
    bf, f32 = jnp.bfloat16, jnp.float32
    return pl.pallas_call(
        cross_backward_kernel,
        grid=(PAIRS // CROSS_BACKWARD,),
        in_specs=[
            full(TGT, D),
            full(1, D),
            full(TGT, D),
            pl.BlockSpec((D, D), lambda j: (0, 0)),
            pl.BlockSpec((D, D), lambda j: (0, 3)),
            full(TGT, D),
            full(KEYS, D),
            full(KEYS, D),
            pl.BlockSpec((CROSS_BACKWARD, 512, KEYS), lambda j: (j, 0, 0)),
        ],
        out_specs=[full(TGT, D), full(KEYS, 2 * D), full(TGT, D), full(1, D)],
        out_shape=[
            shaped(bf, TGT, D),
            shaped(bf, KEYS, 2 * D),
            shaped(f32, TGT, D),
            shaped(f32, 1, D),
        ],
        scratch_shapes=[pltpu.VMEM((TGT, D), bf)],
        compiler_params=params(),
        cost_estimate=cost(16, 20),
        name="cross_backward",
    )(h1, gain, g2, w, w, q, k, v, p)


def cross_grads_kernel(
    rings, pos_ref, h1_ref, gain_ref, g2_ref, mem_t_ref, mixed_ref, dq_ref, dkv_ref, *refs
):
    mine_ref, other_ref, whole, sem = refs
    bf = jnp.bfloat16
    hidden = h1_ref[...]
    normed = (hidden * rms_scale(hidden) * gain_ref[...]).astype(bf)

    def send(matrix):
        for source, out_ref in enumerate((mine_ref, other_ref)):
            core = pos_ref[3] ^ source
            start_split(
                pos_ref,
                rings,
                matrix,
                lambda m: pl.multiple_of(m * D + core * 384, 128),
                whole,
                lambda *places: out_ref.at[places],
                core,
                sem,
            )

    whole[:, :768] = mm_tn(normed, dq_ref[...]).astype(bf)
    send(0)
    whole[:, 2304:] = mm_tn(mixed_ref[...], g2_ref[...].astype(bf)).astype(bf)
    send(3)
    for k in range(4):
        at = pl.ds(768 + 384 * k, 384)
        whole[:, at] = mm(mem_t_ref[...], dkv_ref[:, pl.ds(384 * k, 384)]).astype(bf)
        if k % 2:
            send(1 + k // 2)
    wait_whole([whole], sem)


def cross_grads(rings, pos, h1, gain, g2, mem_t, mixed, dq, dkv):
    bf = jnp.bfloat16
    pieces = shaped(bf, 4, 4, 4, BLOCK, 384)
    return pl.pallas_call(
        functools.partial(cross_grads_kernel, rings),
        in_specs=[SCALARS] + [pl.BlockSpec(memory_space=pltpu.VMEM)] * 7,
        out_specs=[HBM, HBM],
        out_shape=[pieces, pieces],
        scratch_shapes=[pltpu.VMEM((D, 4 * D), bf), pltpu.SemaphoreType.DMA],
        compiler_params=params(),
        cost_estimate=cost(6, 12),
        name="cross_grads",
    )(pos, h1, gain, g2, mem_t, mixed, dq, dkv)


def self_backward_kernel(
    pos_ref, slot_ref, kept_ref, gain_ref, g1_ref, w_ref, qkv_ref, p_ref, *refs
):
    dg2_ref, dg3_ref, mine_ref, other_ref, out_ref, grad_mixed, dqkv = refs
    j = pl.program_id(0)
    bf, f32 = jnp.bfloat16, jnp.float32

    @pl.when(j == 0)
    def _():
        grad_mixed[...] = mm_nt(g1_ref[...].astype(bf), w_ref[:, 2304:]).astype(bf)

    for s, pair in pairs_here(SELF_BACKWARD):
        at = pair_columns(pair)
        d_pair = stacked_heads(grad_mixed[:, at])
        queries = stacked_heads(qkv_ref[:, at])
        weights = p_ref[s]
        grads = softmax_back(weights, mm_nt(d_pair, qkv_ref[:, pair_columns(pair, 1536)]))
        dqkv[:, at] = (joined_heads(mm(grads, qkv_ref[:, pair_columns(pair, 768)])) * 0.125).astype(bf)
        dqkv[:, pair_columns(pair, 768)] = (mm_tn(grads, queries) * 0.125).astype(bf)
        dqkv[:, pair_columns(pair, 1536)] = mm_tn(weights, d_pair).astype(bf)

    @pl.when(j == PAIRS // SELF_BACKWARD - 1)
    def _():
        for source, half_ref in enumerate((mine_ref, other_ref)):
            first = pl.multiple_of((pos_ref[3] ^ source) * 384, 128)
            for k in range(3):
                half_ref[:, 384 * k : 384 * k + 384] = dqkv[:, pl.ds(768 * k + first, 384)]
            half_ref[:, 1152:] = g1_ref[:, pl.ds(first, 384)].astype(bf)
        hidden = kept_ref[:, :D].astype(f32)
        back, dgain = rms_back(hidden, gain_ref[...], mm_nt(dqkv[...], w_ref[:, :2304]))
        slots = out_ref.shape[0]
        hits = slot_ref[...] == lax.broadcasted_iota(jnp.int32, (TGT, slots), 1)
        out_ref[:, :D] = mm_tn(hits.astype(bf), (g1_ref[...] + back).astype(bf)).astype(bf)
        row = lax.broadcasted_iota(jnp.int32, (slots, D), 0)
        feature = lax.broadcasted_iota(jnp.int32, (slots, D), 1)
        first = (row // SLOTS) * 6
        owned = (row % SLOTS == 0) & (feature >= first) & (feature < first + 6)
        lane = lax.broadcasted_iota(jnp.int32, (D, 128), 1)
        place = lax.broadcasted_iota(jnp.int32, (D, 128), 0) % 6
        extra = jnp.zeros((slots, 128), f32)
        for k, grad in enumerate((dgain, dg2_ref[...], dg3_ref[...])):
            spread = jnp.where(owned, grad, 0.0).astype(bf)
            extra += mm(spread, (lane == place + 6 * k).astype(bf))
        out_ref[:, D:] = extra.astype(bf)


def self_backward(pos, slot, kept, gain, g1, w, qkv, p, dg2, dg3):
    bf = jnp.bfloat16
    return pl.pallas_call(
        self_backward_kernel,
        grid=(PAIRS // SELF_BACKWARD,),
        in_specs=[
            SCALARS,
            full(TGT, 1),
            full(TGT, 2 * D),
            full(1, D),
            full(TGT, D),
            full(D, 4 * D),
            full(TGT, 3 * D),
            pl.BlockSpec((SELF_BACKWARD, 512, TGT), lambda j: (j, 0, 0)),
            full(1, D),
            full(1, D),
        ],
        out_specs=[full(TGT, 2 * D), full(TGT, 2 * D), full(512, D + 128)],
        out_shape=[shaped(bf, TGT, 2 * D), shaped(bf, TGT, 2 * D), shaped(bf, 512, D + 128)],
        scratch_shapes=[pltpu.VMEM((TGT, D), bf), pltpu.VMEM((TGT, 3 * D), bf)],
        compiler_params=params(),
        cost_estimate=cost(8, 10),
        name="self_backward",
    )(pos, slot, kept, gain, g1, w, qkv, p, dg2, dg3)


def self_grads_kernel(rings, pos_ref, gain_ref, kept_ref, kept_other_ref, half_ref, half_other_ref, *refs):
    *outs, whole, sem = refs
    bf, f32 = jnp.bfloat16, jnp.float32

    def normed(kept):
        hidden = kept[:, :D].astype(f32)
        return turned((hidden * rms_scale(hidden) * gain_ref[...]).astype(bf))

    whole[:, :1152] = (
        mm(normed(kept_ref), half_ref[:, :1152])
        + mm(normed(kept_other_ref), half_other_ref[:, :1152])
    ).astype(bf)
    whole[:, 1152:] = (
        mm_tn(kept_ref[:, D:], half_ref[:, 1152:])
        + mm_tn(kept_other_ref[:, D:], half_other_ref[:, 1152:])
    ).astype(bf)
    me, at = my_place(pos_ref), {}
    flips = partners(pos_ref[3])
    for k3 in range(4):
        at[rings[0]] = me[rings[0]] ^ flips[k3]
        for k2 in range(4):
            at[rings[1]] = me[rings[1]] ^ flips[k2]
            for k1 in range(4):
                at[rings[2]] = me[rings[2]] ^ flips[k1]
                group, member = group_member(at, 0)
                row = pl.multiple_of(group * BLOCK, 16)
                column = pl.multiple_of((member >> 1) * 384, 128)
                pltpu.make_async_copy(
                    whole.at[pl.ds(row, BLOCK), pl.ds(column, 384)],
                    outs[k3 // 2].at[k3 % 2, k2, k1],
                    sem,
                ).start()
    wait_whole([whole], sem)


def self_grads(rings, pos, gain, kept, kept_other, half, half_other):
    bf = jnp.bfloat16
    return pl.pallas_call(
        functools.partial(self_grads_kernel, rings),
        in_specs=[SCALARS] + [pl.BlockSpec(memory_space=pltpu.VMEM)] * 5,
        out_specs=[HBM, HBM],
        out_shape=[shaped(bf, 2, 4, 4, BLOCK, 384)] * 2,
        scratch_shapes=[pltpu.VMEM((D, 2 * D), bf), pltpu.SemaphoreType.DMA],
        compiler_params=params(),
        cost_estimate=cost(3, 8),
        name="self_grads",
    )(pos, gain, kept, kept_other, half, half_other)


def column_blocks(self_qkv, self_out, cross_qkv, cross_out, ffn_in):
    def chunks(v):
        return v.reshape(6, 8, -1).swapaxes(0, 1)

    flat = [
        jnp.concatenate([jnp.swapaxes(qkv, 0, 1).reshape(6, -1), out], axis=1)
        for qkv, out in ((self_qkv, self_out), (cross_qkv, cross_out))
    ]
    flat.append(jnp.swapaxes(ffn_in, 0, 1).reshape(6, -1))
    whole = jnp.concatenate([chunks(v) for v in flat], axis=2)
    return lax.all_to_all(whole, EIGHT, 0, 0, tiled=True).reshape(BLOCK, -1)


def all_weights(whole, ffn_out):
    tail = ffn_out.reshape(16, 3, 256).swapaxes(0, 1).reshape(BLOCK, 256)
    piece = jnp.concatenate([whole, tail], axis=1)
    return lax.all_gather(piece, TORUS).reshape(4, 4, 4, 2, BLOCK, -1)


def body(
    target_ids,
    tgt_len,
    mem_len,
    embed_table,
    memory,
    self_qkv,
    self_out,
    gain_self,
    cross_qkv,
    cross_out,
    gain_cross,
    ffn_in,
    ffn_out,
    gain_ffn,
    out_grad,
):
    tgt_count = target_ids.shape[1]
    model_width = memory.shape[2]
    own_rows = embed_table.shape[0]
    owner_count = 128
    place_in = [lax.axis_index(ring) for ring in (RING_X, RING_Y, RING_Z, ("c",))]
    pos = jnp.stack(place_in).astype(jnp.int32)

    flat_ids = target_ids.reshape(tgt_count)
    owner_of = flat_ids // own_rows
    local_row = flat_ids - owner_of * own_rows
    owner_hits = (owner_of[:, None] == jnp.arange(owner_count)[None, :]).astype(jnp.int32)
    row_rank = jnp.sum(jnp.cumsum(owner_hits, axis=0) * owner_hits, axis=1) - 1
    slot_index = owner_of * SLOTS + row_rank
    slot_hits = slot_index[:, None] == jnp.arange(owner_count * SLOTS)[None, :]
    wanted = jnp.sum(jnp.where(slot_hits, local_row[:, None] + 1, 0), axis=0)
    gains = jnp.concatenate([gain_self, gain_cross, gain_ffn]).astype(jnp.float32)
    request = jnp.concatenate(
        [
            wanted.astype(jnp.float32).reshape(owner_count, SLOTS),
            jnp.broadcast_to(gains[None], (owner_count, GAINS)),
            jnp.zeros((owner_count, 32 - SLOTS - GAINS), jnp.float32),
        ],
        axis=1,
    )
    whole = column_blocks(self_qkv, self_out, cross_qkv, cross_out, ffn_in)
    arrived = lax.all_to_all(then(request, whole), AXES, split_axis=0, concat_axis=0, tiled=True)
    gain_self_all, gain_cross_all, gain_ffn_all = (
        arrived[:, SLOTS + 6 * k : SLOTS + 6 * k + 6].reshape(1, model_width) for k in range(3)
    )
    rows_wanted = arrived[:, :SLOTS].reshape(owner_count * SLOTS).astype(jnp.int32) - 1
    row_hits = (rows_wanted[:, None] == jnp.arange(own_rows)[None, :]).astype(jnp.bfloat16)
    fetched = jnp.dot(row_hits, embed_table, preferred_element_type=jnp.float32)
    fetched = fetched.astype(jnp.bfloat16).reshape(owner_count, SLOTS, model_width)
    returned = lax.all_to_all(fetched, AXES, split_axis=0, concat_axis=0, tiled=True)
    memory_rows = memory[0]
    memory_turned = jnp.pad(memory_rows.T, ((0, 0), (0, KEYS - MEM)))
    blocks = all_weights(whole, ffn_out)
    slot = slot_index.reshape(tgt_count, 1)

    kept, self_proj, self_p, hidden_one, self_w = self_forward(
        returned.reshape(owner_count * SLOTS, model_width), slot, gain_self_all, memory_turned,
        blocks,
    )
    query, key, value, cross_p, cross_mixed, hidden_two, cross_w = cross_forward(
        mem_len, hidden_one, gain_cross_all, memory_rows, blocks
    )
    result, grad_two, gain_ffn_grad, pieces = ffn_both(
        tgt_len, hidden_two, gain_ffn_all, out_grad[0], blocks
    )
    kept_other = swap_cores(kept)
    ffn_x = lax.psum_scatter(pieces.reshape(8, 4, 4, BLOCK, 768), ("x", "c"))
    ffn_y = lax.psum_scatter(ffn_x, RING_Y)
    ffn_sum = lax.psum_scatter(ffn_y, RING_Z)
    grad_query, grad_kv, grad_one, gain_cross_grad = cross_backward(
        hidden_one, gain_cross_all, grad_two, cross_w, query, key, value, cross_p
    )
    rings = ("z", "y", "x")
    mine, other = cross_grads(
        rings, pos, hidden_one, gain_cross_all, grad_two, memory_turned, cross_mixed,
        grad_query, grad_kv,
    )
    other = swap_cores(other)
    half, half_other, outgoing = self_backward(
        pos, slot, kept, gain_self_all, then(grad_one, mine), self_w, self_proj, self_p,
        gain_cross_grad, gain_ffn_grad,
    )
    cross_start = ring_sum_start(then(mine, half), other)
    outgoing = then(outgoing, cross_start).reshape(owner_count, SLOTS, model_width + 128)
    incoming = lax.all_to_all(outgoing, AXES, split_axis=0, concat_axis=0, tiled=True)
    self_rings = ("x", "z", "y")
    self_low, self_high = self_grads(
        self_rings, pos, then(gain_self_all, outgoing), kept, kept_other, half,
        swap_cores(half_other),
    )
    cross_low, cross_high = cross_start
    cross_terms = ring_first(then(cross_low, self_low), cross_high, rings[0])
    memory_grad = jnp.einsum(
        "me,de->md", then(grad_kv, cross_terms[2], ffn_x)[:MEM], cross_w[:, 768:2304],
        preferred_element_type=jnp.float32,
    )[None]
    self_terms = ring_first(then(self_low, memory_grad), self_high, self_rings[0])
    cross_terms = ring_second(cross_terms, rings[0])
    cross_low, cross_high = ring_halves((then(cross_terms[0], self_terms[2]), *cross_terms[1:]))
    self_terms = ring_second(self_terms, self_rings[0])
    self_low, self_high = ring_halves((then(self_terms[0], cross_low, incoming), *self_terms[1:]))
    cross_terms = ring_first(then(cross_low, self_low, ffn_y), cross_high, rings[1])
    incoming = then(incoming, cross_terms[2]).reshape(
        owner_count * SLOTS, model_width + 128
    )
    gain_sums = jnp.sum(incoming[:, model_width : model_width + GAINS].astype(jnp.float32), axis=0)
    table_grad = jnp.einsum(
        "sr,sd->rd", row_hits, incoming[:, :model_width], preferred_element_type=jnp.float32
    )
    cross_terms = ring_second(cross_terms, rings[1])
    cross_low, cross_high = ring_halves(cross_terms)
    self_terms = ring_first(self_low, self_high, self_rings[1])
    self_low, self_high = ring_halves(ring_second(self_terms, self_rings[1]))
    cross_sum = ring_total(cross_low, cross_high, rings[2])
    self_sum = ring_total(then(self_low, ffn_sum), self_high, self_rings[2])

    sums = jnp.concatenate([self_sum, cross_sum, ffn_sum[:, :512].astype(jnp.float32)], axis=1)
    sums = lax.all_to_all(sums.reshape(8, 6, -1), EIGHT, 0, 0, tiled=True)

    def rows_of(v):
        return jnp.swapaxes(v, 0, 1).reshape(6, -1)

    done = []
    for at in (0, 384):
        whole = rows_of(sums[:, :, at : at + 384])
        done.append(jnp.swapaxes(whole[:, :2304].reshape(6, 3, model_width), 0, 1))
        done.append(whole[:, 2304:])
    ffn_in_sum = jnp.swapaxes(rows_of(sums[:, :, 768:]).reshape(6, 2, 2048), 0, 1)
    ffn_out_sum = ffn_sum[:, 512:].astype(jnp.float32).reshape(3, 16, 256).swapaxes(0, 1).reshape(16, model_width)
    return (
        result[None],
        memory_grad,
        table_grad,
        done[0],
        done[1],
        gain_sums[:6],
        done[2],
        done[3],
        gain_sums[6:12],
        ffn_in_sum,
        ffn_out_sum,
        gain_sums[12:18],
    )


def solution(mesh):
    fine = Mesh(mesh.devices.reshape(SIZES), AXES)
    in_specs = (
        P(AXES, None),
        P(AXES),
        P(AXES),
        P(AXES, None),
        P(AXES, None, None),
        P(None, AXES, None),
        P(AXES, None),
        P(AXES),
        P(None, AXES, None),
        P(AXES, None),
        P(AXES),
        P(None, AXES, None),
        P(AXES, None),
        P(AXES),
        P(AXES, None, None),
    )
    out_specs = (
        P(AXES, None, None),
        P(AXES, None, None),
        P(AXES, None),
        P(None, AXES, None),
        P(AXES, None),
        P(AXES),
        P(None, AXES, None),
        P(AXES, None),
        P(AXES),
        P(None, AXES, None),
        P(AXES, None),
        P(AXES),
    )
    return jax.shard_map(body, mesh=fine, in_specs=in_specs, out_specs=out_specs, check_vma=False)
```
